32 devices in a mesh: pole: 2 (over y), prow: 4 (over z), pcol: 4 (over x, core).
Axes of the slice: x: 2, y: 2, z: 4, core: 2. Of those that a mesh axis runs over, the one named last changes fastest.
Arguments:
- inverse_top: bfloat16 [4096, 2048], P(('pole', 'prow'), 'pcol'), parts along dimension 0, as said below
- diag_inverse: float32 [8, 256, 256], P(('pole', 'pcol')), parts along dimension 0, as said below
- cross_blocks: float32 [4096, 1024], P(('pole', 'prow'), 'pcol'), parts along dimension 0, may hold values from -0.75 to 0.75
- pattern: int32 [8, 4], P('prow', 'pcol'), may hold values 0 or 1
Outputs:
- inverse_cross: float32 [4096, 1024], P(('pole', 'prow'), 'pcol'), parts along dimension 0
- inverse_diag: float32 [8, 256, 256], P(('pole', 'pcol')), parts along dimension 0
The draws below stay inside these ranges and needn't reach their ends.
There are 2 independent parts, one for each index of `pole`. The reference program is written for one: setup_inputs(seed, part) draws one part's arguments, and reference() takes and returns one part's arrays. A program takes and returns all parts, laid end to end along the dimension named above; an argument that names none is the same for every part. Nothing has to cross between parts.
Inputs may be any that keep to these rules, and one draw needn't show every extreme that they name: inverse_top is symmetric. Each diag_inverse[k] is symmetric.
All inputs are finite; a program needn't handle non-finite values. No bound on the sum of `pattern` on one device may be relied on, other than what follows from the above.
Results may differ from the reference program's by a relative error of at most 0.009.
Values may be sent and summed in bfloat16 or wider, within the bound.
No kernel may reach another device: no remote copies, remote signals or barrier semaphores. Data moves between devices by JAX's collectives and lax.ppermute only.
A program may use at most 64 MiB of HBM per device.

```python
import math
import jax
import jax.numpy as jnp
from jax import lax

B = 256
TB = 2
NT = 8
NK = 4


def draw_inverse_top(key, part):
    key = jax.random.fold_in(key, 11)
    order = NT * B
    first, second, third = jax.random.split(key, 3)
    entries = jnp.clip(jax.random.normal(first, (order, order), jnp.float32), -6.0, 6.0)
    scales = jnp.exp(jax.random.uniform(third, (order,), jnp.float32, 0.0, 0.0))
    symmetric = (entries + entries.T) * (0.7071 / math.sqrt(order))
    diagonal = jax.random.uniform(second, (order,), jnp.float32, 1.0, 3.0)
    full = symmetric + jnp.eye(order, dtype=jnp.float32) * diagonal[None, :]
    full = full * scales[:, None] * scales[None, :]
    return full.astype(jnp.bfloat16)


def draw_diag_inverse(key, part):
    key = jax.random.fold_in(key, 23)
    first, second = jax.random.split(key, 2)
    entries = jnp.clip(jax.random.normal(first, (NK, B, B), jnp.float32), -6.0, 6.0)
    symmetric = (entries + jnp.swapaxes(entries, 1, 2)) * (0.7071 * 0.4 / math.sqrt(B))
    diagonal = jax.random.uniform(second, (NK, B), jnp.float32, 0.6, 1.6)
    full = symmetric + jnp.eye(B, dtype=jnp.float32)[None, :, :] * diagonal[:, None, :]
    return full


def place_ends(result, own_key, smallest, top_value):
    place = [jax.random.randint(jax.random.fold_in(own_key, axis), (), 0, length) for axis, length in enumerate(result.shape)]
    main_axis = result.shape.index(max(result.shape))
    neighbour = place[:main_axis] + [(place[main_axis] + 1) % result.shape[main_axis]] + place[main_axis + 1:]
    return result.at[tuple(place)].set(smallest).at[tuple(neighbour)].set(top_value)


def raised(drawn, rng, source, target, blocks, factor):
    owner, partner = [(jnp.arange(drawn.shape[position]) // (drawn.shape[position] // blocks)).reshape([-1 if axis == position else 1 for axis in range(drawn.ndim)]) for position in (source, target)]
    chosen = jax.random.permutation(rng, blocks)[partner]
    strong = (owner == chosen) | (owner == (partner + blocks // 2) % blocks)
    return jnp.where(strong, factor * drawn, drawn)


def levels(stream_key, dims, pieces, smallest, top_value):
    level, own = 1.0, jax.random.fold_in(stream_key, 6)
    for dim, parts in pieces:
        steps = jnp.exp(jax.random.uniform(jax.random.fold_in(own, dim), (parts,), jnp.float32, smallest / len(pieces), top_value / len(pieces)))
        level = level * jnp.repeat(steps, dims[dim] // parts).reshape([-1 if axis == dim else 1 for axis in range(len(dims))])
    return level


def heavy_noise(key, shape, width, reach, cuts, heavy, kind=jnp.bfloat16):
    result = width * jax.random.normal(key, shape, jnp.float32)
    if cuts:
        result = result * levels(key, shape, cuts, -0.22, 0.18)
    return jnp.clip(raised(result, jax.random.fold_in(key, 3), *heavy), -reach, reach).astype(kind)


def setup_inputs(seed: int = 0, part: int = 0) -> dict:
    keys = jax.random.split(jax.random.key(seed), 5)
    part_splits = jax.random.split(jax.random.fold_in(keys[4], part), 5)
    inverse_top = draw_inverse_top(jax.random.fold_in(jax.random.fold_in(keys[4], part), 71), part)
    diag_inverse = draw_diag_inverse(jax.random.fold_in(jax.random.fold_in(keys[4], part), 71), part)
    cross_blocks = heavy_noise(part_splits[2], (NT * B, NK * B), (NT * B // 16) ** -0.5, 0.75, ((0, 4), (1, 4)), (0, 1, 4, 2.0), jnp.float32)
    pattern = place_ends((jax.random.randint(keys[3], (NT, NK), 0, 2) < 1).astype(jnp.int32), jax.random.fold_in(keys[3], 1), 0, 1)
    return dict(inverse_top=inverse_top, diag_inverse=diag_inverse, cross_blocks=cross_blocks, pattern=pattern)


def reference(inverse_top, diag_inverse, cross_blocks, pattern):
    masked = cross_blocks.reshape(NT, B, NK, B) * pattern.astype(jnp.float32)[:, None, :, None]
    solved = jnp.einsum("awkv,kvu->awku", masked, diag_inverse, precision=lax.Precision.HIGHEST)
    factor_panel = solved.reshape(NT * B, NK * B).astype(jnp.bfloat16)
    span = TB * B

    def accumulate(carried, index):
        begin = (index * span).astype(jnp.int32)
        columns = lax.dynamic_slice_in_dim(inverse_top, begin, span, 1)
        panel_rows = lax.dynamic_slice_in_dim(factor_panel, begin, span, 0)
        partial_g = jnp.dot(columns, panel_rows, preferred_element_type=jnp.float32).astype(jnp.bfloat16)
        return carried + partial_g.astype(jnp.float32), None

    selected, _ = lax.scan(accumulate, jnp.zeros((NT * B, NK * B), jnp.float32), jnp.arange(NT // TB, dtype=jnp.int32))
    inverse_cross = -selected
    update = jnp.einsum("iku,ikv->kuv", factor_panel.astype(jnp.float32).reshape(NT * B, NK, B), selected.reshape(NT * B, NK, B), precision=lax.Precision.HIGHEST)
    inverse_diag = diag_inverse + update
    return inverse_cross, inverse_diag
```

```python
import functools
import jax
import jax.numpy as jnp
from jax import lax
from jax.experimental import pallas as pl
from jax.experimental.pallas import tpu as pltpu
from jax.sharding import PartitionSpec as P

CORES = 2
VMEM_LIMIT = 40 * 1024 * 1024


def panel_kernel(pattern_ref, cross_ref, diag_ref, panel_ref):
    width = diag_ref.shape[1]
    for a in range(pattern_ref.shape[0]):
        rows = pl.ds(a * width, width)
        masked = cross_ref[rows, :] * pattern_ref[a, 0].astype(jnp.float32)
        solved = jnp.dot(
            masked, diag_ref[0], precision=lax.Precision.HIGHEST, preferred_element_type=jnp.float32
        )
        panel_ref[rows, :] = solved.astype(jnp.bfloat16)


def build_panel(cross_blocks, diag_inverse, pattern):
    return pl.pallas_call(
        panel_kernel,
        out_shape=jax.ShapeDtypeStruct(cross_blocks.shape, jnp.bfloat16),
        in_specs=[
            pl.BlockSpec(memory_space=pltpu.SMEM),
            pl.BlockSpec(memory_space=pltpu.VMEM),
            pl.BlockSpec(memory_space=pltpu.VMEM),
        ],
        out_specs=pl.BlockSpec(memory_space=pltpu.VMEM),
        compiler_params=pltpu.CompilerParams(vmem_limit_bytes=VMEM_LIMIT),
        name="panel",
    )(pattern, cross_blocks, diag_inverse)


def product_kernel(n, slots_ref, *refs):
    tops, panels = refs[:n], refs[n:2 * n]
    cross_ref, update_ref, top_buf, panel_buf, top_sems, panel_sems = refs[2 * n:]
    copies = []
    for s in range(n):
        copy = pltpu.make_async_copy(panels[s], panel_buf.at[slots_ref[s]], panel_sems.at[s])
        copy.start()
        copies.append(copy)
    for t in range(n):
        copy = pltpu.make_async_copy(tops[t], top_buf.at[t], top_sems.at[t])
        copy.start()
        copies.append(copy)
    for copy in copies:
        copy.wait()
    total = jnp.dot(top_buf[0], panel_buf[0], preferred_element_type=jnp.float32)
    for t in range(1, n):
        total += jnp.dot(top_buf[t], panel_buf[t], preferred_element_type=jnp.float32)
    cross_ref[...] = -total
    own = panel_buf[slots_ref[0]]
    high = total.astype(jnp.bfloat16)
    low = (total - high.astype(jnp.float32)).astype(jnp.bfloat16)
    contract = (((0,), (0,)), ((), ()))
    update = lax.dot_general(own, high, contract, preferred_element_type=jnp.float32)
    update += lax.dot_general(own, low, contract, preferred_element_type=jnp.float32)
    update_ref[...] = update.astype(jnp.bfloat16)


def products(tops, panels, slots):
    n = len(tops)
    rows, width = panels[0].shape
    anywhere = pl.BlockSpec(memory_space=pl.ANY)
    vmem = pl.BlockSpec(memory_space=pltpu.VMEM)
    return pl.pallas_call(
        functools.partial(product_kernel, n),
        out_shape=(
            jax.ShapeDtypeStruct((rows, width), jnp.float32),
            jax.ShapeDtypeStruct((width, width), jnp.bfloat16),
        ),
        in_specs=[pl.BlockSpec(memory_space=pltpu.SMEM)] + [anywhere] * (2 * n),
        out_specs=(vmem, vmem),
        scratch_shapes=[
            pltpu.VMEM((n,) + tops[0].shape, jnp.bfloat16),
            pltpu.VMEM((n, rows, width), jnp.bfloat16),
            pltpu.SemaphoreType.DMA((n,)),
            pltpu.SemaphoreType.DMA((n,)),
        ],
        compiler_params=pltpu.CompilerParams(vmem_limit_bytes=VMEM_LIMIT),
        name="products",
    )(slots, *tops, *panels)


def on_device(n, inverse_top, diag_inverse, cross_blocks, pattern):
    chips = n // CORES
    row, col = lax.axis_index("prow"), lax.axis_index("pcol")

    def along_chips(block, shift):
        pairs = [(((x + shift) % chips) * CORES + c, x * CORES + c) for x in range(chips) for c in range(CORES)]
        return lax.ppermute(block, "pcol", pairs)

    def other_core(block):
        pairs = [(x * CORES + (c + 1) % CORES, x * CORES + c) for x in range(chips) for c in range(CORES)]
        return lax.ppermute(block, "pcol", pairs)

    def along_rows(block, shift):
        return lax.ppermute(block, "prow", [((i + shift) % n, i) for i in range(n)])

    near = [inverse_top] + [along_chips(inverse_top, d) for d in range(1, chips)]
    tops = [block for mine in near for block in (mine, other_core(mine))]

    factor_panel = build_panel(cross_blocks, diag_inverse, pattern)
    panels = [factor_panel] + [along_rows(factor_panel, s) for s in range(1, n)]

    wanted = (row + jnp.arange(n, dtype=jnp.int32)) % n
    across = (wanted // CORES - col // CORES) % chips
    slots = across * CORES + (wanted % CORES - col % CORES) % CORES

    inverse_cross, update = products(tops, panels, slots)
    updates = [update] + [along_rows(update, s) for s in range(1, n)]
    total = functools.reduce(jnp.add, [u.astype(jnp.float32) for u in updates])
    return inverse_cross, diag_inverse + total[None]


def solution(mesh):
    placed = (
        P(("pole", "prow"), "pcol"),
        P(("pole", "pcol"), None, None),
        P(("pole", "prow"), "pcol"),
        P("prow", "pcol"),
    )
    return jax.shard_map(
        functools.partial(on_device, mesh.shape["pcol"]),
        mesh=mesh,
        in_specs=placed,
        out_specs=(P(("pole", "prow"), "pcol"), P(("pole", "pcol"), None, None)),
        check_vma=False,
    )
```

```python
import functools
import jax
import jax.numpy as jnp
from jax import lax
from jax.experimental import pallas as pl
from jax.experimental.pallas import tpu as pltpu
from jax.sharding import PartitionSpec as P

PAIR = 2
VMEM_LIMIT = 40 * 1024 * 1024
PARAMS = pltpu.CompilerParams(vmem_limit_bytes=VMEM_LIMIT)
SMEM = pl.BlockSpec(memory_space=pltpu.SMEM)
VMEM = pl.BlockSpec(memory_space=pltpu.VMEM)
ANY = pl.BlockSpec(memory_space=pl.ANY)
HBM = pl.BlockSpec(memory_space=pltpu.HBM)


def panel_kernel(pattern_ref, cross_hbm, diag_hbm, panel_ref, cross_ref, diag_ref, sems):
    width = diag_ref.shape[1]
    blocks = pattern_ref.shape[0]
    diag_copy = pltpu.make_async_copy(diag_hbm, diag_ref, sems.at[blocks])
    diag_copy.start()
    copies = []
    for a in range(blocks):
        rows = pl.ds(a * width, width)
        copies.append(pltpu.make_async_copy(cross_hbm.at[rows], cross_ref.at[rows], sems.at[a]))
        copies[a].start()
    diag_copy.wait()
    for a in range(blocks):
        copies[a].wait()
        rows = pl.ds(a * width, width)
        masked = cross_ref[rows, :] * pattern_ref[a].astype(jnp.float32)
        solved = jnp.dot(
            masked, diag_ref[0], precision=lax.Precision.HIGHEST, preferred_element_type=jnp.float32
        )
        panel_ref[rows, :] = solved.astype(jnp.bfloat16)


def build_panel(cross_blocks, diag_inverse, pattern):
    return pl.pallas_call(
        panel_kernel,
        out_shape=jax.ShapeDtypeStruct(cross_blocks.shape, jnp.bfloat16),
        in_specs=[SMEM, HBM, HBM],
        out_specs=VMEM,
        scratch_shapes=[
            pltpu.VMEM(cross_blocks.shape, jnp.float32),
            pltpu.VMEM(diag_inverse.shape, jnp.float32),
            pltpu.SemaphoreType.DMA((pattern.shape[0] + 1,)),
        ],
        compiler_params=pltpu.CompilerParams(vmem_limit_bytes=56*1024*1024),
        name="panel",
    )(pattern.reshape(-1), cross_blocks, diag_inverse)


def relay_kernel(block_ref, gate_ref, out_ref):
    del block_ref, gate_ref, out_ref


def after(block, gate):
    return pl.pallas_call(
        relay_kernel,
        out_shape=jax.ShapeDtypeStruct(block.shape, block.dtype),
        in_specs=[ANY, ANY],
        out_specs=ANY,
        input_output_aliases={0: 0},
        name="relay",
    )(block, gate)


def product_kernel(n, slots_ref, *refs):
    tops, panels = refs[:n], refs[n:2 * n]
    selected_ref, update_ref, panel_buf = refs[2 * n:]
    for s in range(n):
        panel_buf[slots_ref[s]] = panels[s][...]
    total = jnp.dot(tops[0][...], panel_buf[0], preferred_element_type=jnp.float32)
    for t in range(1, n):
        total += jnp.dot(tops[t][...], panel_buf[t], preferred_element_type=jnp.float32)
    selected_ref[...] = total
    high = total.astype(jnp.bfloat16)
    low = (total - high.astype(jnp.float32)).astype(jnp.bfloat16)
    contract = (((0,), (0,)), ((), ()))
    half = high.shape[1] // 2
    own = panels[0]
    upper = lax.dot_general(own[:, :half], high, contract, preferred_element_type=jnp.float32)
    upper += lax.dot_general(own[:, :half], low, contract, preferred_element_type=jnp.float32)
    lower = lax.dot_general(own[:, half:], high[:, half:], contract, preferred_element_type=jnp.float32)
    lower += lax.dot_general(own[:, half:], low[:, half:], contract, preferred_element_type=jnp.float32)
    update_ref[:, :2 * half] = upper.astype(jnp.bfloat16)
    update_ref[:, 2 * half:] = lower.astype(jnp.bfloat16)


def products(tops, panels, slots):
    n = len(tops)
    rows, width = panels[0].shape
    return pl.pallas_call(
        functools.partial(product_kernel, n),
        out_shape=(
            jax.ShapeDtypeStruct((rows, width), jnp.float32),
            jax.ShapeDtypeStruct((width // 2, 3 * (width // 2)), jnp.bfloat16),
        ),
        in_specs=[SMEM] + [VMEM] * (2 * n),
        out_specs=(VMEM, VMEM),
        scratch_shapes=[pltpu.VMEM((n, rows, width), jnp.bfloat16)],
        compiler_params=PARAMS,
        name="products",
    )(slots, *tops, *panels)


def finish_kernel(diag_ref, *refs):
    out_ref = refs[-1]
    total = refs[0][...].astype(jnp.float32)
    for ref in refs[1:-1]:
        total += ref[...].astype(jnp.float32)
    half = total.shape[0]
    out_ref[0, :half, :] = diag_ref[0, :half, :] + total[:, :2 * half]
    out_ref[0, half:, :half] = diag_ref[0, half:, :half] + total[:, half:2 * half].T
    out_ref[0, half:, half:] = diag_ref[0, half:, half:] + total[:, 2 * half:]


def finish(diag_inverse, updates):
    return pl.pallas_call(
        finish_kernel,
        out_shape=jax.ShapeDtypeStruct(diag_inverse.shape, jnp.float32),
        in_specs=[VMEM] * (1 + len(updates)),
        out_specs=VMEM,
        compiler_params=PARAMS,
        name="finish",
    )(diag_inverse, *updates)


def on_device(n, inverse_top, diag_inverse, cross_blocks, pattern):
    pairs = n // PAIR
    row, col = lax.axis_index("prow"), lax.axis_index("pcol")

    def from_pair(block, axis, shift, flip):
        moves = [
            (((m + shift) % pairs) * PAIR + (b ^ flip), m * PAIR + b) for m in range(pairs) for b in range(PAIR)
        ]
        return lax.ppermute(block, axis, moves)

    def mate(block, axis):
        return from_pair(block, axis, 0, 1)

    factor_panel = build_panel(cross_blocks, diag_inverse, pattern)
    crossed = [from_pair(factor_panel, "prow", d, 1) for d in range(1, pairs)]
    beside = mate(factor_panel, "prow")
    panels = [factor_panel, beside]
    for block in crossed:
        block = after(block, beside)
        panels += [mate(block, "prow"), block]

    near = [from_pair(inverse_top, "pcol", d, 0) for d in range(1, pairs)]
    tops = [inverse_top, mate(inverse_top, "pcol")]
    for block in near:
        block = after(block, panels[-1])
        tops += [block, mate(block, "pcol")]

    place = jnp.arange(n, dtype=jnp.int32)
    wanted_pair = (row // PAIR + place // PAIR) % pairs
    wanted_side = (row % PAIR) ^ (place % PAIR)
    slots = ((wanted_pair - col // PAIR) % pairs) * PAIR + (wanted_side ^ (col % PAIR))

    selected, update = products(tops, panels, slots)
    paired = (update.astype(jnp.float32) + mate(update, "prow").astype(jnp.float32)).astype(jnp.bfloat16)
    updates = [paired] + [from_pair(paired, "prow", d, 1) for d in range(1, pairs)]
    return -selected, finish(diag_inverse, updates)


def solution(mesh):
    placed = (
        P(("pole", "prow"), "pcol"),
        P(("pole", "pcol"), None, None),
        P(("pole", "prow"), "pcol"),
        P("prow", "pcol"),
    )
    return jax.shard_map(
        functools.partial(on_device, mesh.shape["pcol"]),
        mesh=mesh,
        in_specs=placed,
        out_specs=(P(("pole", "prow"), "pcol"), P(("pole", "pcol"), None, None)),
        check_vma=False,
    )
```

```python
import functools
import jax
import jax.numpy as jnp
from jax import lax
from jax.experimental import pallas as pl
from jax.experimental.pallas import tpu as pltpu
from jax.sharding import PartitionSpec as P

PAIR = 2
VMEM_LIMIT = 40 * 1024 * 1024
PARAMS = pltpu.CompilerParams(vmem_limit_bytes=VMEM_LIMIT)
WHOLE = pltpu.CompilerParams(vmem_limit_bytes=56 * 1024 * 1024)
SMALL = pltpu.CompilerParams(vmem_limit_bytes=1024 * 1024)
SMEM = pl.BlockSpec(memory_space=pltpu.SMEM)
VMEM = pl.BlockSpec(memory_space=pltpu.VMEM)
ANY = pl.BlockSpec(memory_space=pl.ANY)
HBM = pl.BlockSpec(memory_space=pltpu.HBM)


def panel_kernel(pattern_ref, cross_hbm, diag_hbm, panel_hbm, cross_ref, diag_ref, panel_ref, in_sems, out_sems):
    width = diag_ref.shape[1]
    blocks = pattern_ref.shape[0]
    rows = [pl.ds(a * width, width) for a in range(blocks)]
    diag_copy = pltpu.make_async_copy(diag_hbm, diag_ref, in_sems.at[blocks])
    diag_copy.start()
    loads = [pltpu.make_async_copy(cross_hbm.at[r], cross_ref.at[r], in_sems.at[a]) for a, r in enumerate(rows)]
    stores = [pltpu.make_async_copy(panel_ref.at[r], panel_hbm.at[r], out_sems.at[a]) for a, r in enumerate(rows)]
    for load in loads:
        load.start()
    diag_copy.wait()
    for a in range(blocks):
        loads[a].wait()
        masked = cross_ref[rows[a], :] * pattern_ref[a].astype(jnp.float32)
        solved = jnp.dot(
            masked, diag_ref[0], precision=lax.Precision.HIGHEST, preferred_element_type=jnp.float32
        )
        panel_ref[rows[a], :] = solved.astype(jnp.bfloat16)
        stores[a].start()
    for store in stores:
        store.wait()


def build_panel(cross_blocks, diag_inverse, pattern):
    return pl.pallas_call(
        panel_kernel,
        out_shape=jax.ShapeDtypeStruct(cross_blocks.shape, jnp.bfloat16),
        in_specs=[SMEM, HBM, HBM],
        out_specs=HBM,
        scratch_shapes=[
            pltpu.VMEM(cross_blocks.shape, jnp.float32),
            pltpu.VMEM(diag_inverse.shape, jnp.float32),
            pltpu.VMEM(cross_blocks.shape, jnp.bfloat16),
            pltpu.SemaphoreType.DMA((pattern.shape[0] + 1,)),
            pltpu.SemaphoreType.DMA((pattern.shape[0],)),
        ],
        compiler_params=WHOLE,
        name="panel",
    )(pattern.reshape(-1), cross_blocks, diag_inverse)


def relay_kernel(block_ref, gate_ref, out_ref):
    del block_ref, gate_ref, out_ref


def after(block, gate):
    return pl.pallas_call(
        relay_kernel,
        out_shape=jax.ShapeDtypeStruct(block.shape, block.dtype),
        in_specs=[ANY, ANY],
        out_specs=ANY,
        input_output_aliases={0: 0},
        compiler_params=SMALL,
        name="relay",
    )(block, gate)


def product_kernel(n, slots_ref, *refs):
    tops, panels = refs[:n], refs[n:2 * n]
    selected_ref, update_ref, panel_buf = refs[2 * n:]
    for s in range(n):
        panel_buf[slots_ref[s]] = panels[s][...]
    total = jnp.dot(tops[0][...], panel_buf[0], preferred_element_type=jnp.float32)
    for t in range(1, n):
        total += jnp.dot(tops[t][...], panel_buf[t], preferred_element_type=jnp.float32)
    selected_ref[...] = total
    high = total.astype(jnp.bfloat16)
    low = (total - high.astype(jnp.float32)).astype(jnp.bfloat16)
    contract = (((0,), (0,)), ((), ()))
    half = high.shape[1] // 2
    own = panels[0]
    upper = lax.dot_general(own[:, :half], high, contract, preferred_element_type=jnp.float32)
    upper += lax.dot_general(own[:, :half], low, contract, preferred_element_type=jnp.float32)
    lower = lax.dot_general(own[:, half:], high[:, half:], contract, preferred_element_type=jnp.float32)
    lower += lax.dot_general(own[:, half:], low[:, half:], contract, preferred_element_type=jnp.float32)
    update_ref[:, :2 * half] = upper.astype(jnp.bfloat16)
    update_ref[:, 2 * half:] = lower.astype(jnp.bfloat16)


def products(tops, panels, slots):
    n = len(tops)
    rows, width = panels[0].shape
    return pl.pallas_call(
        functools.partial(product_kernel, n),
        out_shape=(
            jax.ShapeDtypeStruct((rows, width), jnp.float32),
            jax.ShapeDtypeStruct((width // 2, 3 * (width // 2)), jnp.bfloat16),
        ),
        in_specs=[SMEM] + [VMEM] * (2 * n),
        out_specs=(VMEM, VMEM),
        scratch_shapes=[pltpu.VMEM((n, rows, width), jnp.bfloat16)],
        compiler_params=PARAMS,
        name="products",
    )(slots, *tops, *panels)


def finish_kernel(diag_ref, *refs):
    out_ref = refs[-1]
    total = refs[0][...].astype(jnp.float32)
    for ref in refs[1:-1]:
        total += ref[...].astype(jnp.float32)
    half = total.shape[0]
    out_ref[0, :half, :] = diag_ref[0, :half, :] + total[:, :2 * half]
    out_ref[0, half:, :half] = diag_ref[0, half:, :half] + total[:, half:2 * half].T
    out_ref[0, half:, half:] = diag_ref[0, half:, half:] + total[:, 2 * half:]


def finish(diag_inverse, updates):
    return pl.pallas_call(
        finish_kernel,
        out_shape=jax.ShapeDtypeStruct(diag_inverse.shape, jnp.float32),
        in_specs=[VMEM] * (1 + len(updates)),
        out_specs=VMEM,
        compiler_params=PARAMS,
        name="finish",
    )(diag_inverse, *updates)


def on_device(n, inverse_top, diag_inverse, cross_blocks, pattern):
    pairs = n // PAIR
    row, col = lax.axis_index("prow"), lax.axis_index("pcol")

    def from_pair(block, axis, shift, flip):
        moves = [
            (((m + shift) % pairs) * PAIR + (b ^ flip), m * PAIR + b) for m in range(pairs) for b in range(PAIR)
        ]
        return lax.ppermute(block, axis, moves)

    def mate(block, axis):
        return from_pair(block, axis, 0, 1)

    factor_panel = build_panel(cross_blocks, diag_inverse, pattern)
    crossed = [from_pair(factor_panel, "prow", d, 1) for d in range(1, pairs)]
    beside = mate(factor_panel, "prow")
    panels = [factor_panel, beside]
    for block in crossed:
        block = after(block, beside)
        panels += [mate(block, "prow"), block]

    near = [from_pair(inverse_top, "pcol", d, 0) for d in range(1, pairs)]
    tops = [inverse_top, mate(inverse_top, "pcol")]
    for block in near:
        block = after(block, beside)
        tops += [block, mate(block, "pcol")]

    place = jnp.arange(n, dtype=jnp.int32)
    wanted_pair = (row // PAIR + place // PAIR) % pairs
    wanted_side = (row % PAIR) ^ (place % PAIR)
    slots = ((wanted_pair - col // PAIR) % pairs) * PAIR + (wanted_side ^ (col % PAIR))

    selected, update = products(tops, panels, slots)
    paired = (update.astype(jnp.float32) + mate(update, "prow").astype(jnp.float32)).astype(jnp.bfloat16)
    updates = [paired] + [from_pair(paired, "prow", d, 1) for d in range(1, pairs)]
    return -selected, finish(diag_inverse, updates)


def solution(mesh):
    placed = (
        P(("pole", "prow"), "pcol"),
        P(("pole", "pcol"), None, None),
        P(("pole", "prow"), "pcol"),
        P("prow", "pcol"),
    )
    return jax.shard_map(
        functools.partial(on_device, mesh.shape["pcol"]),
        mesh=mesh,
        in_specs=placed,
        out_specs=(P(("pole", "prow"), "pcol"), P(("pole", "pcol"), None, None)),
        check_vma=False,
    )
```

```python
import functools
import jax
import jax.numpy as jnp
from jax import lax
from jax.experimental import pallas as pl
from jax.experimental.pallas import tpu as pltpu
from jax.sharding import PartitionSpec as P

PAIR = 2
VMEM_LIMIT = 40 * 1024 * 1024
PARAMS = pltpu.CompilerParams(vmem_limit_bytes=VMEM_LIMIT)
SMALL = pltpu.CompilerParams(vmem_limit_bytes=1024 * 1024)
SMEM = pl.BlockSpec(memory_space=pltpu.SMEM)
VMEM = pl.BlockSpec(memory_space=pltpu.VMEM)
ANY = pl.BlockSpec(memory_space=pl.ANY)
HBM = pl.BlockSpec(memory_space=pltpu.HBM)


def panel_kernel(pattern_hbm, cross_hbm, diag_hbm, top_hbm, panel_ref, top_ref, pattern_ref, cross_ref, diag_ref, sems):
    width = diag_ref.shape[1]
    blocks = pattern_hbm.shape[0]
    rows = [pl.ds(a * width, width) for a in range(blocks)]
    loads = [pltpu.make_async_copy(cross_hbm.at[r], cross_ref.at[r], sems.at[a]) for a, r in enumerate(rows)]
    diag_copy = pltpu.make_async_copy(diag_hbm, diag_ref, sems.at[blocks])
    pattern_copy = pltpu.make_async_copy(pattern_hbm, pattern_ref, sems.at[blocks + 1])
    top_copy = pltpu.make_async_copy(top_hbm, top_ref, sems.at[blocks + 2])
    for copy in [pattern_copy, diag_copy] + loads + [top_copy]:
        copy.start()
    pattern_copy.wait()
    diag_copy.wait()
    for a in range(blocks):
        loads[a].wait()
        masked = cross_ref[rows[a], :] * pattern_ref[a].astype(jnp.float32)
        solved = jnp.dot(
            masked, diag_ref[0], precision=lax.Precision.HIGHEST, preferred_element_type=jnp.float32
        )
        panel_ref[rows[a], :] = solved.astype(jnp.bfloat16)
    top_copy.wait()


def build_panel(cross_blocks, diag_inverse, pattern, inverse_top):
    inputs = [pattern.reshape(-1), cross_blocks, diag_inverse, inverse_top]
    return pl.pallas_call(
        panel_kernel,
        out_shape=(
            pltpu.VMEM(cross_blocks.shape, jnp.bfloat16),
            pltpu.VMEM(inverse_top.shape, inverse_top.dtype),
        ),
        in_specs=[HBM] * 4,
        out_specs=(VMEM, VMEM),
        scratch_shapes=[
            pltpu.SMEM((pattern.size,), jnp.int32),
            pltpu.VMEM(cross_blocks.shape, jnp.float32),
            pltpu.VMEM(diag_inverse.shape, jnp.float32),
            pltpu.SemaphoreType.DMA((pattern.size + 3,)),
        ],
        compiler_params=PARAMS,
        name="panel",
    )(*[pltpu.with_memory_space_constraint(x, pltpu.HBM) for x in inputs])


def relay_kernel(block_ref, gate_ref, out_ref):
    del block_ref, gate_ref, out_ref


def after(block, gate):
    return pl.pallas_call(
        relay_kernel,
        out_shape=jax.ShapeDtypeStruct(block.shape, block.dtype),
        in_specs=[ANY, ANY],
        out_specs=ANY,
        input_output_aliases={0: 0},
        compiler_params=SMALL,
        name="relay",
    )(block, gate)


def product_kernel(n, slots_ref, *refs):
    tops, panels = refs[:n], refs[n:2 * n]
    selected_ref, update_ref, panel_buf = refs[2 * n:]
    for s in range(n):
        panel_buf[slots_ref[s]] = panels[s][...]
    total = jnp.dot(tops[0][...], panel_buf[0], preferred_element_type=jnp.float32)
    for t in range(1, n):
        total += jnp.dot(tops[t][...], panel_buf[t], preferred_element_type=jnp.float32)
    selected_ref[...] = total
    high = total.astype(jnp.bfloat16)
    low = (total - high.astype(jnp.float32)).astype(jnp.bfloat16)
    contract = (((0,), (0,)), ((), ()))
    half = high.shape[1] // 2
    own = panels[0]
    upper = lax.dot_general(own[:, :half], high, contract, preferred_element_type=jnp.float32)
    upper += lax.dot_general(own[:, :half], low, contract, preferred_element_type=jnp.float32)
    lower = lax.dot_general(own[:, half:], high[:, half:], contract, preferred_element_type=jnp.float32)
    lower += lax.dot_general(own[:, half:], low[:, half:], contract, preferred_element_type=jnp.float32)
    update_ref[:, :2 * half] = upper.astype(jnp.bfloat16)
    update_ref[:, 2 * half:] = lower.astype(jnp.bfloat16)


def products(tops, panels, slots):
    n = len(tops)
    rows, width = panels[0].shape
    return pl.pallas_call(
        functools.partial(product_kernel, n),
        out_shape=(
            jax.ShapeDtypeStruct((rows, width), jnp.float32),
            jax.ShapeDtypeStruct((width // 2, 3 * (width // 2)), jnp.bfloat16),
        ),
        in_specs=[SMEM] + [VMEM] * (2 * n),
        out_specs=(VMEM, VMEM),
        scratch_shapes=[pltpu.VMEM((n, rows, width), jnp.bfloat16)],
        compiler_params=PARAMS,
        name="products",
    )(slots, *tops, *panels)


def finish_kernel(diag_ref, *refs):
    out_ref = refs[-1]
    total = refs[0][...].astype(jnp.float32)
    for ref in refs[1:-1]:
        total += ref[...].astype(jnp.float32)
    half = total.shape[0]
    out_ref[0, :half, :] = diag_ref[0, :half, :] + total[:, :2 * half]
    out_ref[0, half:, :half] = diag_ref[0, half:, :half] + total[:, half:2 * half].T
    out_ref[0, half:, half:] = diag_ref[0, half:, half:] + total[:, 2 * half:]


def finish(diag_inverse, updates):
    return pl.pallas_call(
        finish_kernel,
        out_shape=jax.ShapeDtypeStruct(diag_inverse.shape, jnp.float32),
        in_specs=[VMEM] * (1 + len(updates)),
        out_specs=VMEM,
        compiler_params=PARAMS,
        name="finish",
    )(diag_inverse, *updates)


def on_device(n, inverse_top, diag_inverse, cross_blocks, pattern):
    pairs = n // PAIR
    row, col = lax.axis_index("prow"), lax.axis_index("pcol")

    def from_pair(block, axis, shift, flip):
        moves = [
            (((m + shift) % pairs) * PAIR + (b ^ flip), m * PAIR + b) for m in range(pairs) for b in range(PAIR)
        ]
        return lax.ppermute(block, axis, moves)

    def mate(block, axis):
        return from_pair(block, axis, 0, 1)

    factor_panel, inverse_top = build_panel(cross_blocks, diag_inverse, pattern, inverse_top)
    crossed = [from_pair(factor_panel, "prow", d, 1) for d in range(1, pairs)]
    beside = mate(factor_panel, "prow")
    panels = [factor_panel, beside]
    for block in crossed:
        block = after(block, beside)
        panels += [mate(block, "prow"), block]

    near = [from_pair(inverse_top, "pcol", d, 0) for d in range(1, pairs)]
    tops = [inverse_top, mate(inverse_top, "pcol")]
    for block in near:
        block = after(block, beside)
        tops += [block, mate(block, "pcol")]

    place = jnp.arange(n, dtype=jnp.int32)
    wanted_pair = (row // PAIR + place // PAIR) % pairs
    wanted_side = (row % PAIR) ^ (place % PAIR)
    slots = ((wanted_pair - col // PAIR) % pairs) * PAIR + (wanted_side ^ (col % PAIR))

    selected, update = products(tops, panels, slots)
    paired = (update.astype(jnp.float32) + mate(update, "prow").astype(jnp.float32)).astype(jnp.bfloat16)
    updates = [paired] + [from_pair(paired, "prow", d, 1) for d in range(1, pairs)]
    return -selected, finish(diag_inverse, updates)


def solution(mesh):
    placed = (
        P(("pole", "prow"), "pcol"),
        P(("pole", "pcol"), None, None),
        P(("pole", "prow"), "pcol"),
        P("prow", "pcol"),
    )
    return jax.shard_map(
        functools.partial(on_device, mesh.shape["pcol"]),
        mesh=mesh,
        in_specs=placed,
        out_specs=(P(("pole", "prow"), "pcol"), P(("pole", "pcol"), None, None)),
        check_vma=False,
    )
```

```python
import functools
import jax
import jax.numpy as jnp
from jax import lax
from jax.experimental import pallas as pl
from jax.experimental.pallas import tpu as pltpu
from jax.sharding import PartitionSpec as P

PAIR = 2
VMEM_LIMIT = 40 * 1024 * 1024
PARAMS = pltpu.CompilerParams(vmem_limit_bytes=VMEM_LIMIT)
SMALL = pltpu.CompilerParams(vmem_limit_bytes=1024 * 1024)
SMEM = pl.BlockSpec(memory_space=pltpu.SMEM)
VMEM = pl.BlockSpec(memory_space=pltpu.VMEM)
ANY = pl.BlockSpec(memory_space=pl.ANY)
HBM = pl.BlockSpec(memory_space=pltpu.HBM)


def panel_kernel(
    pattern_hbm, cross_hbm, diag_hbm, top_hbm, first_ref, second_ref, top_ref, pattern_ref, cross_ref, diag_ref, sems
):
    width = diag_ref.shape[1]
    blocks = pattern_hbm.shape[0]
    rows = [pl.ds(a * width, width) for a in range(blocks)]
    loads = [pltpu.make_async_copy(cross_hbm.at[r], cross_ref.at[r], sems.at[a]) for a, r in enumerate(rows)]
    diag_copy = pltpu.make_async_copy(diag_hbm, diag_ref, sems.at[blocks])
    pattern_copy = pltpu.make_async_copy(pattern_hbm, pattern_ref, sems.at[blocks + 1])
    top_copy = pltpu.make_async_copy(top_hbm, top_ref, sems.at[blocks + 2])
    for copy in [pattern_copy, diag_copy] + loads + [top_copy]:
        copy.start()
    pattern_copy.wait()
    diag_copy.wait()
    for a in range(blocks):
        loads[a].wait()
        masked = cross_ref[rows[a], :] * pattern_ref[a].astype(jnp.float32)
        solved = jnp.dot(
            masked, diag_ref[0], precision=lax.Precision.HIGHEST, preferred_element_type=jnp.float32
        )
        first_ref[rows[a], :] = solved[:, : width // 2].astype(jnp.bfloat16)
        second_ref[rows[a], :] = solved[:, width // 2 :].astype(jnp.bfloat16)
    top_copy.wait()


def build_panel(cross_blocks, diag_inverse, pattern, inverse_top):
    half = (cross_blocks.shape[0], cross_blocks.shape[1] // 2)
    inputs = [pattern.reshape(-1), cross_blocks, diag_inverse, inverse_top]
    return pl.pallas_call(
        panel_kernel,
        out_shape=(
            pltpu.VMEM(half, jnp.bfloat16),
            pltpu.VMEM(half, jnp.bfloat16),
            pltpu.VMEM(inverse_top.shape, inverse_top.dtype),
        ),
        in_specs=[HBM] * 4,
        out_specs=(VMEM, VMEM, VMEM),
        scratch_shapes=[
            pltpu.SMEM((pattern.size,), jnp.int32),
            pltpu.VMEM(cross_blocks.shape, jnp.float32),
            pltpu.VMEM(diag_inverse.shape, jnp.float32),
            pltpu.SemaphoreType.DMA((pattern.size + 3,)),
        ],
        compiler_params=PARAMS,
        name="panel",
    )(*[pltpu.with_memory_space_constraint(x, pltpu.HBM) for x in inputs])


def relay_kernel(*refs):
    del refs


def after(block, *gates):
    return pl.pallas_call(
        relay_kernel,
        out_shape=jax.ShapeDtypeStruct(block.shape, block.dtype),
        in_specs=[ANY] * (1 + len(gates)),
        out_specs=ANY,
        input_output_aliases={0: 0},
        compiler_params=SMALL,
        name="relay",
    )(block, *gates)


def product_kernel(n, slots_ref, *refs):
    tops, panels, lefts = refs[:n], refs[n:2 * n], refs[2 * n:-3]
    selected_ref, update_ref, panel_buf = refs[-3:]
    for s in range(n):
        panel_buf[slots_ref[s]] = panels[s][...]
    total = jnp.dot(tops[0][...], panel_buf[0], preferred_element_type=jnp.float32)
    for t in range(1, n):
        total += jnp.dot(tops[t][...], panel_buf[t], preferred_element_type=jnp.float32)
    selected_ref[...] = total
    high = total.astype(jnp.bfloat16)
    low = (total - high.astype(jnp.float32)).astype(jnp.bfloat16)
    contract = (((0,), (0,)), ((), ()))
    half = total.shape[1]
    for p, left in enumerate(lefts):
        update = lax.dot_general(left[...], high, contract, preferred_element_type=jnp.float32)
        update += lax.dot_general(left[...], low, contract, preferred_element_type=jnp.float32)
        update_ref[p * half:(p + 1) * half, :] = update.astype(jnp.bfloat16)


def products(tops, panels, lefts, slots):
    n = len(tops)
    rows, half = panels[0].shape
    return pl.pallas_call(
        functools.partial(product_kernel, n),
        out_shape=(
            jax.ShapeDtypeStruct((rows, half), jnp.float32),
            jax.ShapeDtypeStruct((len(lefts) * half, half), jnp.bfloat16),
        ),
        in_specs=[SMEM] + [VMEM] * (2 * n + len(lefts)),
        out_specs=(VMEM, VMEM),
        scratch_shapes=[pltpu.VMEM((n, rows, half), jnp.bfloat16)],
        compiler_params=PARAMS,
        name="products",
    )(slots, *tops, *panels, *lefts)


def finish_kernel(count, diag_ref, *refs):
    out_ref = refs[-1]

    def total(parts):
        value = parts[0][...].astype(jnp.float32)
        for part in parts[1:]:
            value += part[...].astype(jnp.float32)
        return value

    left, corner = total(refs[:count]), total(refs[count:2 * count])
    half = corner.shape[0]
    out_ref[0, :, :half] = diag_ref[0, :, :half] + left
    out_ref[0, :half, half:] = diag_ref[0, :half, half:] + left[half:].T
    out_ref[0, half:, half:] = diag_ref[0, half:, half:] + corner


def finish(diag_inverse, lefts, corners):
    return pl.pallas_call(
        functools.partial(finish_kernel, len(lefts)),
        out_shape=jax.ShapeDtypeStruct(diag_inverse.shape, jnp.float32),
        in_specs=[VMEM] * (1 + len(lefts) + len(corners)),
        out_specs=VMEM,
        compiler_params=PARAMS,
        name="finish",
    )(diag_inverse, *lefts, *corners)


def on_device(n, inverse_top, diag_inverse, cross_blocks, pattern):
    pairs = n // PAIR
    row, col = lax.axis_index("prow"), lax.axis_index("pcol")

    def from_pair(block, axis, shift, flip):
        moves = [
            (((m + shift) % pairs) * PAIR + (b ^ flip), m * PAIR + b) for m in range(pairs) for b in range(PAIR)
        ]
        return lax.ppermute(block, axis, moves)

    def mate(block, axis):
        return from_pair(block, axis, 0, 1)

    def exchange(update, swapped):
        paired = (update.astype(jnp.float32) + swapped.astype(jnp.float32)).astype(jnp.bfloat16)
        return [paired] + [from_pair(paired, "prow", d, 1) for d in range(1, pairs)]

    first, second, inverse_top = build_panel(cross_blocks, diag_inverse, pattern, inverse_top)

    crossed = [from_pair(first, "prow", d, 1) for d in range(1, pairs)]
    beside = mate(first, "prow")
    crossed = [after(block, beside) for block in crossed]
    swapped = [mate(block, "prow") for block in crossed]
    later = after(second, beside)
    crossed_later = [from_pair(later, "prow", d, 1) for d in range(1, pairs)]
    beside_later = mate(later, "prow")
    crossed_later = [after(block, beside_later) for block in crossed_later]
    swapped_later = [mate(block, "prow") for block in crossed_later]

    near = [from_pair(inverse_top, "pcol", d, 0) for d in range(1, pairs)]
    tops = [inverse_top, mate(inverse_top, "pcol")]
    for block in near:
        block = after(block, swapped[0], *crossed_later)
        tops += [block, mate(block, "pcol")]

    def in_order(own, mates, blocks, others):
        return [own, mates] + [block for pair in zip(others, blocks) for block in pair]

    place = jnp.arange(n, dtype=jnp.int32)
    wanted_pair = (row // PAIR + place // PAIR) % pairs
    wanted_side = (row % PAIR) ^ (place % PAIR)
    slots = ((wanted_pair - col // PAIR) % pairs) * PAIR + (wanted_side ^ (col % PAIR))

    selected_left, update_left = products(tops, in_order(first, beside, crossed, swapped), [first, later], slots)
    swapped_left = mate(update_left, "prow")
    swapped_later = [after(block, swapped_left) for block in swapped_later]
    selected_right, corner = products(
        tops, in_order(later, beside_later, crossed_later, swapped_later), [later], slots
    )
    inverse_cross = -jnp.concatenate([selected_left, selected_right], axis=1)
    left_parts = exchange(update_left, swapped_left)
    corner_parts = exchange(corner, mate(corner, "prow"))
    return inverse_cross, finish(diag_inverse, left_parts, corner_parts)


def solution(mesh):
    placed = (
        P(("pole", "prow"), "pcol"),
        P(("pole", "pcol"), None, None),
        P(("pole", "prow"), "pcol"),
        P("prow", "pcol"),
    )
    return jax.shard_map(
        functools.partial(on_device, mesh.shape["pcol"]),
        mesh=mesh,
        in_specs=placed,
        out_specs=(P(("pole", "prow"), "pcol"), P(("pole", "pcol"), None, None)),
        check_vma=False,
    )
```

```python
import functools
import jax
import jax.numpy as jnp
from jax import lax
from jax.experimental import pallas as pl
from jax.experimental.pallas import tpu as pltpu
from jax.sharding import PartitionSpec as P

PAIR = 2
HOP_COST = 10**10
VMEM_LIMIT = 40 * 1024 * 1024
PARAMS = pltpu.CompilerParams(vmem_limit_bytes=VMEM_LIMIT)
SMALL = pltpu.CompilerParams(vmem_limit_bytes=1024 * 1024)
SMEM = pl.BlockSpec(memory_space=pltpu.SMEM)
VMEM = pl.BlockSpec(memory_space=pltpu.VMEM)
ANY = pl.BlockSpec(memory_space=pl.ANY)
HBM = pl.BlockSpec(memory_space=pltpu.HBM)


def split(value):
    high = value.astype(jnp.bfloat16)
    return high, (value - high.astype(jnp.float32)).astype(jnp.bfloat16)


def dot(left, right):
    return jnp.dot(left, right, preferred_element_type=jnp.float32)


def panel_kernel(pattern_hbm, cross_hbm, diag_hbm, top_hbm, panel_ref, top_ref, pattern_ref, cross_ref, diag_ref, sems):
    width = diag_ref.shape[1]
    blocks = pattern_hbm.shape[0]
    rows = [pl.ds(a * width, width) for a in range(blocks)]
    loads = [pltpu.make_async_copy(cross_hbm.at[r], cross_ref.at[r], sems.at[a]) for a, r in enumerate(rows)]
    diag_copy = pltpu.make_async_copy(diag_hbm, diag_ref, sems.at[blocks])
    pattern_copy = pltpu.make_async_copy(pattern_hbm, pattern_ref, sems.at[blocks + 1])
    top_copy = pltpu.make_async_copy(top_hbm, top_ref, sems.at[blocks + 2])
    for copy in [pattern_copy, diag_copy] + loads + [top_copy]:
        copy.start()
    pattern_copy.wait()
    diag_copy.wait()
    diag_high, diag_low = split(diag_ref[0])
    for a in range(blocks):
        loads[a].wait()
        high, low = split(cross_ref[rows[a], :] * pattern_ref[a].astype(jnp.float32))
        solved = dot(high, diag_high) + (dot(high, diag_low) + dot(low, diag_high))
        panel_ref[rows[a], :] = solved.astype(jnp.bfloat16)
    top_copy.wait()


def build_panel(cross_blocks, diag_inverse, pattern, inverse_top):
    inputs = [pattern.reshape(-1), cross_blocks, diag_inverse, inverse_top]
    return pl.pallas_call(
        panel_kernel,
        out_shape=(
            pltpu.VMEM(cross_blocks.shape, jnp.bfloat16),
            pltpu.VMEM(inverse_top.shape, inverse_top.dtype),
        ),
        in_specs=[HBM] * 4,
        out_specs=(VMEM, VMEM),
        scratch_shapes=[
            pltpu.SMEM((pattern.size,), jnp.int32),
            pltpu.VMEM(cross_blocks.shape, jnp.float32),
            pltpu.VMEM(diag_inverse.shape, jnp.float32),
            pltpu.SemaphoreType.DMA((pattern.size + 3,)),
        ],
        compiler_params=PARAMS,
        name="panel",
    )(*[pltpu.with_memory_space_constraint(x, pltpu.HBM) for x in inputs])


def relay_kernel(block_ref, gate_ref, out_ref):
    del block_ref, gate_ref, out_ref


def after(block, gate, cost=0):
    return pl.pallas_call(
        relay_kernel,
        out_shape=jax.ShapeDtypeStruct(block.shape, block.dtype),
        in_specs=[ANY, ANY],
        out_specs=ANY,
        input_output_aliases={0: 0},
        compiler_params=SMALL,
        cost_estimate=pl.CostEstimate(flops=cost, bytes_accessed=cost // 256, transcendentals=0),
        name="relay",
    )(block, gate)


def partial_kernel(n, slots_ref, *refs):
    tops, panels = refs[:n], refs[n:n + n // 2 + 1]
    partial_ref, chosen_ref, turned_ref, panel_buf = refs[n + n // 2 + 1:]
    places = [0] + list(range(1, n, 2))
    for place, panel in zip(places, panels):
        panel_buf[slots_ref[place]] = panel[...]
    for d, place in enumerate(range(2, n, 2)):
        slot = slots_ref[place]
        panel_buf[slot] = jnp.zeros(panel_buf.shape[1:], panel_buf.dtype)
        for t in range(n):
            @pl.when(slot == t)
            def _():
                chosen_ref[d] = tops[t][...]
    total = dot(tops[0][...], panel_buf[0])
    for t in range(1, n):
        total += dot(tops[t][...], panel_buf[t])
    partial_ref[...] = total
    turned_ref[...] = panels[0][...].astype(jnp.float32).T.astype(jnp.bfloat16)


def partial_product(tops, panels, slots):
    n = len(tops)
    rows, width = panels[0].shape
    return pl.pallas_call(
        functools.partial(partial_kernel, n),
        out_shape=(
            jax.ShapeDtypeStruct((rows, width), jnp.float32),
            jax.ShapeDtypeStruct((n // 2 - 1,) + tops[0].shape, jnp.bfloat16),
            jax.ShapeDtypeStruct((width, rows), jnp.bfloat16),
        ),
        in_specs=[SMEM] + [VMEM] * (n + len(panels)),
        out_specs=(VMEM, VMEM, VMEM),
        scratch_shapes=[pltpu.VMEM((n, rows, width), jnp.bfloat16)],
        compiler_params=PARAMS,
        cost_estimate=pl.CostEstimate(
            flops=2 * n * rows * rows * width, bytes_accessed=2 * n * rows * (rows + width), transcendentals=0
        ),
        name="partial",
    )(slots, *tops, *panels)


def product_kernel(partial_ref, chosen_ref, turned_ref, *refs):
    panels, (selected_ref, update_ref) = refs[:-2], refs[-2:]
    total = partial_ref[...]
    for d, panel in enumerate(panels):
        total += dot(chosen_ref[d], panel[...])
    selected_ref[...] = total
    rounded = total.astype(jnp.bfloat16)
    half = rounded.shape[1] // 2
    update_ref[:, :2 * half] = dot(turned_ref[:half], rounded).astype(jnp.bfloat16)
    update_ref[:, 2 * half:] = dot(turned_ref[half:], rounded[:, half:]).astype(jnp.bfloat16)


def products(partial, chosen, turned, panels):
    rows, width = panels[0].shape
    return pl.pallas_call(
        product_kernel,
        out_shape=(
            jax.ShapeDtypeStruct((rows, width), jnp.float32),
            jax.ShapeDtypeStruct((width // 2, 3 * (width // 2)), jnp.bfloat16),
        ),
        in_specs=[VMEM] * (3 + len(panels)),
        out_specs=(VMEM, VMEM),
        compiler_params=PARAMS,
        name="products",
    )(partial, chosen, turned, *panels)


def finish_kernel(diag_ref, *refs):
    out_ref = refs[-1]
    total = refs[0][...].astype(jnp.float32)
    for ref in refs[1:-1]:
        total += ref[...].astype(jnp.float32)
    half = total.shape[0]
    out_ref[0, :half, :] = diag_ref[0, :half, :] + total[:, :2 * half]
    out_ref[0, half:, :half] = diag_ref[0, half:, :half] + total[:, half:2 * half].T
    out_ref[0, half:, half:] = diag_ref[0, half:, half:] + total[:, 2 * half:]


def finish(diag_inverse, updates):
    return pl.pallas_call(
        finish_kernel,
        out_shape=jax.ShapeDtypeStruct(diag_inverse.shape, jnp.float32),
        in_specs=[VMEM] * (1 + len(updates)),
        out_specs=VMEM,
        compiler_params=PARAMS,
        name="finish",
    )(diag_inverse, *updates)


def on_device(n, inverse_top, diag_inverse, cross_blocks, pattern):
    pairs = n // PAIR
    row, col = lax.axis_index("prow"), lax.axis_index("pcol")

    def from_pair(block, axis, shift, flip):
        moves = [
            (((m + shift) % pairs) * PAIR + (b ^ flip), m * PAIR + b) for m in range(pairs) for b in range(PAIR)
        ]
        return lax.ppermute(block, axis, moves)

    def mate(block, axis):
        return from_pair(block, axis, 0, 1)

    factor_panel, inverse_top = build_panel(cross_blocks, diag_inverse, pattern, inverse_top)
    beside = mate(factor_panel, "prow")
    crossed = [from_pair(factor_panel, "prow", d, 1) for d in range(1, pairs)]
    crossed = [after(block, beside, HOP_COST) for block in crossed]
    swapped = [mate(block, "prow") for block in crossed]

    near = [from_pair(inverse_top, "pcol", d, 0) for d in range(1, pairs)]
    tops = [inverse_top, mate(inverse_top, "pcol")]
    for block in near:
        block = after(block, crossed[-1])
        tops += [block, mate(block, "pcol")]

    place = jnp.arange(n, dtype=jnp.int32)
    wanted_pair = (row // PAIR + place // PAIR) % pairs
    wanted_side = (row % PAIR) ^ (place % PAIR)
    slots = ((wanted_pair - col // PAIR) % pairs) * PAIR + (wanted_side ^ (col % PAIR))

    parts = partial_product(tops, [factor_panel, beside] + crossed, slots)
    selected, update = products(*parts, swapped)
    paired = (update.astype(jnp.float32) + mate(update, "prow").astype(jnp.float32)).astype(jnp.bfloat16)
    updates = [paired] + [from_pair(paired, "prow", d, 1) for d in range(1, pairs)]
    return -selected, finish(diag_inverse, updates)


def solution(mesh):
    placed = (
        P(("pole", "prow"), "pcol"),
        P(("pole", "pcol"), None, None),
        P(("pole", "prow"), "pcol"),
        P("prow", "pcol"),
    )
    return jax.shard_map(
        functools.partial(on_device, mesh.shape["pcol"]),
        mesh=mesh,
        in_specs=placed,
        out_specs=(P(("pole", "prow"), "pcol"), P(("pole", "pcol"), None, None)),
        check_vma=False,
    )
```

```python
import functools
import jax
import jax.numpy as jnp
from jax import lax
from jax.experimental import pallas as pl
from jax.experimental.pallas import tpu as pltpu
from jax.sharding import PartitionSpec as P

PAIR = 2
HOP_COST = 10**10
VMEM_LIMIT = 40 * 1024 * 1024
PARAMS = pltpu.CompilerParams(vmem_limit_bytes=VMEM_LIMIT)
SMALL = pltpu.CompilerParams(vmem_limit_bytes=1024 * 1024)
SMEM = pl.BlockSpec(memory_space=pltpu.SMEM)
VMEM = pl.BlockSpec(memory_space=pltpu.VMEM)
ANY = pl.BlockSpec(memory_space=pl.ANY)
HBM = pl.BlockSpec(memory_space=pltpu.HBM)


def split(value):
    high = value.astype(jnp.bfloat16)
    return high, (value - high.astype(jnp.float32)).astype(jnp.bfloat16)


def dot(left, right):
    return jnp.dot(left, right, preferred_element_type=jnp.float32)


def panel_kernel(pattern_hbm, cross_hbm, diag_hbm, top_hbm, panel_ref, top_ref, pattern_ref, cross_ref, diag_ref, sems):
    width = diag_ref.shape[1]
    blocks = pattern_hbm.shape[0]
    rows = [pl.ds(a * width, width) for a in range(blocks)]
    loads = [pltpu.make_async_copy(cross_hbm.at[r], cross_ref.at[r], sems.at[a]) for a, r in enumerate(rows)]
    diag_copy = pltpu.make_async_copy(diag_hbm, diag_ref, sems.at[blocks])
    pattern_copy = pltpu.make_async_copy(pattern_hbm, pattern_ref, sems.at[blocks + 1])
    top_copy = pltpu.make_async_copy(top_hbm, top_ref, sems.at[blocks + 2])
    for copy in [pattern_copy, diag_copy] + loads + [top_copy]:
        copy.start()
    pattern_copy.wait()
    diag_copy.wait()
    diag_high, diag_low = split(diag_ref[0])
    for a in range(blocks):
        loads[a].wait()
        high, low = split(cross_ref[rows[a], :] * pattern_ref[a].astype(jnp.float32))
        solved = dot(high, diag_high) + (dot(high, diag_low) + dot(low, diag_high))
        panel_ref[rows[a], :] = solved.astype(jnp.bfloat16)
    top_copy.wait()


def build_panel(cross_blocks, diag_inverse, pattern, inverse_top):
    inputs = [pattern.reshape(-1), cross_blocks, diag_inverse, inverse_top]
    return pl.pallas_call(
        panel_kernel,
        out_shape=(
            pltpu.VMEM(cross_blocks.shape, jnp.bfloat16),
            pltpu.VMEM(inverse_top.shape, inverse_top.dtype),
        ),
        in_specs=[HBM] * 4,
        out_specs=(VMEM, VMEM),
        scratch_shapes=[
            pltpu.SMEM((pattern.size,), jnp.int32),
            pltpu.VMEM(cross_blocks.shape, jnp.float32),
            pltpu.VMEM(diag_inverse.shape, jnp.float32),
            pltpu.SemaphoreType.DMA((pattern.size + 3,)),
        ],
        compiler_params=PARAMS,
        name="panel",
    )(*[pltpu.with_memory_space_constraint(x, pltpu.HBM) for x in inputs])


def relay_kernel(block_ref, gate_ref, out_ref):
    del block_ref, gate_ref, out_ref


def after(block, gate, cost=0):
    return pl.pallas_call(
        relay_kernel,
        out_shape=jax.ShapeDtypeStruct(block.shape, block.dtype),
        in_specs=[ANY, ANY],
        out_specs=ANY,
        input_output_aliases={0: 0},
        compiler_params=SMALL,
        cost_estimate=pl.CostEstimate(flops=cost, bytes_accessed=cost // 256, transcendentals=0),
        name="relay",
    )(block, gate)


def store_upper(out_ref, update):
    half = update.shape[0] // 2
    out_ref[:, :2 * half] = update[:half].astype(jnp.bfloat16)
    out_ref[:, 2 * half:] = update[half:, half:].astype(jnp.bfloat16)


def partial_kernel(n, slots_ref, *refs):
    tops, panels = refs[:n], refs[n:n + n // 2 + 1]
    partial_ref, chosen_ref, turned_ref, update_ref, panel_buf = refs[n + n // 2 + 1:]
    places = [0] + list(range(1, n, 2))
    for place, panel in zip(places, panels):
        panel_buf[slots_ref[place]] = panel[...]
    for d, place in enumerate(range(2, n, 2)):
        slot = slots_ref[place]
        panel_buf[slot] = jnp.zeros(panel_buf.shape[1:], panel_buf.dtype)
        for t in range(n):
            @pl.when(slot == t)
            def _():
                chosen_ref[d] = tops[t][...]
    total = dot(tops[0][...], panel_buf[0])
    for t in range(1, n):
        total += dot(tops[t][...], panel_buf[t])
    partial_ref[...] = total
    turned = panels[0][...].astype(jnp.float32).T.astype(jnp.bfloat16)
    turned_ref[...] = turned
    store_upper(update_ref, dot(turned, total.astype(jnp.bfloat16)))


def partial_product(tops, panels, slots):
    n = len(tops)
    rows, width = panels[0].shape
    return pl.pallas_call(
        functools.partial(partial_kernel, n),
        out_shape=(
            jax.ShapeDtypeStruct((rows, width), jnp.float32),
            jax.ShapeDtypeStruct((n // 2 - 1,) + tops[0].shape, jnp.bfloat16),
            jax.ShapeDtypeStruct((width, rows), jnp.bfloat16),
            jax.ShapeDtypeStruct((width // 2, 3 * (width // 2)), jnp.bfloat16),
        ),
        in_specs=[SMEM] + [VMEM] * (n + len(panels)),
        out_specs=(VMEM, VMEM, VMEM, VMEM),
        scratch_shapes=[pltpu.VMEM((n, rows, width), jnp.bfloat16)],
        compiler_params=PARAMS,
        cost_estimate=pl.CostEstimate(
            flops=2 * n * rows * rows * width, bytes_accessed=2 * n * rows * (rows + width), transcendentals=0
        ),
        name="partial",
    )(slots, *tops, *panels)


def product_kernel(alone, partial_ref, chosen_ref, turned_ref, *refs):
    panels, (selected_ref, update_ref) = refs[:-2], refs[-2:]
    rest = dot(chosen_ref[0], panels[0][...])
    for d, panel in enumerate(panels[1:], 1):
        rest += dot(chosen_ref[d], panel[...])
    selected_ref[...] = partial_ref[...] + rest
    update = dot(turned_ref[...], rest.astype(jnp.bfloat16))
    if alone:
        update += update.T
    store_upper(update_ref, update)


def products(partial, chosen, turned, panels):
    rows, width = panels[0].shape
    return pl.pallas_call(
        functools.partial(product_kernel, len(panels) == 1),
        out_shape=(
            jax.ShapeDtypeStruct((rows, width), jnp.float32),
            jax.ShapeDtypeStruct((width // 2, 3 * (width // 2)), jnp.bfloat16),
        ),
        in_specs=[VMEM] * (3 + len(panels)),
        out_specs=(VMEM, VMEM),
        compiler_params=PARAMS,
        name="products",
    )(partial, chosen, turned, *panels)


def finish_kernel(diag_ref, *refs):
    out_ref = refs[-1]
    total = refs[0][...].astype(jnp.float32)
    for ref in refs[1:-1]:
        total += ref[...].astype(jnp.float32)
    half = total.shape[0]
    out_ref[0, :half, :] = diag_ref[0, :half, :] + total[:, :2 * half]
    out_ref[0, half:, :half] = diag_ref[0, half:, :half] + total[:, half:2 * half].T
    out_ref[0, half:, half:] = diag_ref[0, half:, half:] + total[:, 2 * half:]


def finish(diag_inverse, updates):
    return pl.pallas_call(
        finish_kernel,
        out_shape=jax.ShapeDtypeStruct(diag_inverse.shape, jnp.float32),
        in_specs=[VMEM] * (1 + len(updates)),
        out_specs=VMEM,
        compiler_params=PARAMS,
        name="finish",
    )(diag_inverse, *updates)


def on_device(n, inverse_top, diag_inverse, cross_blocks, pattern):
    pairs = n // PAIR
    row, col = lax.axis_index("prow"), lax.axis_index("pcol")

    def from_pair(block, axis, shift, flip):
        moves = [
            (((m + shift) % pairs) * PAIR + (b ^ flip), m * PAIR + b) for m in range(pairs) for b in range(PAIR)
        ]
        return lax.ppermute(block, axis, moves)

    def mate(block, axis):
        return from_pair(block, axis, 0, 1)

    factor_panel, inverse_top = build_panel(cross_blocks, diag_inverse, pattern, inverse_top)
    beside = mate(factor_panel, "prow")
    crossed = [from_pair(factor_panel, "prow", d, 1) for d in range(1, pairs)]
    crossed = [after(block, beside, HOP_COST) for block in crossed]
    swapped = [mate(block, "prow") for block in crossed]

    near = [from_pair(inverse_top, "pcol", d, 0) for d in range(1, pairs)]
    tops = [inverse_top, mate(inverse_top, "pcol")]
    for block in near:
        block = after(block, crossed[-1])
        tops += [block, mate(block, "pcol")]

    place = jnp.arange(n, dtype=jnp.int32)
    wanted_pair = (row // PAIR + place // PAIR) % pairs
    wanted_side = (row % PAIR) ^ (place % PAIR)
    slots = ((wanted_pair - col // PAIR) % pairs) * PAIR + (wanted_side ^ (col % PAIR))

    partial, chosen, turned, early = partial_product(tops, [factor_panel, beside] + crossed, slots)
    arrived = after(mate(early, "prow"), swapped[-1])
    early = (early.astype(jnp.float32) + arrived.astype(jnp.float32)).astype(jnp.bfloat16)
    updates = [early] + [after(from_pair(early, "prow", d, 1), early, HOP_COST) for d in range(1, pairs)]

    swapped = [after(block, early) for block in swapped]
    selected, late = products(partial, chosen, turned, swapped)
    if pairs > 2:
        parts = [late] + [from_pair(late, "prow", d, 0) for d in range(1, pairs)]
        late = functools.reduce(jnp.add, [part.astype(jnp.float32) for part in parts]).astype(jnp.bfloat16)
    updates += [late, mate(late, "prow")]
    return -selected, finish(diag_inverse, updates)


def solution(mesh):
    placed = (
        P(("pole", "prow"), "pcol"),
        P(("pole", "pcol"), None, None),
        P(("pole", "prow"), "pcol"),
        P("prow", "pcol"),
    )
    return jax.shard_map(
        functools.partial(on_device, mesh.shape["pcol"]),
        mesh=mesh,
        in_specs=placed,
        out_specs=(P(("pole", "prow"), "pcol"), P(("pole", "pcol"), None, None)),
        check_vma=False,
    )
```

```python
import functools
import jax
import jax.numpy as jnp
from jax import lax
from jax.experimental import pallas as pl
from jax.experimental.pallas import tpu as pltpu
from jax.sharding import PartitionSpec as P

PAIR = 2
HOP_COST = 10**10
VMEM_LIMIT = 40 * 1024 * 1024
PARAMS = pltpu.CompilerParams(vmem_limit_bytes=VMEM_LIMIT)
SMALL = pltpu.CompilerParams(vmem_limit_bytes=1024 * 1024)
SMEM = pl.BlockSpec(memory_space=pltpu.SMEM)
VMEM = pl.BlockSpec(memory_space=pltpu.VMEM)
ANY = pl.BlockSpec(memory_space=pl.ANY)
HBM = pl.BlockSpec(memory_space=pltpu.HBM)


def split(value):
    high = value.astype(jnp.bfloat16)
    return high, (value - high.astype(jnp.float32)).astype(jnp.bfloat16)


def dot(left, right):
    return jnp.dot(left, right, preferred_element_type=jnp.float32)


def panel_kernel(pattern_hbm, cross_hbm, diag_hbm, top_hbm, panel_ref, top_ref, pattern_ref, cross_ref, diag_ref, sems):
    width = diag_ref.shape[1]
    blocks = pattern_hbm.shape[0]
    rows = [pl.ds(a * width, width) for a in range(blocks)]
    loads = [pltpu.make_async_copy(cross_hbm.at[r], cross_ref.at[r], sems.at[a]) for a, r in enumerate(rows)]
    diag_copy = pltpu.make_async_copy(diag_hbm, diag_ref, sems.at[blocks])
    pattern_copy = pltpu.make_async_copy(pattern_hbm, pattern_ref, sems.at[blocks + 1])
    top_copy = pltpu.make_async_copy(top_hbm, top_ref, sems.at[blocks + 2])
    for copy in [pattern_copy, diag_copy] + loads + [top_copy]:
        copy.start()
    pattern_copy.wait()
    diag_copy.wait()
    diag_high, diag_low = split(diag_ref[0])
    for a in range(blocks):
        loads[a].wait()
        high, low = split(cross_ref[rows[a], :] * pattern_ref[a].astype(jnp.float32))
        solved = dot(high, diag_high) + (dot(high, diag_low) + dot(low, diag_high))
        panel_ref[rows[a], :] = solved.astype(jnp.bfloat16)
    top_copy.wait()


def build_panel(cross_blocks, diag_inverse, pattern, inverse_top):
    inputs = [pattern.reshape(-1), cross_blocks, diag_inverse, inverse_top]
    return pl.pallas_call(
        panel_kernel,
        out_shape=(
            pltpu.VMEM(cross_blocks.shape, jnp.bfloat16),
            pltpu.VMEM(inverse_top.shape, inverse_top.dtype),
        ),
        in_specs=[HBM] * 4,
        out_specs=(VMEM, VMEM),
        scratch_shapes=[
            pltpu.SMEM((pattern.size,), jnp.int32),
            pltpu.VMEM(cross_blocks.shape, jnp.float32),
            pltpu.VMEM(diag_inverse.shape, jnp.float32),
            pltpu.SemaphoreType.DMA((pattern.size + 3,)),
        ],
        compiler_params=PARAMS,
        name="panel",
    )(*[pltpu.with_memory_space_constraint(x, pltpu.HBM) for x in inputs])


def relay_kernel(block_ref, gate_ref, out_ref):
    del block_ref, gate_ref, out_ref


def after(block, gate, cost=0):
    return pl.pallas_call(
        relay_kernel,
        out_shape=jax.ShapeDtypeStruct(block.shape, block.dtype),
        in_specs=[ANY, ANY],
        out_specs=ANY,
        input_output_aliases={0: 0},
        compiler_params=SMALL,
        cost_estimate=pl.CostEstimate(flops=cost, bytes_accessed=cost // 256, transcendentals=0),
        name="relay",
    )(block, gate)


def store_upper(out_ref, update, *others):
    half = update.shape[0] // 2
    for columns, value in ((pl.ds(0, 2 * half), update[:half]), (pl.ds(2 * half, half), update[half:, half:])):
        for other in others:
            value += other[:, columns].astype(jnp.float32)
        out_ref[:, columns] = value.astype(jnp.bfloat16)


def partial_kernel(n, slots_ref, *refs):
    tops, panels = refs[:n], refs[n:n + n // 2 + 1]
    partial_ref, chosen_ref, turned_ref, update_ref, panel_buf = refs[n + n // 2 + 1:]
    places = [0] + list(range(1, n, 2))
    for place, panel in zip(places, panels):
        panel_buf[slots_ref[place]] = panel[...]
    for d, place in enumerate(range(2, n, 2)):
        slot = slots_ref[place]
        panel_buf[slot] = jnp.zeros(panel_buf.shape[1:], panel_buf.dtype)
        for t in range(n):
            @pl.when(slot == t)
            def _():
                chosen_ref[d] = tops[t][...]
    total = dot(tops[0][...], panel_buf[0])
    for t in range(1, n):
        total += dot(tops[t][...], panel_buf[t])
    partial_ref[...] = total
    turned = panels[0][...].astype(jnp.float32).T.astype(jnp.bfloat16)
    turned_ref[...] = turned
    store_upper(update_ref, dot(turned, total.astype(jnp.bfloat16)))


def partial_product(tops, panels, slots):
    n = len(tops)
    rows, width = panels[0].shape
    return pl.pallas_call(
        functools.partial(partial_kernel, n),
        out_shape=(
            jax.ShapeDtypeStruct((rows, width), jnp.float32),
            jax.ShapeDtypeStruct((n // 2 - 1,) + tops[0].shape, jnp.bfloat16),
            jax.ShapeDtypeStruct((width, rows), jnp.bfloat16),
            jax.ShapeDtypeStruct((width // 2, 3 * (width // 2)), jnp.bfloat16),
        ),
        in_specs=[SMEM] + [VMEM] * (n + len(panels)),
        out_specs=(VMEM, VMEM, VMEM, VMEM),
        scratch_shapes=[pltpu.VMEM((n, rows, width), jnp.bfloat16)],
        compiler_params=PARAMS,
        cost_estimate=pl.CostEstimate(
            flops=2 * n * rows * rows * width, bytes_accessed=2 * n * rows * (rows + width), transcendentals=0
        ),
        name="partial",
    )(slots, *tops, *panels)


def product_kernel(count, alone, partial_ref, chosen_ref, turned_ref, *refs):
    panels, early, (selected_ref, update_ref) = refs[:count], refs[count:-2], refs[-2:]
    rest = dot(chosen_ref[0], panels[0][...])
    for d, panel in enumerate(panels[1:], 1):
        rest += dot(chosen_ref[d], panel[...])
    selected_ref[...] = partial_ref[...] + rest
    update = dot(turned_ref[...], rest.astype(jnp.bfloat16))
    if alone:
        update += update.T
    store_upper(update_ref, update, *early)


def products(partial, chosen, turned, panels, early):
    rows, width = panels[0].shape
    alone = len(panels) == 1
    return pl.pallas_call(
        functools.partial(product_kernel, len(panels), alone),
        out_shape=(
            jax.ShapeDtypeStruct((rows, width), jnp.float32),
            jax.ShapeDtypeStruct((width // 2, 3 * (width // 2)), jnp.bfloat16),
        ),
        in_specs=[VMEM] * (3 + len(panels) + len(early)),
        out_specs=(VMEM, VMEM),
        compiler_params=PARAMS,
        name="products",
    )(partial, chosen, turned, *panels, *early)


def finish_kernel(diag_ref, *refs):
    out_ref = refs[-1]
    total = refs[0][...].astype(jnp.float32)
    for ref in refs[1:-1]:
        total += ref[...].astype(jnp.float32)
    half = total.shape[0]
    out_ref[0, :half, :] = diag_ref[0, :half, :] + total[:, :2 * half]
    out_ref[0, half:, :half] = diag_ref[0, half:, :half] + total[:, half:2 * half].T
    out_ref[0, half:, half:] = diag_ref[0, half:, half:] + total[:, 2 * half:]


def finish(diag_inverse, updates):
    return pl.pallas_call(
        finish_kernel,
        out_shape=jax.ShapeDtypeStruct(diag_inverse.shape, jnp.float32),
        in_specs=[VMEM] * (1 + len(updates)),
        out_specs=VMEM,
        compiler_params=PARAMS,
        name="finish",
    )(diag_inverse, *updates)


def on_device(n, inverse_top, diag_inverse, cross_blocks, pattern):
    pairs = n // PAIR
    row, col = lax.axis_index("prow"), lax.axis_index("pcol")

    def from_pair(block, axis, shift, flip):
        moves = [
            (((m + shift) % pairs) * PAIR + (b ^ flip), m * PAIR + b) for m in range(pairs) for b in range(PAIR)
        ]
        return lax.ppermute(block, axis, moves)

    def mate(block, axis):
        return from_pair(block, axis, 0, 1)

    factor_panel, inverse_top = build_panel(cross_blocks, diag_inverse, pattern, inverse_top)
    beside = mate(factor_panel, "prow")
    crossed = [from_pair(factor_panel, "prow", d, 1) for d in range(1, pairs)]
    crossed = [after(block, beside, HOP_COST) for block in crossed]
    swapped = [mate(block, "prow") for block in crossed]

    near = [from_pair(inverse_top, "pcol", d, 0) for d in range(1, pairs)]
    tops = [inverse_top, mate(inverse_top, "pcol")]
    for block in near:
        block = after(block, crossed[-1])
        tops += [block, mate(block, "pcol")]

    place = jnp.arange(n, dtype=jnp.int32)
    wanted_pair = (row // PAIR + place // PAIR) % pairs
    wanted_side = (row % PAIR) ^ (place % PAIR)
    slots = ((wanted_pair - col // PAIR) % pairs) * PAIR + (wanted_side ^ (col % PAIR))

    partial, chosen, turned, early = partial_product(tops, [factor_panel, beside] + crossed, slots)
    early = [early] + [after(from_pair(early, "prow", d, 1), swapped[-1]) for d in range(1, pairs)]
    if pairs > 2:
        selected, late = products(partial, chosen, turned, swapped, [])
        parts = early + [late] + [from_pair(late, "prow", d, 0) for d in range(1, pairs)]
        update = functools.reduce(jnp.add, [part.astype(jnp.float32) for part in parts]).astype(jnp.bfloat16)
    else:
        selected, update = products(partial, chosen, turned, swapped, early)
    return -selected, finish(diag_inverse, [update, mate(update, "prow")])


def solution(mesh):
    placed = (
        P(("pole", "prow"), "pcol"),
        P(("pole", "pcol"), None, None),
        P(("pole", "prow"), "pcol"),
        P("prow", "pcol"),
    )
    return jax.shard_map(
        functools.partial(on_device, mesh.shape["pcol"]),
        mesh=mesh,
        in_specs=placed,
        out_specs=(P(("pole", "prow"), "pcol"), P(("pole", "pcol"), None, None)),
        check_vma=False,
    )
```

```python
import functools
import jax
import jax.numpy as jnp
from jax import lax
from jax.experimental import pallas as pl
from jax.experimental.pallas import tpu as pltpu
from jax.sharding import PartitionSpec as P

PAIR = 2
HOP_COST = 10**10
VMEM_LIMIT = 40 * 1024 * 1024
PARAMS = pltpu.CompilerParams(vmem_limit_bytes=VMEM_LIMIT)
SMALL = pltpu.CompilerParams(vmem_limit_bytes=1024 * 1024)
SMEM = pl.BlockSpec(memory_space=pltpu.SMEM)
VMEM = pl.BlockSpec(memory_space=pltpu.VMEM)
ANY = pl.BlockSpec(memory_space=pl.ANY)
HBM = pl.BlockSpec(memory_space=pltpu.HBM)


def split(value):
    high = value.astype(jnp.bfloat16)
    return high, (value - high.astype(jnp.float32)).astype(jnp.bfloat16)


def dot(left, right):
    return jnp.dot(left, right, preferred_element_type=jnp.float32)


def panel_kernel(pattern_hbm, cross_hbm, diag_hbm, top_hbm, panel_ref, top_ref, pattern_ref, cross_ref, diag_ref, sems):
    width = diag_ref.shape[1]
    blocks = pattern_hbm.shape[0]
    rows = [pl.ds(a * width, width) for a in range(blocks)]
    loads = [pltpu.make_async_copy(cross_hbm.at[r], cross_ref.at[r], sems.at[a]) for a, r in enumerate(rows)]
    diag_copy = pltpu.make_async_copy(diag_hbm, diag_ref, sems.at[blocks])
    pattern_copy = pltpu.make_async_copy(pattern_hbm, pattern_ref, sems.at[blocks + 1])
    top_copy = pltpu.make_async_copy(top_hbm, top_ref, sems.at[blocks + 2])
    for copy in [pattern_copy, diag_copy] + loads + [top_copy]:
        copy.start()
    pattern_copy.wait()
    diag_copy.wait()
    diag_high, diag_low = split(diag_ref[0])
    for a in range(blocks):
        loads[a].wait()
        high, low = split(cross_ref[rows[a], :] * pattern_ref[a].astype(jnp.float32))
        solved = dot(high, diag_high) + (dot(high, diag_low) + dot(low, diag_high))
        panel_ref[rows[a], :] = solved.astype(jnp.bfloat16)
    top_copy.wait()


def build_panel(cross_blocks, diag_inverse, pattern, inverse_top):
    inputs = [pattern.reshape(-1), cross_blocks, diag_inverse, inverse_top]
    return pl.pallas_call(
        panel_kernel,
        out_shape=(
            pltpu.VMEM(cross_blocks.shape, jnp.bfloat16),
            pltpu.VMEM(inverse_top.shape, inverse_top.dtype),
        ),
        in_specs=[HBM] * 4,
        out_specs=(VMEM, VMEM),
        scratch_shapes=[
            pltpu.SMEM((pattern.size,), jnp.int32),
            pltpu.VMEM(cross_blocks.shape, jnp.float32),
            pltpu.VMEM(diag_inverse.shape, jnp.float32),
            pltpu.SemaphoreType.DMA((pattern.size + 3,)),
        ],
        compiler_params=PARAMS,
        name="panel",
    )(*[pltpu.with_memory_space_constraint(x, pltpu.HBM) for x in inputs])


def relay_kernel(*refs):
    del refs


def after(block, *gates, cost=0):
    return pl.pallas_call(
        relay_kernel,
        out_shape=jax.ShapeDtypeStruct(block.shape, block.dtype),
        in_specs=[ANY] * (1 + len(gates)),
        out_specs=ANY,
        input_output_aliases={0: 0},
        compiler_params=SMALL,
        cost_estimate=pl.CostEstimate(flops=cost, bytes_accessed=cost // 256, transcendentals=0),
        name="relay",
    )(block, *gates)


def store_upper(out_ref, update, *others):
    half = update.shape[0] // 2
    for columns, value in ((pl.ds(0, 2 * half), update[:half]), (pl.ds(2 * half, half), update[half:, half:])):
        for other in others:
            value += other[:, columns].astype(jnp.float32)
        out_ref[:, columns] = value.astype(jnp.bfloat16)


def partial_kernel(n, slots_ref, *refs):
    tops, panels = refs[:n], refs[n:n + n // 2 + 1]
    partial_ref, chosen_ref, turned_ref, update_ref, panel_buf = refs[n + n // 2 + 1:]
    places = [0] + list(range(1, n, 2))
    for place, panel in zip(places, panels):
        panel_buf[slots_ref[place]] = panel[...]
    for d, place in enumerate(range(2, n, 2)):
        slot = slots_ref[place]
        panel_buf[slot] = jnp.zeros(panel_buf.shape[1:], panel_buf.dtype)
        for t in range(n):
            @pl.when(slot == t)
            def _():
                chosen_ref[d] = tops[t][...]
    total = dot(tops[0][...], panel_buf[0])
    for t in range(1, n):
        total += dot(tops[t][...], panel_buf[t])
    partial_ref[...] = total
    turned = panels[0][...].astype(jnp.float32).T.astype(jnp.bfloat16)
    turned_ref[...] = turned
    store_upper(update_ref, dot(turned, total.astype(jnp.bfloat16)))


def partial_product(tops, panels, slots):
    n = len(tops)
    rows, width = panels[0].shape
    return pl.pallas_call(
        functools.partial(partial_kernel, n),
        out_shape=(
            jax.ShapeDtypeStruct((rows, width), jnp.float32),
            jax.ShapeDtypeStruct((n // 2 - 1,) + tops[0].shape, jnp.bfloat16),
            jax.ShapeDtypeStruct((width, rows), jnp.bfloat16),
            jax.ShapeDtypeStruct((width // 2, 3 * (width // 2)), jnp.bfloat16),
        ),
        in_specs=[SMEM] + [VMEM] * (n + len(panels)),
        out_specs=(VMEM, VMEM, VMEM, VMEM),
        scratch_shapes=[pltpu.VMEM((n, rows, width), jnp.bfloat16)],
        compiler_params=PARAMS,
        cost_estimate=pl.CostEstimate(
            flops=2 * n * rows * rows * width, bytes_accessed=2 * n * rows * (rows + width), transcendentals=0
        ),
        name="partial",
    )(slots, *tops, *panels)


def product_kernel(count, alone, partial_ref, chosen_ref, turned_ref, *refs):
    panels, early, (selected_ref, update_ref) = refs[:count], refs[count:-2], refs[-2:]
    rest = dot(chosen_ref[0], panels[0][...])
    for d, panel in enumerate(panels[1:], 1):
        rest += dot(chosen_ref[d], panel[...])
    selected_ref[...] = partial_ref[...] + rest
    update = dot(turned_ref[...], rest.astype(jnp.bfloat16))
    if alone:
        update += update.T
    store_upper(update_ref, update, *early)


def products(partial, chosen, turned, panels, early):
    rows, width = panels[0].shape
    alone = len(panels) == 1
    return pl.pallas_call(
        functools.partial(product_kernel, len(panels), alone),
        out_shape=(
            jax.ShapeDtypeStruct((rows, width), jnp.float32),
            jax.ShapeDtypeStruct((width // 2, 3 * (width // 2)), jnp.bfloat16),
        ),
        in_specs=[VMEM] * (3 + len(panels) + len(early)),
        out_specs=(VMEM, VMEM),
        compiler_params=PARAMS,
        name="products",
    )(partial, chosen, turned, *panels, *early)


def finish_kernel(diag_ref, *refs):
    out_ref = refs[-1]
    total = refs[0][...].astype(jnp.float32)
    for ref in refs[1:-1]:
        total += ref[...].astype(jnp.float32)
    half = total.shape[0]
    out_ref[0, :half, :] = diag_ref[0, :half, :] + total[:, :2 * half]
    out_ref[0, half:, :half] = diag_ref[0, half:, :half] + total[:, half:2 * half].T
    out_ref[0, half:, half:] = diag_ref[0, half:, half:] + total[:, 2 * half:]


def finish(diag_inverse, updates):
    return pl.pallas_call(
        finish_kernel,
        out_shape=jax.ShapeDtypeStruct(diag_inverse.shape, jnp.float32),
        in_specs=[VMEM] * (1 + len(updates)),
        out_specs=VMEM,
        compiler_params=PARAMS,
        name="finish",
    )(diag_inverse, *updates)


def on_device(n, inverse_top, diag_inverse, cross_blocks, pattern):
    pairs = n // PAIR
    row, col = lax.axis_index("prow"), lax.axis_index("pcol")

    def from_pair(block, axis, shift, flip):
        moves = [
            (((m + shift) % pairs) * PAIR + (b ^ flip), m * PAIR + b) for m in range(pairs) for b in range(PAIR)
        ]
        return lax.ppermute(block, axis, moves)

    def mate(block, axis):
        return from_pair(block, axis, 0, 1)

    factor_panel, inverse_top = build_panel(cross_blocks, diag_inverse, pattern, inverse_top)
    beside = mate(factor_panel, "prow")
    crossed = [from_pair(factor_panel, "prow", d, 1) for d in range(1, pairs)]
    crossed = [after(block, factor_panel, cost=HOP_COST) for block in crossed]
    beside = after(beside, *crossed, cost=HOP_COST)
    swapped = [mate(block, "prow") for block in crossed]

    near = [from_pair(inverse_top, "pcol", d, 0) for d in range(1, pairs)]
    tops = [inverse_top, mate(inverse_top, "pcol")]
    for block in near:
        block = after(block, crossed[-1])
        tops += [block, mate(block, "pcol")]

    place = jnp.arange(n, dtype=jnp.int32)
    wanted_pair = (row // PAIR + place // PAIR) % pairs
    wanted_side = (row % PAIR) ^ (place % PAIR)
    slots = ((wanted_pair - col // PAIR) % pairs) * PAIR + (wanted_side ^ (col % PAIR))

    partial, chosen, turned, early = partial_product(tops, [factor_panel, beside] + crossed, slots)
    early = [early] + [after(from_pair(early, "prow", d, 1), swapped[-1]) for d in range(1, pairs)]
    if pairs > 2:
        selected, late = products(partial, chosen, turned, swapped, [])
        parts = early + [late] + [from_pair(late, "prow", d, 0) for d in range(1, pairs)]
        update = functools.reduce(jnp.add, [part.astype(jnp.float32) for part in parts]).astype(jnp.bfloat16)
    else:
        selected, update = products(partial, chosen, turned, swapped, early)
    return -selected, finish(diag_inverse, [update, mate(update, "prow")])


def solution(mesh):
    placed = (
        P(("pole", "prow"), "pcol"),
        P(("pole", "pcol"), None, None),
        P(("pole", "prow"), "pcol"),
        P("prow", "pcol"),
    )
    return jax.shard_map(
        functools.partial(on_device, mesh.shape["pcol"]),
        mesh=mesh,
        in_specs=placed,
        out_specs=(P(("pole", "prow"), "pcol"), P(("pole", "pcol"), None, None)),
        check_vma=False,
    )
```

```python
import functools
import jax
import jax.numpy as jnp
from jax import lax
from jax.experimental import pallas as pl
from jax.experimental.pallas import tpu as pltpu
from jax.sharding import PartitionSpec as P

PAIR = 2
HOP_COST = 10**10
VMEM_LIMIT = 40 * 1024 * 1024
PARAMS = pltpu.CompilerParams(vmem_limit_bytes=VMEM_LIMIT)
SMALL = pltpu.CompilerParams(vmem_limit_bytes=1024 * 1024)
SMEM = pl.BlockSpec(memory_space=pltpu.SMEM)
VMEM = pl.BlockSpec(memory_space=pltpu.VMEM)
ANY = pl.BlockSpec(memory_space=pl.ANY)
HBM = pl.BlockSpec(memory_space=pltpu.HBM)


def split(value):
    high = value.astype(jnp.bfloat16)
    return high, (value - high.astype(jnp.float32)).astype(jnp.bfloat16)


def dot(left, right):
    return jnp.dot(left, right, preferred_element_type=jnp.float32)


def panel_kernel(pattern_hbm, cross_hbm, diag_hbm, top_hbm, panel_ref, top_ref, pattern_ref, cross_ref, diag_ref, sems):
    width = diag_ref.shape[1]
    blocks = pattern_hbm.shape[0]
    rows = [pl.ds(a * width, width) for a in range(blocks)]
    loads = [pltpu.make_async_copy(cross_hbm.at[r], cross_ref.at[r], sems.at[a]) for a, r in enumerate(rows)]
    diag_copy = pltpu.make_async_copy(diag_hbm, diag_ref, sems.at[blocks])
    pattern_copy = pltpu.make_async_copy(pattern_hbm, pattern_ref, sems.at[blocks + 1])
    top_copy = pltpu.make_async_copy(top_hbm, top_ref, sems.at[blocks + 2])
    for copy in [pattern_copy, diag_copy] + loads + [top_copy]:
        copy.start()
    pattern_copy.wait()
    diag_copy.wait()
    diag_high, diag_low = split(diag_ref[0])
    for a in range(blocks):
        loads[a].wait()
        high, low = split(cross_ref[rows[a], :] * pattern_ref[a].astype(jnp.float32))
        solved = dot(high, diag_high) + (dot(high, diag_low) + dot(low, diag_high))
        panel_ref[rows[a], :] = solved.astype(jnp.bfloat16)
    top_copy.wait()


def build_panel(cross_blocks, diag_inverse, pattern, inverse_top):
    inputs = [pattern.reshape(-1), cross_blocks, diag_inverse, inverse_top]
    return pl.pallas_call(
        panel_kernel,
        out_shape=(
            pltpu.VMEM(cross_blocks.shape, jnp.bfloat16),
            pltpu.VMEM(inverse_top.shape, inverse_top.dtype),
        ),
        in_specs=[HBM] * 4,
        out_specs=(VMEM, VMEM),
        scratch_shapes=[
            pltpu.SMEM((pattern.size,), jnp.int32),
            pltpu.VMEM(cross_blocks.shape, jnp.float32),
            pltpu.VMEM(diag_inverse.shape, jnp.float32),
            pltpu.SemaphoreType.DMA((pattern.size + 3,)),
        ],
        compiler_params=PARAMS,
        name="panel",
    )(*[pltpu.with_memory_space_constraint(x, pltpu.HBM) for x in inputs])


def relay_kernel(*refs):
    del refs


def after(block, *gates, cost=0):
    return pl.pallas_call(
        relay_kernel,
        out_shape=jax.ShapeDtypeStruct(block.shape, block.dtype),
        in_specs=[ANY] * (1 + len(gates)),
        out_specs=ANY,
        input_output_aliases={0: 0},
        compiler_params=SMALL,
        cost_estimate=pl.CostEstimate(flops=cost, bytes_accessed=cost // 256, transcendentals=0),
        name="relay",
    )(block, *gates)


def store_upper(out_ref, update, *others):
    half = update.shape[0] // 2
    for columns, value in ((pl.ds(0, 2 * half), update[:half]), (pl.ds(2 * half, half), update[half:, half:])):
        for other in others:
            value += other[:, columns].astype(jnp.float32)
        out_ref[:, columns] = value.astype(jnp.bfloat16)


def partial_kernel(n, slots_ref, *refs):
    tops, panels = refs[:n], refs[n:n + n // 2 + 1]
    partial_ref, chosen_ref, turned_ref, update_ref, panel_buf = refs[n + n // 2 + 1:]
    places = [0] + list(range(1, n, 2))
    for place, panel in zip(places, panels):
        panel_buf[slots_ref[place]] = panel[...]
    for d, place in enumerate(range(2, n, 2)):
        slot = slots_ref[place]
        panel_buf[slot] = jnp.zeros(panel_buf.shape[1:], panel_buf.dtype)
        for t in range(n):
            @pl.when(slot == t)
            def _():
                chosen_ref[d] = tops[t][...]
    total = dot(tops[0][...], panel_buf[0])
    for t in range(1, n):
        total += dot(tops[t][...], panel_buf[t])
    partial_ref[...] = total
    turned = panels[0][...].astype(jnp.float32).T.astype(jnp.bfloat16)
    turned_ref[...] = turned
    store_upper(update_ref, dot(turned, total.astype(jnp.bfloat16)))


def partial_product(tops, panels, slots):
    n = len(tops)
    rows, width = panels[0].shape
    return pl.pallas_call(
        functools.partial(partial_kernel, n),
        out_shape=(
            jax.ShapeDtypeStruct((rows, width), jnp.float32),
            jax.ShapeDtypeStruct((n // 2 - 1,) + tops[0].shape, jnp.bfloat16),
            jax.ShapeDtypeStruct((width, rows), jnp.bfloat16),
            jax.ShapeDtypeStruct((width // 2, 3 * (width // 2)), jnp.bfloat16),
        ),
        in_specs=[SMEM] + [VMEM] * (n + len(panels)),
        out_specs=(VMEM, VMEM, VMEM, VMEM),
        scratch_shapes=[pltpu.VMEM((n, rows, width), jnp.bfloat16)],
        compiler_params=PARAMS,
        cost_estimate=pl.CostEstimate(
            flops=2 * n * rows * rows * width, bytes_accessed=2 * n * rows * (rows + width), transcendentals=0
        ),
        name="partial",
    )(slots, *tops, *panels)


def product_kernel(count, alone, partial_ref, chosen_ref, turned_ref, *refs):
    panels, early, (selected_ref, update_ref) = refs[:count], refs[count:-2], refs[-2:]
    rest = dot(chosen_ref[0], panels[0][...])
    for d, panel in enumerate(panels[1:], 1):
        rest += dot(chosen_ref[d], panel[...])
    selected_ref[...] = partial_ref[...] + rest
    update = dot(turned_ref[...], rest.astype(jnp.bfloat16))
    if alone:
        update += update.T
    store_upper(update_ref, update, *early)


def products(partial, chosen, turned, panels, early):
    rows, width = panels[0].shape
    alone = len(panels) == 1
    return pl.pallas_call(
        functools.partial(product_kernel, len(panels), alone),
        out_shape=(
            jax.ShapeDtypeStruct((rows, width), jnp.float32),
            jax.ShapeDtypeStruct((width // 2, 3 * (width // 2)), jnp.bfloat16),
        ),
        in_specs=[VMEM] * (3 + len(panels) + len(early)),
        out_specs=(VMEM, VMEM),
        compiler_params=PARAMS,
        name="products",
    )(partial, chosen, turned, *panels, *early)


def finish_kernel(diag_ref, *refs):
    out_ref = refs[-1]
    total = refs[0][...].astype(jnp.float32)
    for ref in refs[1:-1]:
        total += ref[...].astype(jnp.float32)
    half = total.shape[0]
    out_ref[0, :half, :] = diag_ref[0, :half, :] + total[:, :2 * half]
    out_ref[0, half:, :half] = diag_ref[0, half:, :half] + total[:, half:2 * half].T
    out_ref[0, half:, half:] = diag_ref[0, half:, half:] + total[:, 2 * half:]


def finish(diag_inverse, updates):
    return pl.pallas_call(
        finish_kernel,
        out_shape=jax.ShapeDtypeStruct(diag_inverse.shape, jnp.float32),
        in_specs=[VMEM] * (1 + len(updates)),
        out_specs=VMEM,
        compiler_params=PARAMS,
        name="finish",
    )(diag_inverse, *updates)


def on_device(n, inverse_top, diag_inverse, cross_blocks, pattern):
    pairs = n // PAIR
    row, col = lax.axis_index("prow"), lax.axis_index("pcol")

    def from_pair(block, axis, shift, flip):
        moves = [
            (((m + shift) % pairs) * PAIR + (b ^ flip), m * PAIR + b) for m in range(pairs) for b in range(PAIR)
        ]
        return lax.ppermute(block, axis, moves)

    def mate(block, axis):
        return from_pair(block, axis, 0, 1)

    near = [from_pair(inverse_top, "pcol", d, 0) for d in range(1, pairs)]
    factor_panel, inverse_top = build_panel(cross_blocks, diag_inverse, pattern, inverse_top)
    beside = mate(factor_panel, "prow")
    crossed = [from_pair(factor_panel, "prow", d, 1) for d in range(1, pairs)]
    near = [after(block, factor_panel) for block in near]
    crossed = [after(block, near[0], cost=HOP_COST) for block in crossed]
    beside = after(beside, *crossed, cost=2 * HOP_COST)
    swapped = [mate(block, "prow") for block in crossed]

    tops = [inverse_top, mate(inverse_top, "pcol")]
    for block in near:
        tops += [block, mate(block, "pcol")]

    place = jnp.arange(n, dtype=jnp.int32)
    wanted_pair = (row // PAIR + place // PAIR) % pairs
    wanted_side = (row % PAIR) ^ (place % PAIR)
    slots = ((wanted_pair - col // PAIR) % pairs) * PAIR + (wanted_side ^ (col % PAIR))

    partial, chosen, turned, early = partial_product(tops, [factor_panel, beside] + crossed, slots)
    early = [early] + [after(from_pair(early, "prow", d, 1), swapped[-1]) for d in range(1, pairs)]
    if pairs > 2:
        selected, late = products(partial, chosen, turned, swapped, [])
        parts = early + [late] + [from_pair(late, "prow", d, 0) for d in range(1, pairs)]
        update = functools.reduce(jnp.add, [part.astype(jnp.float32) for part in parts]).astype(jnp.bfloat16)
    else:
        selected, update = products(partial, chosen, turned, swapped, early)
    return -selected, finish(diag_inverse, [update, mate(update, "prow")])


def solution(mesh):
    placed = (
        P(("pole", "prow"), "pcol"),
        P(("pole", "pcol"), None, None),
        P(("pole", "prow"), "pcol"),
        P("prow", "pcol"),
    )
    return jax.shard_map(
        functools.partial(on_device, mesh.shape["pcol"]),
        mesh=mesh,
        in_specs=placed,
        out_specs=(P(("pole", "prow"), "pcol"), P(("pole", "pcol"), None, None)),
        check_vma=False,
    )
```

```python
import functools
import jax
import jax.numpy as jnp
from jax import lax
from jax.experimental import pallas as pl
from jax.experimental.pallas import tpu as pltpu
from jax.sharding import PartitionSpec as P

PAIR = 2
HOP_COST = 10**10
VMEM_LIMIT = 40 * 1024 * 1024
PARAMS = pltpu.CompilerParams(vmem_limit_bytes=VMEM_LIMIT)
SMALL = pltpu.CompilerParams(vmem_limit_bytes=1024 * 1024)
SMEM = pl.BlockSpec(memory_space=pltpu.SMEM)
VMEM = pl.BlockSpec(memory_space=pltpu.VMEM)
ANY = pl.BlockSpec(memory_space=pl.ANY)
HBM = pl.BlockSpec(memory_space=pltpu.HBM)


def split(value):
    high = value.astype(jnp.bfloat16)
    return high, (value - high.astype(jnp.float32)).astype(jnp.bfloat16)


def dot(left, right):
    return jnp.dot(left, right, preferred_element_type=jnp.float32)


def panel_kernel(pattern_hbm, cross_hbm, diag_hbm, top_hbm, panel_ref, top_ref, pattern_ref, cross_ref, diag_ref, sems):
    width = diag_ref.shape[1]
    blocks = pattern_hbm.shape[0]
    rows = [pl.ds(a * width, width) for a in range(blocks)]
    loads = [pltpu.make_async_copy(cross_hbm.at[r], cross_ref.at[r], sems.at[a]) for a, r in enumerate(rows)]
    diag_copy = pltpu.make_async_copy(diag_hbm, diag_ref, sems.at[blocks])
    pattern_copy = pltpu.make_async_copy(pattern_hbm, pattern_ref, sems.at[blocks + 1])
    top_copy = pltpu.make_async_copy(top_hbm, top_ref, sems.at[blocks + 2])
    for copy in [pattern_copy, diag_copy] + loads + [top_copy]:
        copy.start()
    pattern_copy.wait()
    diag_copy.wait()
    diag_high, diag_low = split(diag_ref[0])
    for a in range(blocks):
        loads[a].wait()
        high, low = split(cross_ref[rows[a], :] * pattern_ref[a].astype(jnp.float32))
        solved = dot(high, diag_high) + (dot(high, diag_low) + dot(low, diag_high))
        panel_ref[rows[a], :] = solved.astype(jnp.bfloat16)
    top_copy.wait()


def build_panel(cross_blocks, diag_inverse, pattern, inverse_top):
    inputs = [pattern.reshape(-1), cross_blocks, diag_inverse, inverse_top]
    return pl.pallas_call(
        panel_kernel,
        out_shape=(
            pltpu.VMEM(cross_blocks.shape, jnp.bfloat16),
            pltpu.VMEM(inverse_top.shape, inverse_top.dtype),
        ),
        in_specs=[HBM] * 4,
        out_specs=(VMEM, VMEM),
        scratch_shapes=[
            pltpu.SMEM((pattern.size,), jnp.int32),
            pltpu.VMEM(cross_blocks.shape, jnp.float32),
            pltpu.VMEM(diag_inverse.shape, jnp.float32),
            pltpu.SemaphoreType.DMA((pattern.size + 3,)),
        ],
        compiler_params=PARAMS,
        name="panel",
    )(*[pltpu.with_memory_space_constraint(x, pltpu.HBM) for x in inputs])


def relay_kernel(*refs):
    del refs


def after(block, *gates, cost=0):
    return pl.pallas_call(
        relay_kernel,
        out_shape=jax.ShapeDtypeStruct(block.shape, block.dtype),
        in_specs=[ANY] * (1 + len(gates)),
        out_specs=ANY,
        input_output_aliases={0: 0},
        compiler_params=SMALL,
        cost_estimate=pl.CostEstimate(flops=cost, bytes_accessed=cost // 256, transcendentals=0),
        name="relay",
    )(block, *gates)


def store_upper(out_ref, update, *others):
    half = update.shape[0] // 2
    for columns, value in ((pl.ds(0, 2 * half), update[:half]), (pl.ds(2 * half, half), update[half:, half:])):
        for other in others:
            value += other[:, columns].astype(jnp.float32)
        out_ref[:, columns] = value.astype(jnp.bfloat16)


def partial_kernel(n, slots_ref, *refs):
    tops, panels = refs[:n], refs[n:n + n // 2 + 1]
    partial_ref, chosen_ref, turned_ref, update_ref, panel_buf = refs[n + n // 2 + 1:]
    places = [0, 1] + list(range(2, n, 2))
    for place, panel in zip(places, panels):
        panel_buf[slots_ref[place]] = panel[...]
    for d, place in enumerate(range(3, n, 2)):
        slot = slots_ref[place]
        panel_buf[slot] = jnp.zeros(panel_buf.shape[1:], panel_buf.dtype)
        for t in range(n):
            @pl.when(slot == t)
            def _():
                chosen_ref[d] = tops[t][...]
    total = dot(tops[0][...], panel_buf[0])
    for t in range(1, n):
        total += dot(tops[t][...], panel_buf[t])
    partial_ref[...] = total
    turned = panels[0][...].astype(jnp.float32).T.astype(jnp.bfloat16)
    turned_ref[...] = turned
    store_upper(update_ref, dot(turned, total.astype(jnp.bfloat16)))


def partial_product(tops, panels, slots):
    n = len(tops)
    rows, width = panels[0].shape
    return pl.pallas_call(
        functools.partial(partial_kernel, n),
        out_shape=(
            jax.ShapeDtypeStruct((rows, width), jnp.float32),
            jax.ShapeDtypeStruct((n // 2 - 1,) + tops[0].shape, jnp.bfloat16),
            jax.ShapeDtypeStruct((width, rows), jnp.bfloat16),
            jax.ShapeDtypeStruct((width // 2, 3 * (width // 2)), jnp.bfloat16),
        ),
        in_specs=[SMEM] + [VMEM] * (n + len(panels)),
        out_specs=(VMEM, VMEM, VMEM, VMEM),
        scratch_shapes=[pltpu.VMEM((n, rows, width), jnp.bfloat16)],
        compiler_params=PARAMS,
        cost_estimate=pl.CostEstimate(
            flops=2 * n * rows * rows * width, bytes_accessed=2 * n * rows * (rows + width), transcendentals=0
        ),
        name="partial",
    )(slots, *tops, *panels)


def product_kernel(count, alone, partial_ref, chosen_ref, turned_ref, *refs):
    panels, early, (selected_ref, update_ref) = refs[:count], refs[count:-2], refs[-2:]
    rest = dot(chosen_ref[0], panels[0][...])
    for d, panel in enumerate(panels[1:], 1):
        rest += dot(chosen_ref[d], panel[...])
    selected_ref[...] = partial_ref[...] + rest
    update = dot(turned_ref[...], rest.astype(jnp.bfloat16))
    if alone:
        update += update.T
    store_upper(update_ref, update, *early)


def products(partial, chosen, turned, panels, early):
    rows, width = panels[0].shape
    alone = len(panels) == 1
    return pl.pallas_call(
        functools.partial(product_kernel, len(panels), alone),
        out_shape=(
            jax.ShapeDtypeStruct((rows, width), jnp.float32),
            jax.ShapeDtypeStruct((width // 2, 3 * (width // 2)), jnp.bfloat16),
        ),
        in_specs=[VMEM] * (3 + len(panels) + len(early)),
        out_specs=(VMEM, VMEM),
        compiler_params=PARAMS,
        name="products",
    )(partial, chosen, turned, *panels, *early)


def finish_kernel(diag_ref, *refs):
    out_ref = refs[-1]
    total = refs[0][...].astype(jnp.float32)
    for ref in refs[1:-1]:
        total += ref[...].astype(jnp.float32)
    half = total.shape[0]
    out_ref[0, :half, :] = diag_ref[0, :half, :] + total[:, :2 * half]
    out_ref[0, half:, :half] = diag_ref[0, half:, :half] + total[:, half:2 * half].T
    out_ref[0, half:, half:] = diag_ref[0, half:, half:] + total[:, 2 * half:]


def finish(diag_inverse, updates):
    return pl.pallas_call(
        finish_kernel,
        out_shape=jax.ShapeDtypeStruct(diag_inverse.shape, jnp.float32),
        in_specs=[VMEM] * (1 + len(updates)),
        out_specs=VMEM,
        compiler_params=PARAMS,
        name="finish",
    )(diag_inverse, *updates)


def on_device(n, inverse_top, diag_inverse, cross_blocks, pattern):
    pairs = n // PAIR
    row, col = lax.axis_index("prow"), lax.axis_index("pcol")

    def from_pair(block, axis, shift, flip):
        moves = [
            (((m + shift) % pairs) * PAIR + (b ^ flip), m * PAIR + b) for m in range(pairs) for b in range(PAIR)
        ]
        return lax.ppermute(block, axis, moves)

    def mate(block, axis):
        return from_pair(block, axis, 0, 1)

    near = [from_pair(inverse_top, "pcol", d, 0) for d in range(1, pairs)]
    factor_panel, inverse_top = build_panel(cross_blocks, diag_inverse, pattern, inverse_top)
    beside = mate(factor_panel, "prow")
    crossed = [from_pair(factor_panel, "prow", d, 0) for d in range(1, pairs)]
    near = [after(block, factor_panel) for block in near]
    crossed = [after(block, near[0], cost=HOP_COST) for block in crossed]
    beside = after(beside, *crossed, cost=2 * HOP_COST)
    swapped = [mate(block, "prow") for block in crossed]

    tops = [inverse_top, mate(inverse_top, "pcol")]
    for block in near:
        tops += [block, mate(block, "pcol")]

    place = jnp.arange(n, dtype=jnp.int32)
    wanted_pair = (row // PAIR + place // PAIR) % pairs
    wanted_side = (row % PAIR) ^ (place % PAIR)
    slots = ((wanted_pair - col // PAIR) % pairs) * PAIR + (wanted_side ^ (col % PAIR))

    partial, chosen, turned, early = partial_product(tops, [factor_panel, beside] + crossed, slots)
    early = [early] + [after(from_pair(early, "prow", d, 0), swapped[-1]) for d in range(1, pairs)]
    if pairs > 2:
        selected, late = products(partial, chosen, turned, swapped, [])
        parts = early + [late] + [from_pair(late, "prow", d, 0) for d in range(1, pairs)]
        update = functools.reduce(jnp.add, [part.astype(jnp.float32) for part in parts]).astype(jnp.bfloat16)
    else:
        selected, update = products(partial, chosen, turned, swapped, early)
    return -selected, finish(diag_inverse, [update, mate(update, "prow")])


def solution(mesh):
    placed = (
        P(("pole", "prow"), "pcol"),
        P(("pole", "pcol"), None, None),
        P(("pole", "prow"), "pcol"),
        P("prow", "pcol"),
    )
    return jax.shard_map(
        functools.partial(on_device, mesh.shape["pcol"]),
        mesh=mesh,
        in_specs=placed,
        out_specs=(P(("pole", "prow"), "pcol"), P(("pole", "pcol"), None, None)),
        check_vma=False,
    )
```

```python
import functools
import jax
import jax.numpy as jnp
from jax import lax
from jax.experimental import pallas as pl
from jax.experimental.pallas import tpu as pltpu
from jax.sharding import PartitionSpec as P

PAIR = 2
HOP_COST = 10**10
VMEM_LIMIT = 40 * 1024 * 1024
PARAMS = pltpu.CompilerParams(vmem_limit_bytes=VMEM_LIMIT)
SMALL = pltpu.CompilerParams(vmem_limit_bytes=1024 * 1024)
SMEM = pl.BlockSpec(memory_space=pltpu.SMEM)
VMEM = pl.BlockSpec(memory_space=pltpu.VMEM)
ANY = pl.BlockSpec(memory_space=pl.ANY)
HBM = pl.BlockSpec(memory_space=pltpu.HBM)


def split(value):
    high = value.astype(jnp.bfloat16)
    return high, (value - high.astype(jnp.float32)).astype(jnp.bfloat16)


def dot(left, right):
    return jnp.dot(left, right, preferred_element_type=jnp.float32)


def panel_kernel(pattern_hbm, cross_hbm, diag_hbm, top_hbm, panel_ref, top_ref, pattern_ref, cross_ref, diag_ref, sems):
    width = diag_ref.shape[1]
    blocks = pattern_hbm.shape[0]
    rows = [pl.ds(a * width, width) for a in range(blocks)]
    loads = [pltpu.make_async_copy(cross_hbm.at[r], cross_ref.at[r], sems.at[a]) for a, r in enumerate(rows)]
    diag_copy = pltpu.make_async_copy(diag_hbm, diag_ref, sems.at[blocks])
    pattern_copy = pltpu.make_async_copy(pattern_hbm, pattern_ref, sems.at[blocks + 1])
    top_copy = pltpu.make_async_copy(top_hbm, top_ref, sems.at[blocks + 2])
    for copy in [pattern_copy, diag_copy] + loads + [top_copy]:
        copy.start()
    pattern_copy.wait()
    diag_copy.wait()
    diag_high, diag_low = split(diag_ref[0])
    for a in range(blocks):
        loads[a].wait()
        high, low = split(cross_ref[rows[a], :] * pattern_ref[a].astype(jnp.float32))
        solved = dot(high, diag_high) + (dot(high, diag_low) + dot(low, diag_high))
        panel_ref[rows[a], :] = solved.astype(jnp.bfloat16)
    top_copy.wait()


def build_panel(cross_blocks, diag_inverse, pattern, inverse_top):
    inputs = [pattern.reshape(-1), cross_blocks, diag_inverse, inverse_top]
    return pl.pallas_call(
        panel_kernel,
        out_shape=(
            pltpu.VMEM(cross_blocks.shape, jnp.bfloat16),
            pltpu.VMEM(inverse_top.shape, inverse_top.dtype),
        ),
        in_specs=[HBM] * 4,
        out_specs=(VMEM, VMEM),
        scratch_shapes=[
            pltpu.SMEM((pattern.size,), jnp.int32),
            pltpu.VMEM(cross_blocks.shape, jnp.float32),
            pltpu.VMEM(diag_inverse.shape, jnp.float32),
            pltpu.SemaphoreType.DMA((pattern.size + 3,)),
        ],
        compiler_params=PARAMS,
        name="panel",
    )(*[pltpu.with_memory_space_constraint(x, pltpu.HBM) for x in inputs])


def relay_kernel(*refs):
    del refs


def after(block, *gates, cost=0):
    return pl.pallas_call(
        relay_kernel,
        out_shape=jax.ShapeDtypeStruct(block.shape, block.dtype),
        in_specs=[ANY] * (1 + len(gates)),
        out_specs=ANY,
        input_output_aliases={0: 0},
        compiler_params=SMALL,
        cost_estimate=pl.CostEstimate(flops=cost, bytes_accessed=cost // 256, transcendentals=0),
        name="relay",
    )(block, *gates)


def store_upper(out_ref, update, *others):
    half = update.shape[0] // 2
    for columns, value in ((pl.ds(0, 2 * half), update[:half]), (pl.ds(2 * half, half), update[half:, half:])):
        for other in others:
            value += other[:, columns].astype(jnp.float32)
        out_ref[:, columns] = value.astype(jnp.bfloat16)


def partial_kernel(n, slots_ref, *refs):
    tops, panels = refs[:n], refs[n:n + n // 2 + 1]
    partial_ref, chosen_ref, turned_ref, update_ref, panel_buf = refs[n + n // 2 + 1:]
    places = [0] + list(range(1, n, 2))
    for place, panel in zip(places, panels):
        panel_buf[slots_ref[place]] = panel[...]
    for d, place in enumerate(range(2, n, 2)):
        slot = slots_ref[place]
        panel_buf[slot] = jnp.zeros(panel_buf.shape[1:], panel_buf.dtype)
        for t in range(n):
            @pl.when(slot == t)
            def _():
                chosen_ref[d] = tops[t][...]
    total = dot(tops[0][...], panel_buf[0])
    for t in range(1, n):
        total += dot(tops[t][...], panel_buf[t])
    partial_ref[...] = total
    turned = panels[0][...].astype(jnp.float32).T.astype(jnp.bfloat16)
    turned_ref[...] = turned
    store_upper(update_ref, dot(turned, total.astype(jnp.bfloat16)))


def partial_product(tops, panels, slots):
    n = len(tops)
    rows, width = panels[0].shape
    return pl.pallas_call(
        functools.partial(partial_kernel, n),
        out_shape=(
            jax.ShapeDtypeStruct((rows, width), jnp.float32),
            jax.ShapeDtypeStruct((n // 2 - 1,) + tops[0].shape, jnp.bfloat16),
            jax.ShapeDtypeStruct((width, rows), jnp.bfloat16),
            jax.ShapeDtypeStruct((width // 2, 3 * (width // 2)), jnp.bfloat16),
        ),
        in_specs=[SMEM] + [VMEM] * (n + len(panels)),
        out_specs=(VMEM, VMEM, VMEM, VMEM),
        scratch_shapes=[pltpu.VMEM((n, rows, width), jnp.bfloat16)],
        compiler_params=PARAMS,
        cost_estimate=pl.CostEstimate(
            flops=2 * n * rows * rows * width, bytes_accessed=2 * n * rows * (rows + width), transcendentals=0
        ),
        name="partial",
    )(slots, *tops, *panels)


def product_kernel(count, alone, partial_ref, chosen_ref, turned_ref, *refs):
    panels, early, (selected_ref, update_ref) = refs[:count], refs[count:-2], refs[-2:]
    rest = dot(chosen_ref[0], panels[0][...])
    for d, panel in enumerate(panels[1:], 1):
        rest += dot(chosen_ref[d], panel[...])
    selected_ref[...] = partial_ref[...] + rest
    update = dot(turned_ref[...], rest.astype(jnp.bfloat16))
    if alone:
        update += update.T
    store_upper(update_ref, update, *early)


def products(partial, chosen, turned, panels, early):
    rows, width = panels[0].shape
    alone = len(panels) == 1
    return pl.pallas_call(
        functools.partial(product_kernel, len(panels), alone),
        out_shape=(
            jax.ShapeDtypeStruct((rows, width), jnp.float32),
            jax.ShapeDtypeStruct((width // 2, 3 * (width // 2)), jnp.bfloat16),
        ),
        in_specs=[VMEM] * (3 + len(panels) + len(early)),
        out_specs=(VMEM, VMEM),
        compiler_params=PARAMS,
        name="products",
    )(partial, chosen, turned, *panels, *early)


def finish_kernel(diag_ref, *refs):
    out_ref = refs[-1]
    total = refs[0][...].astype(jnp.float32)
    for ref in refs[1:-1]:
        total += ref[...].astype(jnp.float32)
    half = total.shape[0]
    out_ref[0, :half, :] = diag_ref[0, :half, :] + total[:, :2 * half]
    out_ref[0, half:, :half] = diag_ref[0, half:, :half] + total[:, half:2 * half].T
    out_ref[0, half:, half:] = diag_ref[0, half:, half:] + total[:, 2 * half:]


def finish(diag_inverse, updates):
    return pl.pallas_call(
        finish_kernel,
        out_shape=jax.ShapeDtypeStruct(diag_inverse.shape, jnp.float32),
        in_specs=[VMEM] * (1 + len(updates)),
        out_specs=VMEM,
        compiler_params=PARAMS,
        name="finish",
    )(diag_inverse, *updates)


def on_device(n, inverse_top, diag_inverse, cross_blocks, pattern):
    pairs = n // PAIR
    row, col = lax.axis_index("prow"), lax.axis_index("pcol")

    def from_pair(block, axis, shift, flip):
        moves = [
            (((m + shift) % pairs) * PAIR + (b ^ flip), m * PAIR + b) for m in range(pairs) for b in range(PAIR)
        ]
        return lax.ppermute(block, axis, moves)

    def mate(block, axis):
        return from_pair(block, axis, 0, 1)

    near = [from_pair(inverse_top, "pcol", d, 0) for d in range(1, pairs)]
    factor_panel, inverse_top = build_panel(cross_blocks, diag_inverse, pattern, inverse_top)
    beside = mate(factor_panel, "prow")
    crossed = [from_pair(factor_panel, "prow", d, 1) for d in range(1, pairs)]
    near = [after(block, factor_panel) for block in near]
    crossed = [after(block, near[0], cost=HOP_COST) for block in crossed]
    beside = after(beside, *crossed, cost=2 * HOP_COST)
    swapped = [mate(block, "prow") for block in crossed]

    tops = [inverse_top, mate(inverse_top, "pcol")]
    for block in near:
        tops += [block, mate(block, "pcol")]

    place = jnp.arange(n, dtype=jnp.int32)
    wanted_pair = (row // PAIR + place // PAIR) % pairs
    wanted_side = (row % PAIR) ^ (place % PAIR)
    slots = ((wanted_pair - col // PAIR) % pairs) * PAIR + (wanted_side ^ (col % PAIR))

    partial, chosen, turned, early = partial_product(tops, [factor_panel, beside] + crossed, slots)
    early = [early] + [after(from_pair(early, "prow", d, 0), swapped[-1]) for d in range(1, pairs)]
    if pairs > 2:
        selected, late = products(partial, chosen, turned, swapped, [])
        parts = early + [late] + [from_pair(late, "prow", d, 0) for d in range(1, pairs)]
        update = functools.reduce(jnp.add, [part.astype(jnp.float32) for part in parts]).astype(jnp.bfloat16)
    else:
        selected, update = products(partial, chosen, turned, swapped, early)
    return -selected, finish(diag_inverse, [update, mate(update, "prow")])


def solution(mesh):
    placed = (
        P(("pole", "prow"), "pcol"),
        P(("pole", "pcol"), None, None),
        P(("pole", "prow"), "pcol"),
        P("prow", "pcol"),
    )
    return jax.shard_map(
        functools.partial(on_device, mesh.shape["pcol"]),
        mesh=mesh,
        in_specs=placed,
        out_specs=(P(("pole", "prow"), "pcol"), P(("pole", "pcol"), None, None)),
        check_vma=False,
    )
```

```python
import functools
import jax
import jax.numpy as jnp
from jax import lax
from jax.experimental import pallas as pl
from jax.experimental.pallas import tpu as pltpu
from jax.sharding import PartitionSpec as P

PAIR = 2
HOP_COST = 10**10
VMEM_LIMIT = 40 * 1024 * 1024
PARAMS = pltpu.CompilerParams(vmem_limit_bytes=VMEM_LIMIT)
SMALL = pltpu.CompilerParams(vmem_limit_bytes=1024 * 1024)
SMEM = pl.BlockSpec(memory_space=pltpu.SMEM)
VMEM = pl.BlockSpec(memory_space=pltpu.VMEM)
ANY = pl.BlockSpec(memory_space=pl.ANY)
HBM = pl.BlockSpec(memory_space=pltpu.HBM)


def split(value):
    high = value.astype(jnp.bfloat16)
    return high, (value - high.astype(jnp.float32)).astype(jnp.bfloat16)


def dot(left, right):
    return jnp.dot(left, right, preferred_element_type=jnp.float32)


def panel_kernel(pattern_hbm, cross_hbm, diag_hbm, top_hbm, panel_ref, top_ref, pattern_ref, cross_ref, diag_ref, sems):
    width = diag_ref.shape[1]
    blocks = pattern_hbm.shape[0]
    rows = [pl.ds(a * width, width) for a in range(blocks)]
    loads = [pltpu.make_async_copy(cross_hbm.at[r], cross_ref.at[r], sems.at[a]) for a, r in enumerate(rows)]
    diag_copy = pltpu.make_async_copy(diag_hbm, diag_ref, sems.at[blocks])
    pattern_copy = pltpu.make_async_copy(pattern_hbm, pattern_ref, sems.at[blocks + 1])
    top_copy = pltpu.make_async_copy(top_hbm, top_ref, sems.at[blocks + 2])
    for copy in [pattern_copy, diag_copy] + loads + [top_copy]:
        copy.start()
    pattern_copy.wait()
    diag_copy.wait()
    diag_high, diag_low = split(diag_ref[0])
    for a in range(blocks):
        loads[a].wait()
        high, low = split(cross_ref[rows[a], :] * pattern_ref[a].astype(jnp.float32))
        solved = dot(high, diag_high) + (dot(high, diag_low) + dot(low, diag_high))
        panel_ref[rows[a], :] = solved.astype(jnp.bfloat16)
    top_copy.wait()


def build_panel(cross_blocks, diag_inverse, pattern, inverse_top):
    inputs = [pattern.reshape(-1), cross_blocks, diag_inverse, inverse_top]
    return pl.pallas_call(
        panel_kernel,
        out_shape=(
            pltpu.VMEM(cross_blocks.shape, jnp.bfloat16),
            pltpu.VMEM(inverse_top.shape, inverse_top.dtype),
        ),
        in_specs=[HBM] * 4,
        out_specs=(VMEM, VMEM),
        scratch_shapes=[
            pltpu.SMEM((pattern.size,), jnp.int32),
            pltpu.VMEM(cross_blocks.shape, jnp.float32),
            pltpu.VMEM(diag_inverse.shape, jnp.float32),
            pltpu.SemaphoreType.DMA((pattern.size + 3,)),
        ],
        compiler_params=PARAMS,
        name="panel",
    )(*[pltpu.with_memory_space_constraint(x, pltpu.HBM) for x in inputs])


def relay_kernel(*refs):
    del refs


def after(block, *gates, cost=0):
    return pl.pallas_call(
        relay_kernel,
        out_shape=jax.ShapeDtypeStruct(block.shape, block.dtype),
        in_specs=[ANY] * (1 + len(gates)),
        out_specs=ANY,
        input_output_aliases={0: 0},
        compiler_params=SMALL,
        cost_estimate=pl.CostEstimate(flops=cost, bytes_accessed=cost // 256, transcendentals=0),
        name="relay",
    )(block, *gates)


def store_upper(out_ref, update, *others):
    half = update.shape[0] // 2
    quarter = half // 2
    left, right = update[:, :half], update[:, half:]
    lanes = lax.broadcasted_iota(jnp.int32, (quarter, half), 1)
    last = jnp.where(lanes < quarter, pltpu.roll(right[3 * quarter:], quarter, 1), left[quarter:half])
    tiles = [left[:quarter], right[:quarter], right[quarter:half], right[half:3 * quarter], last]
    for t, tile in enumerate(tiles):
        columns = pl.ds(t * half, half)
        for other in others:
            tile += other[:, columns].astype(jnp.float32)
        out_ref[:, columns] = tile.astype(jnp.bfloat16)


def partial_kernel(n, slots_ref, *refs):
    tops, panels = refs[:n], refs[n:n + n // 2 + 1]
    partial_ref, chosen_ref, turned_ref, update_ref, panel_buf = refs[n + n // 2 + 1:]
    places = [0] + list(range(1, n, 2))
    for place, panel in zip(places, panels):
        panel_buf[slots_ref[place]] = panel[...]
    for d, place in enumerate(range(2, n, 2)):
        slot = slots_ref[place]
        panel_buf[slot] = jnp.zeros(panel_buf.shape[1:], panel_buf.dtype)
        for t in range(n):
            @pl.when(slot == t)
            def _():
                chosen_ref[d] = tops[t][...]
    total = dot(tops[0][...], panel_buf[0])
    for t in range(1, n):
        total += dot(tops[t][...], panel_buf[t])
    partial_ref[...] = total
    turned = panels[0][...].astype(jnp.float32).T.astype(jnp.bfloat16)
    turned_ref[...] = turned
    store_upper(update_ref, dot(turned, total.astype(jnp.bfloat16)))


def partial_product(tops, panels, slots):
    n = len(tops)
    rows, width = panels[0].shape
    return pl.pallas_call(
        functools.partial(partial_kernel, n),
        out_shape=(
            jax.ShapeDtypeStruct((rows, width), jnp.float32),
            jax.ShapeDtypeStruct((n // 2 - 1,) + tops[0].shape, jnp.bfloat16),
            jax.ShapeDtypeStruct((width, rows), jnp.bfloat16),
            jax.ShapeDtypeStruct((width // 4, 5 * (width // 2)), jnp.bfloat16),
        ),
        in_specs=[SMEM] + [VMEM] * (n + len(panels)),
        out_specs=(VMEM, VMEM, VMEM, VMEM),
        scratch_shapes=[pltpu.VMEM((n, rows, width), jnp.bfloat16)],
        compiler_params=PARAMS,
        cost_estimate=pl.CostEstimate(
            flops=2 * n * rows * rows * width, bytes_accessed=2 * n * rows * (rows + width), transcendentals=0
        ),
        name="partial",
    )(slots, *tops, *panels)


def product_kernel(count, alone, partial_ref, chosen_ref, turned_ref, *refs):
    panels, early, (selected_ref, update_ref) = refs[:count], refs[count:-2], refs[-2:]
    rest = dot(chosen_ref[0], panels[0][...])
    for d, panel in enumerate(panels[1:], 1):
        rest += dot(chosen_ref[d], panel[...])
    selected_ref[...] = partial_ref[...] + rest
    update = dot(turned_ref[...], rest.astype(jnp.bfloat16))
    if alone:
        update += update.T
    store_upper(update_ref, update, *early)


def products(partial, chosen, turned, panels, early):
    rows, width = panels[0].shape
    alone = len(panels) == 1
    return pl.pallas_call(
        functools.partial(product_kernel, len(panels), alone),
        out_shape=(
            jax.ShapeDtypeStruct((rows, width), jnp.float32),
            jax.ShapeDtypeStruct((width // 4, 5 * (width // 2)), jnp.bfloat16),
        ),
        in_specs=[VMEM] * (3 + len(panels) + len(early)),
        out_specs=(VMEM, VMEM),
        compiler_params=PARAMS,
        name="products",
    )(partial, chosen, turned, *panels, *early)


def finish_kernel(diag_ref, *refs):
    out_ref = refs[-1]
    total = refs[0][...].astype(jnp.float32)
    for ref in refs[1:-1]:
        total += ref[...].astype(jnp.float32)
    quarter = total.shape[0]
    half = 2 * quarter
    tiles = [total[:, t * half:(t + 1) * half] for t in range(5)]
    rows = lax.broadcasted_iota(jnp.int32, (half, half), 0)
    columns = lax.broadcasted_iota(jnp.int32, (half, half), 1)
    mirrored = (rows >= quarter) & (columns < quarter)

    def corner(top, bottom):
        block = jnp.concatenate([top, bottom], axis=0)
        return jnp.where(mirrored, block.T, block)

    side = jnp.concatenate([tiles[1], tiles[2]], axis=0)
    out_ref[0, :half, :half] = diag_ref[0, :half, :half] + corner(tiles[0], tiles[4])
    out_ref[0, :half, half:] = diag_ref[0, :half, half:] + side
    out_ref[0, half:, :half] = diag_ref[0, half:, :half] + side.T
    out_ref[0, half:, half:] = diag_ref[0, half:, half:] + corner(tiles[3], pltpu.roll(tiles[4], quarter, 1))


def finish(diag_inverse, updates):
    return pl.pallas_call(
        finish_kernel,
        out_shape=jax.ShapeDtypeStruct(diag_inverse.shape, jnp.float32),
        in_specs=[VMEM] * (1 + len(updates)),
        out_specs=VMEM,
        compiler_params=PARAMS,
        name="finish",
    )(diag_inverse, *updates)


def on_device(n, inverse_top, diag_inverse, cross_blocks, pattern):
    pairs = n // PAIR
    row, col = lax.axis_index("prow"), lax.axis_index("pcol")

    def from_pair(block, axis, shift, flip):
        moves = [
            (((m + shift) % pairs) * PAIR + (b ^ flip), m * PAIR + b) for m in range(pairs) for b in range(PAIR)
        ]
        return lax.ppermute(block, axis, moves)

    def mate(block, axis):
        return from_pair(block, axis, 0, 1)

    near = [from_pair(inverse_top, "pcol", d, 0) for d in range(1, pairs)]
    factor_panel, inverse_top = build_panel(cross_blocks, diag_inverse, pattern, inverse_top)
    beside = mate(factor_panel, "prow")
    crossed = [from_pair(factor_panel, "prow", d, 1) for d in range(1, pairs)]
    near = [after(block, factor_panel) for block in near]
    crossed = [after(block, near[0], cost=HOP_COST) for block in crossed]
    beside = after(beside, *crossed, cost=2 * HOP_COST)
    swapped = [mate(block, "prow") for block in crossed]

    tops = [inverse_top, mate(inverse_top, "pcol")]
    for block in near:
        tops += [block, mate(block, "pcol")]

    place = jnp.arange(n, dtype=jnp.int32)
    wanted_pair = (row // PAIR + place // PAIR) % pairs
    wanted_side = (row % PAIR) ^ (place % PAIR)
    slots = ((wanted_pair - col // PAIR) % pairs) * PAIR + (wanted_side ^ (col % PAIR))

    partial, chosen, turned, early = partial_product(tops, [factor_panel, beside] + crossed, slots)
    early = [early] + [after(from_pair(early, "prow", d, 1), swapped[-1]) for d in range(1, pairs)]
    if pairs > 2:
        selected, late = products(partial, chosen, turned, swapped, [])
        parts = early + [late] + [from_pair(late, "prow", d, 0) for d in range(1, pairs)]
        update = functools.reduce(jnp.add, [part.astype(jnp.float32) for part in parts]).astype(jnp.bfloat16)
    else:
        selected, update = products(partial, chosen, turned, swapped, early)
    return -selected, finish(diag_inverse, [update, mate(update, "prow")])


def solution(mesh):
    placed = (
        P(("pole", "prow"), "pcol"),
        P(("pole", "pcol"), None, None),
        P(("pole", "prow"), "pcol"),
        P("prow", "pcol"),
    )
    return jax.shard_map(
        functools.partial(on_device, mesh.shape["pcol"]),
        mesh=mesh,
        in_specs=placed,
        out_specs=(P(("pole", "prow"), "pcol"), P(("pole", "pcol"), None, None)),
        check_vma=False,
    )
```

```python
import functools
import jax
import jax.numpy as jnp
from jax import lax
from jax.experimental import pallas as pl
from jax.experimental.pallas import tpu as pltpu
from jax.sharding import PartitionSpec as P

PAIR = 2
HOP_COST = 10**10
VMEM_LIMIT = 40 * 1024 * 1024
PARAMS = pltpu.CompilerParams(vmem_limit_bytes=VMEM_LIMIT)
SMALL = pltpu.CompilerParams(vmem_limit_bytes=1024 * 1024)
SMEM = pl.BlockSpec(memory_space=pltpu.SMEM)
VMEM = pl.BlockSpec(memory_space=pltpu.VMEM)
ANY = pl.BlockSpec(memory_space=pl.ANY)
HBM = pl.BlockSpec(memory_space=pltpu.HBM)


def split(value):
    high = value.astype(jnp.bfloat16)
    return high, (value - high.astype(jnp.float32)).astype(jnp.bfloat16)


def dot(left, right):
    return jnp.dot(left, right, preferred_element_type=jnp.float32)


def token_kernel(out_ref):
    out_ref[...] = jnp.zeros_like(out_ref)


def token():
    return pl.pallas_call(
        token_kernel,
        out_shape=jax.ShapeDtypeStruct((8, 128), jnp.float32),
        out_specs=VMEM,
        compiler_params=SMALL,
        cost_estimate=pl.CostEstimate(flops=HOP_COST, bytes_accessed=0, transcendentals=0),
        name="token",
    )()


def panel_kernel(pattern_ref, cross_ref, diag_ref, top_hbm, token_ref, panel_ref, top_ref, sem):
    del token_ref
    width = diag_ref.shape[1]
    top_copy = pltpu.make_async_copy(top_hbm, top_ref, sem)
    top_copy.start()
    diag_high, diag_low = split(diag_ref[0])
    for a in range(pattern_ref.shape[1]):
        rows = pl.ds(a * width, width)
        high, low = split(cross_ref[rows, :] * pattern_ref[:, a:a + 1].astype(jnp.float32))
        solved = dot(high, diag_high) + (dot(high, diag_low) + dot(low, diag_high))
        panel_ref[rows, :] = solved.astype(jnp.bfloat16)
    top_copy.wait()


def build_panel(cross_blocks, diag_inverse, pattern, inverse_top):
    return pl.pallas_call(
        panel_kernel,
        out_shape=(
            pltpu.VMEM(cross_blocks.shape, jnp.bfloat16),
            pltpu.VMEM(inverse_top.shape, inverse_top.dtype),
        ),
        in_specs=[VMEM, VMEM, VMEM, HBM, ANY],
        out_specs=(VMEM, VMEM),
        scratch_shapes=[pltpu.SemaphoreType.DMA],
        compiler_params=PARAMS,
        name="panel",
    )(pattern.T, cross_blocks, diag_inverse, pltpu.with_memory_space_constraint(inverse_top, pltpu.HBM), token())


def relay_kernel(*refs):
    del refs


def after(block, *gates, cost=0):
    return pl.pallas_call(
        relay_kernel,
        out_shape=jax.ShapeDtypeStruct(block.shape, block.dtype),
        in_specs=[ANY] * (1 + len(gates)),
        out_specs=ANY,
        input_output_aliases={0: 0},
        compiler_params=SMALL,
        cost_estimate=pl.CostEstimate(flops=cost, bytes_accessed=cost // 256, transcendentals=0),
        name="relay",
    )(block, *gates)


def store_upper(out_ref, update, *others):
    half = update.shape[0] // 2
    quarter = half // 2
    left, right = update[:, :half], update[:, half:]
    lanes = lax.broadcasted_iota(jnp.int32, (quarter, half), 1)
    last = jnp.where(lanes < quarter, pltpu.roll(right[3 * quarter:], quarter, 1), left[quarter:half])
    tiles = [left[:quarter], right[:quarter], right[quarter:half], right[half:3 * quarter], last]
    for t, tile in enumerate(tiles):
        columns = pl.ds(t * half, half)
        for other in others:
            tile += other[:, columns].astype(jnp.float32)
        out_ref[:, columns] = tile.astype(jnp.bfloat16)


def partial_kernel(n, slots_ref, *refs):
    tops, panels = refs[:n], refs[n:n + n // 2 + 1]
    partial_ref, chosen_ref, turned_ref, update_ref, panel_buf = refs[n + n // 2 + 1:]
    places = [0] + list(range(1, n, 2))
    for place, panel in zip(places, panels):
        panel_buf[slots_ref[place]] = panel[...]
    for d, place in enumerate(range(2, n, 2)):
        slot = slots_ref[place]
        panel_buf[slot] = jnp.zeros(panel_buf.shape[1:], panel_buf.dtype)
        for t in range(n):
            @pl.when(slot == t)
            def _():
                chosen_ref[d] = tops[t][...]
    total = dot(tops[0][...], panel_buf[0])
    for t in range(1, n):
        total += dot(tops[t][...], panel_buf[t])
    partial_ref[...] = total
    turned = panels[0][...].astype(jnp.float32).T.astype(jnp.bfloat16)
    turned_ref[...] = turned
    store_upper(update_ref, dot(turned, total.astype(jnp.bfloat16)))


def partial_product(tops, panels, slots):
    n = len(tops)
    rows, width = panels[0].shape
    return pl.pallas_call(
        functools.partial(partial_kernel, n),
        out_shape=(
            jax.ShapeDtypeStruct((rows, width), jnp.float32),
            jax.ShapeDtypeStruct((n // 2 - 1,) + tops[0].shape, jnp.bfloat16),
            jax.ShapeDtypeStruct((width, rows), jnp.bfloat16),
            jax.ShapeDtypeStruct((width // 4, 5 * (width // 2)), jnp.bfloat16),
        ),
        in_specs=[SMEM] + [VMEM] * (n + len(panels)),
        out_specs=(VMEM, VMEM, VMEM, VMEM),
        scratch_shapes=[pltpu.VMEM((n, rows, width), jnp.bfloat16)],
        compiler_params=PARAMS,
        cost_estimate=pl.CostEstimate(
            flops=2 * n * rows * rows * width, bytes_accessed=2 * n * rows * (rows + width), transcendentals=0
        ),
        name="partial",
    )(slots, *tops, *panels)


def product_kernel(count, alone, partial_ref, chosen_ref, turned_ref, *refs):
    panels, early, (selected_ref, update_ref) = refs[:count], refs[count:-2], refs[-2:]
    rest = dot(chosen_ref[0], panels[0][...])
    for d, panel in enumerate(panels[1:], 1):
        rest += dot(chosen_ref[d], panel[...])
    selected_ref[...] = partial_ref[...] + rest
    update = dot(turned_ref[...], rest.astype(jnp.bfloat16))
    if alone:
        update += update.T
    store_upper(update_ref, update, *early)


def products(partial, chosen, turned, panels, early):
    rows, width = panels[0].shape
    alone = len(panels) == 1
    return pl.pallas_call(
        functools.partial(product_kernel, len(panels), alone),
        out_shape=(
            jax.ShapeDtypeStruct((rows, width), jnp.float32),
            jax.ShapeDtypeStruct((width // 4, 5 * (width // 2)), jnp.bfloat16),
        ),
        in_specs=[VMEM] * (3 + len(panels) + len(early)),
        out_specs=(VMEM, VMEM),
        compiler_params=PARAMS,
        name="products",
    )(partial, chosen, turned, *panels, *early)


def finish_kernel(diag_ref, *refs):
    out_ref = refs[-1]
    total = refs[0][...].astype(jnp.float32)
    for ref in refs[1:-1]:
        total += ref[...].astype(jnp.float32)
    quarter = total.shape[0]
    half = 2 * quarter
    tiles = [total[:, t * half:(t + 1) * half] for t in range(5)]
    rows = lax.broadcasted_iota(jnp.int32, (half, half), 0)
    columns = lax.broadcasted_iota(jnp.int32, (half, half), 1)
    mirrored = (rows >= quarter) & (columns < quarter)

    def corner(top, bottom):
        block = jnp.concatenate([top, bottom], axis=0)
        return jnp.where(mirrored, block.T, block)

    side = jnp.concatenate([tiles[1], tiles[2]], axis=0)
    out_ref[0, :half, :half] = diag_ref[0, :half, :half] + corner(tiles[0], tiles[4])
    out_ref[0, :half, half:] = diag_ref[0, :half, half:] + side
    out_ref[0, half:, :half] = diag_ref[0, half:, :half] + side.T
    out_ref[0, half:, half:] = diag_ref[0, half:, half:] + corner(tiles[3], pltpu.roll(tiles[4], quarter, 1))


def finish(diag_inverse, updates):
    return pl.pallas_call(
        finish_kernel,
        out_shape=jax.ShapeDtypeStruct(diag_inverse.shape, jnp.float32),
        in_specs=[VMEM] * (1 + len(updates)),
        out_specs=VMEM,
        compiler_params=PARAMS,
        name="finish",
    )(diag_inverse, *updates)


def on_device(n, inverse_top, diag_inverse, cross_blocks, pattern):
    pairs = n // PAIR
    row, col = lax.axis_index("prow"), lax.axis_index("pcol")

    def from_pair(block, axis, shift, flip):
        moves = [
            (((m + shift) % pairs) * PAIR + (b ^ flip), m * PAIR + b) for m in range(pairs) for b in range(PAIR)
        ]
        return lax.ppermute(block, axis, moves)

    def mate(block, axis):
        return from_pair(block, axis, 0, 1)

    near = [from_pair(inverse_top, "pcol", d, 0) for d in range(1, pairs)]
    factor_panel, inverse_top = build_panel(cross_blocks, diag_inverse, pattern, inverse_top)
    beside = mate(factor_panel, "prow")
    crossed = [from_pair(factor_panel, "prow", d, 1) for d in range(1, pairs)]
    near = [after(block, factor_panel) for block in near]
    crossed = [after(block, near[0], cost=HOP_COST) for block in crossed]
    beside = after(beside, *crossed, cost=2 * HOP_COST)
    swapped = [mate(block, "prow") for block in crossed]

    tops = [inverse_top, mate(inverse_top, "pcol")]
    for block in near:
        tops += [block, mate(block, "pcol")]

    place = jnp.arange(n, dtype=jnp.int32)
    wanted_pair = (row // PAIR + place // PAIR) % pairs
    wanted_side = (row % PAIR) ^ (place % PAIR)
    slots = ((wanted_pair - col // PAIR) % pairs) * PAIR + (wanted_side ^ (col % PAIR))

    partial, chosen, turned, early = partial_product(tops, [factor_panel, beside] + crossed, slots)
    early = [early] + [after(from_pair(early, "prow", d, 1), swapped[-1]) for d in range(1, pairs)]
    if pairs > 2:
        selected, late = products(partial, chosen, turned, swapped, [])
        parts = early + [late] + [from_pair(late, "prow", d, 0) for d in range(1, pairs)]
        update = functools.reduce(jnp.add, [part.astype(jnp.float32) for part in parts]).astype(jnp.bfloat16)
    else:
        selected, update = products(partial, chosen, turned, swapped, early)
    return -selected, finish(diag_inverse, [update, mate(update, "prow")])


def solution(mesh):
    placed = (
        P(("pole", "prow"), "pcol"),
        P(("pole", "pcol"), None, None),
        P(("pole", "prow"), "pcol"),
        P("prow", "pcol"),
    )
    return jax.shard_map(
        functools.partial(on_device, mesh.shape["pcol"]),
        mesh=mesh,
        in_specs=placed,
        out_specs=(P(("pole", "prow"), "pcol"), P(("pole", "pcol"), None, None)),
        check_vma=False,
    )
```

```python
import functools
import jax
import jax.numpy as jnp
from jax import lax
from jax.experimental import pallas as pl
from jax.experimental.pallas import tpu as pltpu
from jax.sharding import PartitionSpec as P

PAIR = 2
HOP_COST = 10**10
VMEM_LIMIT = 40 * 1024 * 1024
PARAMS = pltpu.CompilerParams(vmem_limit_bytes=VMEM_LIMIT)
SMALL = pltpu.CompilerParams(vmem_limit_bytes=1024 * 1024)
SMEM = pl.BlockSpec(memory_space=pltpu.SMEM)
VMEM = pl.BlockSpec(memory_space=pltpu.VMEM)
ANY = pl.BlockSpec(memory_space=pl.ANY)
HBM = pl.BlockSpec(memory_space=pltpu.HBM)


def split(value):
    high = value.astype(jnp.bfloat16)
    return high, (value - high.astype(jnp.float32)).astype(jnp.bfloat16)


def dot(left, right):
    return jnp.dot(left, right, preferred_element_type=jnp.float32)


def token_kernel(out_ref):
    out_ref[...] = jnp.zeros_like(out_ref)


def token():
    return pl.pallas_call(
        token_kernel,
        out_shape=jax.ShapeDtypeStruct((8, 128), jnp.float32),
        out_specs=VMEM,
        compiler_params=SMALL,
        cost_estimate=pl.CostEstimate(flops=HOP_COST, bytes_accessed=0, transcendentals=0),
        name="token",
    )()


def panel_kernel(pattern_hbm, cross_ref, diag_ref, top_hbm, token_ref, panel_ref, top_ref, pattern_ref, sems):
    del token_ref
    width = diag_ref.shape[1]
    pattern_copy = pltpu.make_async_copy(pattern_hbm, pattern_ref, sems.at[0])
    pattern_copy.start()
    top_copy = pltpu.make_async_copy(top_hbm, top_ref, sems.at[1])
    top_copy.start()
    diag_high, diag_low = split(diag_ref[0])
    solved = []
    for a in range(pattern_hbm.shape[0]):
        high, low = split(cross_ref[pl.ds(a * width, width), :])
        solved.append(dot(high, diag_high) + (dot(high, diag_low) + dot(low, diag_high)))
    pattern_copy.wait()
    for a, block in enumerate(solved):
        kept = jnp.where(pattern_ref[a] != 0, block, 0.0)
        panel_ref[pl.ds(a * width, width), :] = kept.astype(jnp.bfloat16)
    top_copy.wait()


def build_panel(cross_blocks, diag_inverse, pattern, inverse_top):
    return pl.pallas_call(
        panel_kernel,
        out_shape=(
            pltpu.VMEM(cross_blocks.shape, jnp.bfloat16),
            pltpu.VMEM(inverse_top.shape, inverse_top.dtype),
        ),
        in_specs=[HBM, VMEM, VMEM, HBM, ANY],
        out_specs=(VMEM, VMEM),
        scratch_shapes=[pltpu.SMEM((pattern.size,), jnp.int32), pltpu.SemaphoreType.DMA((2,))],
        compiler_params=PARAMS,
        name="panel",
    )(
        pltpu.with_memory_space_constraint(pattern.reshape(-1), pltpu.HBM),
        cross_blocks,
        diag_inverse,
        pltpu.with_memory_space_constraint(inverse_top, pltpu.HBM),
        token(),
    )


def relay_kernel(*refs):
    del refs


def after(block, *gates, cost=0):
    return pl.pallas_call(
        relay_kernel,
        out_shape=jax.ShapeDtypeStruct(block.shape, block.dtype),
        in_specs=[ANY] * (1 + len(gates)),
        out_specs=ANY,
        input_output_aliases={0: 0},
        compiler_params=SMALL,
        cost_estimate=pl.CostEstimate(flops=cost, bytes_accessed=cost // 256, transcendentals=0),
        name="relay",
    )(block, *gates)


def store_upper(out_ref, update, *others):
    half = update.shape[0] // 2
    quarter = half // 2
    left, right = update[:, :half], update[:, half:]
    lanes = lax.broadcasted_iota(jnp.int32, (quarter, half), 1)
    last = jnp.where(lanes < quarter, pltpu.roll(right[3 * quarter:], quarter, 1), left[quarter:half])
    tiles = [left[:quarter], right[:quarter], right[quarter:half], right[half:3 * quarter], last]
    for t, tile in enumerate(tiles):
        columns = pl.ds(t * half, half)
        for other in others:
            tile += other[:, columns].astype(jnp.float32)
        out_ref[:, columns] = tile.astype(jnp.bfloat16)


def partial_kernel(n, slots_ref, *refs):
    tops, panels = refs[:n], refs[n:n + n // 2 + 1]
    partial_ref, chosen_ref, turned_ref, update_ref, panel_buf = refs[n + n // 2 + 1:]
    places = [0] + list(range(1, n, 2))
    for place, panel in zip(places, panels):
        panel_buf[slots_ref[place]] = panel[...]
    for d, place in enumerate(range(2, n, 2)):
        slot = slots_ref[place]
        panel_buf[slot] = jnp.zeros(panel_buf.shape[1:], panel_buf.dtype)
        for t in range(n):
            @pl.when(slot == t)
            def _():
                chosen_ref[d] = tops[t][...]
    total = dot(tops[0][...], panel_buf[0])
    for t in range(1, n):
        total += dot(tops[t][...], panel_buf[t])
    partial_ref[...] = total
    turned = panels[0][...].astype(jnp.float32).T.astype(jnp.bfloat16)
    turned_ref[...] = turned
    store_upper(update_ref, dot(turned, total.astype(jnp.bfloat16)))


def partial_product(tops, panels, slots):
    n = len(tops)
    rows, width = panels[0].shape
    return pl.pallas_call(
        functools.partial(partial_kernel, n),
        out_shape=(
            jax.ShapeDtypeStruct((rows, width), jnp.float32),
            jax.ShapeDtypeStruct((n // 2 - 1,) + tops[0].shape, jnp.bfloat16),
            jax.ShapeDtypeStruct((width, rows), jnp.bfloat16),
            jax.ShapeDtypeStruct((width // 4, 5 * (width // 2)), jnp.bfloat16),
        ),
        in_specs=[SMEM] + [VMEM] * (n + len(panels)),
        out_specs=(VMEM, VMEM, VMEM, VMEM),
        scratch_shapes=[pltpu.VMEM((n, rows, width), jnp.bfloat16)],
        compiler_params=PARAMS,
        cost_estimate=pl.CostEstimate(
            flops=2 * n * rows * rows * width, bytes_accessed=2 * n * rows * (rows + width), transcendentals=0
        ),
        name="partial",
    )(slots, *tops, *panels)


def product_kernel(count, alone, partial_ref, chosen_ref, turned_ref, *refs):
    panels, early, (selected_ref, update_ref) = refs[:count], refs[count:-2], refs[-2:]
    rest = dot(chosen_ref[0], panels[0][...])
    for d, panel in enumerate(panels[1:], 1):
        rest += dot(chosen_ref[d], panel[...])
    selected_ref[...] = partial_ref[...] + rest
    update = dot(turned_ref[...], rest.astype(jnp.bfloat16))
    if alone:
        update += update.T
    store_upper(update_ref, update, *early)


def products(partial, chosen, turned, panels, early):
    rows, width = panels[0].shape
    alone = len(panels) == 1
    return pl.pallas_call(
        functools.partial(product_kernel, len(panels), alone),
        out_shape=(
            jax.ShapeDtypeStruct((rows, width), jnp.float32),
            jax.ShapeDtypeStruct((width // 4, 5 * (width // 2)), jnp.bfloat16),
        ),
        in_specs=[VMEM] * (3 + len(panels) + len(early)),
        out_specs=(VMEM, VMEM),
        compiler_params=PARAMS,
        name="products",
    )(partial, chosen, turned, *panels, *early)


def finish_kernel(diag_ref, *refs):
    out_ref = refs[-1]
    total = refs[0][...].astype(jnp.float32)
    for ref in refs[1:-1]:
        total += ref[...].astype(jnp.float32)
    quarter = total.shape[0]
    half = 2 * quarter
    tiles = [total[:, t * half:(t + 1) * half] for t in range(5)]
    rows = lax.broadcasted_iota(jnp.int32, (half, half), 0)
    columns = lax.broadcasted_iota(jnp.int32, (half, half), 1)
    mirrored = (rows >= quarter) & (columns < quarter)

    def corner(top, bottom):
        block = jnp.concatenate([top, bottom], axis=0)
        return jnp.where(mirrored, block.T, block)

    side = jnp.concatenate([tiles[1], tiles[2]], axis=0)
    out_ref[0, :half, :half] = diag_ref[0, :half, :half] + corner(tiles[0], tiles[4])
    out_ref[0, :half, half:] = diag_ref[0, :half, half:] + side
    out_ref[0, half:, :half] = diag_ref[0, half:, :half] + side.T
    out_ref[0, half:, half:] = diag_ref[0, half:, half:] + corner(tiles[3], pltpu.roll(tiles[4], quarter, 1))


def finish(diag_inverse, updates):
    return pl.pallas_call(
        finish_kernel,
        out_shape=jax.ShapeDtypeStruct(diag_inverse.shape, jnp.float32),
        in_specs=[VMEM] * (1 + len(updates)),
        out_specs=VMEM,
        compiler_params=PARAMS,
        name="finish",
    )(diag_inverse, *updates)


def on_device(n, inverse_top, diag_inverse, cross_blocks, pattern):
    pairs = n // PAIR
    row, col = lax.axis_index("prow"), lax.axis_index("pcol")

    def from_pair(block, axis, shift, flip):
        moves = [
            (((m + shift) % pairs) * PAIR + (b ^ flip), m * PAIR + b) for m in range(pairs) for b in range(PAIR)
        ]
        return lax.ppermute(block, axis, moves)

    def mate(block, axis):
        return from_pair(block, axis, 0, 1)

    near = [from_pair(inverse_top, "pcol", d, 0) for d in range(1, pairs)]
    factor_panel, inverse_top = build_panel(cross_blocks, diag_inverse, pattern, inverse_top)
    beside = mate(factor_panel, "prow")
    crossed = [from_pair(factor_panel, "prow", d, 1) for d in range(1, pairs)]
    near = [after(block, factor_panel) for block in near]
    crossed = [after(block, near[0], beside, cost=HOP_COST) for block in crossed]
    swapped = [mate(block, "prow") for block in crossed]

    tops = [inverse_top, mate(inverse_top, "pcol")]
    for block in near:
        tops += [block, mate(block, "pcol")]

    place = jnp.arange(n, dtype=jnp.int32)
    wanted_pair = (row // PAIR + place // PAIR) % pairs
    wanted_side = (row % PAIR) ^ (place % PAIR)
    slots = ((wanted_pair - col // PAIR) % pairs) * PAIR + (wanted_side ^ (col % PAIR))

    partial, chosen, turned, early = partial_product(tops, [factor_panel, beside] + crossed, slots)
    early = [early] + [after(from_pair(early, "prow", d, 1), swapped[-1]) for d in range(1, pairs)]
    if pairs > 2:
        selected, late = products(partial, chosen, turned, swapped, [])
        parts = early + [late] + [from_pair(late, "prow", d, 0) for d in range(1, pairs)]
        update = functools.reduce(jnp.add, [part.astype(jnp.float32) for part in parts]).astype(jnp.bfloat16)
    else:
        selected, update = products(partial, chosen, turned, swapped, early)
    return -selected, finish(diag_inverse, [update, mate(update, "prow")])


def solution(mesh):
    placed = (
        P(("pole", "prow"), "pcol"),
        P(("pole", "pcol"), None, None),
        P(("pole", "prow"), "pcol"),
        P("prow", "pcol"),
    )
    return jax.shard_map(
        functools.partial(on_device, mesh.shape["pcol"]),
        mesh=mesh,
        in_specs=placed,
        out_specs=(P(("pole", "prow"), "pcol"), P(("pole", "pcol"), None, None)),
        check_vma=False,
    )
```

```python
import functools
import jax
import jax.numpy as jnp
from jax import lax
from jax.experimental import pallas as pl
from jax.experimental.pallas import tpu as pltpu
from jax.sharding import PartitionSpec as P

PAIR = 2
HOP_COST = 10**10
VMEM_LIMIT = 40 * 1024 * 1024
PARAMS = pltpu.CompilerParams(vmem_limit_bytes=VMEM_LIMIT)
SMALL = pltpu.CompilerParams(vmem_limit_bytes=1024 * 1024)
SMEM = pl.BlockSpec(memory_space=pltpu.SMEM)
VMEM = pl.BlockSpec(memory_space=pltpu.VMEM)
ANY = pl.BlockSpec(memory_space=pl.ANY)
HBM = pl.BlockSpec(memory_space=pltpu.HBM)


def split(value):
    high = value.astype(jnp.bfloat16)
    return high, (value - high.astype(jnp.float32)).astype(jnp.bfloat16)


def dot(left, right):
    return jnp.dot(left, right, preferred_element_type=jnp.float32)


def token_kernel(out_ref):
    out_ref[...] = jnp.zeros_like(out_ref)


def token():
    return pl.pallas_call(
        token_kernel,
        out_shape=jax.ShapeDtypeStruct((8, 128), jnp.float32),
        out_specs=VMEM,
        compiler_params=SMALL,
        cost_estimate=pl.CostEstimate(flops=HOP_COST, bytes_accessed=0, transcendentals=0),
        name="token",
    )()


def panel_kernel(pattern_hbm, cross_ref, diag_ref, top_hbm, token_ref, panel_ref, top_ref, *refs):
    del token_ref
    bands, (pattern_ref, sems) = refs[:-2], refs[-2:]
    width = diag_ref.shape[1]
    pattern_copy = pltpu.make_async_copy(pattern_hbm, pattern_ref, sems.at[0])
    pattern_copy.start()
    top_copy = pltpu.make_async_copy(top_hbm, top_ref, sems.at[1])
    top_copy.start()
    diag_high, diag_low = split(diag_ref[0])
    solved = []
    for a in range(pattern_hbm.shape[0]):
        high, low = split(cross_ref[pl.ds(a * width, width), :])
        solved.append(dot(high, diag_high) + (dot(high, diag_low) + dot(low, diag_high)))
    pattern_copy.wait()
    for a, block in enumerate(solved):
        kept = jnp.where(pattern_ref[a] != 0, block, 0.0).astype(jnp.bfloat16)
        panel_ref[pl.ds(a * width, width), :] = kept
        bands[a][...] = kept
    top_copy.wait()


def build_panel(cross_blocks, diag_inverse, pattern, inverse_top):
    blocks = pattern.size
    band = (cross_blocks.shape[0] // blocks, cross_blocks.shape[1])
    return pl.pallas_call(
        panel_kernel,
        out_shape=(
            pltpu.VMEM(cross_blocks.shape, jnp.bfloat16),
            pltpu.VMEM(inverse_top.shape, inverse_top.dtype),
        )
        + (pltpu.VMEM(band, jnp.bfloat16),) * blocks,
        in_specs=[HBM, VMEM, VMEM, HBM, ANY],
        out_specs=(VMEM,) * (2 + blocks),
        scratch_shapes=[pltpu.SMEM((pattern.size,), jnp.int32), pltpu.SemaphoreType.DMA((2,))],
        compiler_params=PARAMS,
        name="panel",
    )(
        pltpu.with_memory_space_constraint(pattern.reshape(-1), pltpu.HBM),
        cross_blocks,
        diag_inverse,
        pltpu.with_memory_space_constraint(inverse_top, pltpu.HBM),
        token(),
    )


def relay_kernel(*refs):
    del refs


def after(block, *gates, cost=0):
    return pl.pallas_call(
        relay_kernel,
        out_shape=jax.ShapeDtypeStruct(block.shape, block.dtype),
        in_specs=[ANY] * (1 + len(gates)),
        out_specs=ANY,
        input_output_aliases={0: 0},
        compiler_params=SMALL,
        cost_estimate=pl.CostEstimate(flops=cost, bytes_accessed=cost // 256, transcendentals=0),
        name="relay",
    )(block, *gates)


def store_upper(out_ref, update, *others):
    half = update.shape[0] // 2
    quarter = half // 2
    left, right = update[:, :half], update[:, half:]
    lanes = lax.broadcasted_iota(jnp.int32, (quarter, half), 1)
    last = jnp.where(lanes < quarter, pltpu.roll(right[3 * quarter:], quarter, 1), left[quarter:half])
    tiles = [left[:quarter], right[:quarter], right[quarter:half], right[half:3 * quarter], last]
    for t, tile in enumerate(tiles):
        columns = pl.ds(t * half, half)
        for other in others:
            tile += other[:, columns].astype(jnp.float32)
        out_ref[:, columns] = tile.astype(jnp.bfloat16)


def share(turned, product):
    return dot(turned, product.astype(jnp.bfloat16))


def choose(slot, tops, out_ref):
    for t, top in enumerate(tops):
        @pl.when(slot == t)
        def _():
            out_ref[...] = top[...]


def near_kernel(n, slots_ref, *refs):
    tops, panels = refs[:n], refs[n:n + PAIR]
    partial_ref, turned_ref, update_ref, chosen_ref = refs[n + PAIR:]
    for s in range(PAIR):
        choose(slots_ref[s], tops, chosen_ref.at[s])
    turned = panels[0][...].astype(jnp.float32).T.astype(jnp.bfloat16)
    turned_ref[...] = turned
    total = dot(chosen_ref[0], panels[0][...])
    for s in range(1, PAIR):
        total += dot(chosen_ref[s], panels[s][...])
    partial_ref[...] = total
    store_upper(update_ref, share(turned, total))


def near_product(tops, panels, slots):
    rows, width = panels[0].shape
    return pl.pallas_call(
        functools.partial(near_kernel, len(tops)),
        out_shape=(
            jax.ShapeDtypeStruct((rows, width), jnp.float32),
            jax.ShapeDtypeStruct((width, rows), jnp.bfloat16),
            jax.ShapeDtypeStruct((width // 4, 5 * (width // 2)), jnp.bfloat16),
        ),
        in_specs=[SMEM] + [VMEM] * (len(tops) + len(panels)),
        out_specs=(VMEM, VMEM, VMEM),
        scratch_shapes=[pltpu.VMEM((PAIR,) + tops[0].shape, jnp.bfloat16)],
        compiler_params=PARAMS,
        name="near",
    )(slots, *tops, *panels)


def banded_dot(top, bands):
    height = bands[0].shape[0]
    total = dot(top[:, :height], bands[0][...])
    for b, band in enumerate(bands[1:], 1):
        total += dot(top[:, b * height:(b + 1) * height], band[...])
    return total


def far_kernel(n, blocks, slots_ref, partial_ref, turned_ref, *refs):
    count = n // 2 - 1
    tops, bands = refs[:n], refs[n:n + count * blocks]
    out_ref, chosen_ref, update_ref, crossing_ref = refs[n + count * blocks:]
    for d in range(count):
        choose(slots_ref[2 * d + 3], tops, crossing_ref.at[d])
        choose(slots_ref[2 * d + 2], tops, chosen_ref.at[d])
    total = banded_dot(crossing_ref.at[0], bands[:blocks])
    for d in range(1, count):
        total += banded_dot(crossing_ref.at[d], bands[d * blocks:(d + 1) * blocks])
    out_ref[...] = partial_ref[...] + total
    update = share(turned_ref[...], total)
    if count == 1:
        update += update.T
    store_upper(update_ref, update)


def far_product(tops, partial, turned, crossed, slots):
    n, blocks = len(tops), len(crossed[0])
    rows, width = partial.shape
    chosen = (n // 2 - 1,) + tops[0].shape
    bands = [band for bands in crossed for band in bands]
    return pl.pallas_call(
        functools.partial(far_kernel, n, blocks),
        out_shape=(
            jax.ShapeDtypeStruct((rows, width), jnp.float32),
            jax.ShapeDtypeStruct(chosen, jnp.bfloat16),
            jax.ShapeDtypeStruct((width // 4, 5 * (width // 2)), jnp.bfloat16),
        ),
        in_specs=[SMEM] + [VMEM] * (2 + n + len(bands)),
        out_specs=(VMEM, VMEM, VMEM),
        scratch_shapes=[pltpu.VMEM(chosen, jnp.bfloat16)],
        compiler_params=PARAMS,
        name="far",
    )(slots, partial, turned, *tops, *bands)


def last_kernel(count, blocks, partial_ref, chosen_ref, turned_ref, *refs):
    bands, others, (selected_ref, update_ref) = refs[:count * blocks], refs[count * blocks:-2], refs[-2:]
    total = banded_dot(chosen_ref.at[0], bands[:blocks])
    for d in range(1, count):
        total += banded_dot(chosen_ref.at[d], bands[d * blocks:(d + 1) * blocks])
    selected_ref[...] = partial_ref[...] + total
    update = share(turned_ref[...], total)
    if count == 1:
        update += update.T
    store_upper(update_ref, update, *others)


def last_product(partial, chosen, turned, swapped, others):
    rows, width = partial.shape
    bands = [band for bands in swapped for band in bands]
    return pl.pallas_call(
        functools.partial(last_kernel, len(swapped), len(swapped[0])),
        out_shape=(
            jax.ShapeDtypeStruct((rows, width), jnp.float32),
            jax.ShapeDtypeStruct((width // 4, 5 * (width // 2)), jnp.bfloat16),
        ),
        in_specs=[VMEM] * (3 + len(bands) + len(others)),
        out_specs=(VMEM, VMEM),
        compiler_params=PARAMS,
        name="last",
    )(partial, chosen, turned, *bands, *others)


def finish_kernel(diag_ref, *refs):
    out_ref = refs[-1]
    total = refs[0][...].astype(jnp.float32)
    for ref in refs[1:-1]:
        total += ref[...].astype(jnp.float32)
    quarter = total.shape[0]
    half = 2 * quarter
    tiles = [total[:, t * half:(t + 1) * half] for t in range(5)]
    rows = lax.broadcasted_iota(jnp.int32, (half, half), 0)
    columns = lax.broadcasted_iota(jnp.int32, (half, half), 1)
    mirrored = (rows >= quarter) & (columns < quarter)

    def corner(top, bottom):
        block = jnp.concatenate([top, bottom], axis=0)
        return jnp.where(mirrored, block.T, block)

    side = jnp.concatenate([tiles[1], tiles[2]], axis=0)
    out_ref[0, :half, :half] = diag_ref[0, :half, :half] + corner(tiles[0], tiles[4])
    out_ref[0, :half, half:] = diag_ref[0, :half, half:] + side
    out_ref[0, half:, :half] = diag_ref[0, half:, :half] + side.T
    out_ref[0, half:, half:] = diag_ref[0, half:, half:] + corner(tiles[3], pltpu.roll(tiles[4], quarter, 1))


def finish(diag_inverse, updates):
    return pl.pallas_call(
        finish_kernel,
        out_shape=jax.ShapeDtypeStruct(diag_inverse.shape, jnp.float32),
        in_specs=[VMEM] * (1 + len(updates)),
        out_specs=VMEM,
        compiler_params=PARAMS,
        name="finish",
    )(diag_inverse, *updates)


def on_device(n, inverse_top, diag_inverse, cross_blocks, pattern):
    pairs = n // PAIR
    row, col = lax.axis_index("prow"), lax.axis_index("pcol")

    def from_pair(block, axis, shift, flip):
        moves = [
            (((m + shift) % pairs) * PAIR + (b ^ flip), m * PAIR + b) for m in range(pairs) for b in range(PAIR)
        ]
        return lax.ppermute(block, axis, moves)

    def mate(block, axis):
        return from_pair(block, axis, 0, 1)

    near = [from_pair(inverse_top, "pcol", d, 0) for d in range(1, pairs)]
    factor_panel, inverse_top, *bands = build_panel(cross_blocks, diag_inverse, pattern, inverse_top)
    beside = mate(factor_panel, "prow")
    crossed = [[from_pair(band, "prow", d, 1) for band in bands] for d in range(1, pairs)]
    crossed = [[after(held[0], beside, cost=0)] + held[1:] for held in crossed]
    near = [after(block, crossed[0][0], cost=0) for block in near]
    crossed = [held[:1] + [after(band, near[0], cost=4 * HOP_COST) for band in held[1:]] for held in crossed]
    swapped = [[mate(band, "prow") for band in held] for held in crossed]

    tops = [inverse_top, mate(inverse_top, "pcol")]
    for block in near:
        tops += [block, mate(block, "pcol")]

    place = jnp.arange(n, dtype=jnp.int32)
    wanted_pair = (row // PAIR + place // PAIR) % pairs
    wanted_side = (row % PAIR) ^ (place % PAIR)
    slots = ((wanted_pair - col // PAIR) % pairs) * PAIR + (wanted_side ^ (col % PAIR))

    partial, turned, early = near_product(tops, [factor_panel, beside], slots)
    partial, chosen, far = far_product(tops, partial, turned, crossed, slots)
    if pairs > 2:
        selected, update = last_product(partial, chosen, turned, swapped, [early, far])
        parts = [update] + [from_pair(update, "prow", d, 0) for d in range(1, pairs)]
        update = functools.reduce(jnp.add, [part.astype(jnp.float32) for part in parts]).astype(jnp.bfloat16)
    else:
        others = [early, after(from_pair(early, "prow", 1, 1), swapped[0][-1]), far]
        selected, update = last_product(partial, chosen, turned, swapped, others)
    return -selected, finish(diag_inverse, [update, mate(update, "prow")])


def solution(mesh):
    placed = (
        P(("pole", "prow"), "pcol"),
        P(("pole", "pcol"), None, None),
        P(("pole", "prow"), "pcol"),
        P("prow", "pcol"),
    )
    return jax.shard_map(
        functools.partial(on_device, mesh.shape["pcol"]),
        mesh=mesh,
        in_specs=placed,
        out_specs=(P(("pole", "prow"), "pcol"), P(("pole", "pcol"), None, None)),
        check_vma=False,
    )
```

```python
import functools
import jax
import jax.numpy as jnp
from jax import lax
from jax.experimental import pallas as pl
from jax.experimental.pallas import tpu as pltpu
from jax.sharding import PartitionSpec as P

PAIR = 2
HOP_COST = 10**10
VMEM_LIMIT = 40 * 1024 * 1024
PARAMS = pltpu.CompilerParams(vmem_limit_bytes=VMEM_LIMIT)
SMALL = pltpu.CompilerParams(vmem_limit_bytes=1024 * 1024)
SMEM = pl.BlockSpec(memory_space=pltpu.SMEM)
VMEM = pl.BlockSpec(memory_space=pltpu.VMEM)
ANY = pl.BlockSpec(memory_space=pl.ANY)
HBM = pl.BlockSpec(memory_space=pltpu.HBM)


def split(value):
    high = value.astype(jnp.bfloat16)
    return high, (value - high.astype(jnp.float32)).astype(jnp.bfloat16)


def dot(left, right):
    return jnp.dot(left, right, preferred_element_type=jnp.float32)


def token_kernel(out_ref):
    out_ref[...] = jnp.zeros_like(out_ref)


def token():
    return pl.pallas_call(
        token_kernel,
        out_shape=jax.ShapeDtypeStruct((8, 128), jnp.float32),
        out_specs=VMEM,
        compiler_params=SMALL,
        cost_estimate=pl.CostEstimate(flops=HOP_COST, bytes_accessed=0, transcendentals=0),
        name="token",
    )()


def panel_kernel(pattern_hbm, cross_ref, diag_ref, top_hbm, token_ref, panel_ref, top_ref, *refs):
    del token_ref
    bands, (pattern_ref, sems) = refs[:-2], refs[-2:]
    width = diag_ref.shape[1]
    pattern_copy = pltpu.make_async_copy(pattern_hbm, pattern_ref, sems.at[0])
    pattern_copy.start()
    top_copy = pltpu.make_async_copy(top_hbm, top_ref, sems.at[1])
    top_copy.start()
    diag_high, diag_low = split(diag_ref[0])
    solved = []
    for a in range(pattern_hbm.shape[0]):
        high, low = split(cross_ref[pl.ds(a * width, width), :])
        solved.append(dot(high, diag_high) + (dot(high, diag_low) + dot(low, diag_high)))
    pattern_copy.wait()
    for a, block in enumerate(solved):
        kept = jnp.where(pattern_ref[a] != 0, block, 0.0).astype(jnp.bfloat16)
        panel_ref[pl.ds(a * width, width), :] = kept
        bands[a][...] = kept
    top_copy.wait()


def build_panel(cross_blocks, diag_inverse, pattern, inverse_top):
    blocks = pattern.size
    band = (cross_blocks.shape[0] // blocks, cross_blocks.shape[1])
    return pl.pallas_call(
        panel_kernel,
        out_shape=(
            pltpu.VMEM(cross_blocks.shape, jnp.bfloat16),
            pltpu.VMEM(inverse_top.shape, inverse_top.dtype),
        )
        + (pltpu.VMEM(band, jnp.bfloat16),) * blocks,
        in_specs=[HBM, VMEM, VMEM, HBM, ANY],
        out_specs=(VMEM,) * (2 + blocks),
        scratch_shapes=[pltpu.SMEM((pattern.size,), jnp.int32), pltpu.SemaphoreType.DMA((2,))],
        compiler_params=PARAMS,
        name="panel",
    )(
        pltpu.with_memory_space_constraint(pattern.reshape(-1), pltpu.HBM),
        cross_blocks,
        diag_inverse,
        pltpu.with_memory_space_constraint(inverse_top, pltpu.HBM),
        token(),
    )


def relay_kernel(*refs):
    del refs


def after(block, *gates, cost=0):
    return pl.pallas_call(
        relay_kernel,
        out_shape=jax.ShapeDtypeStruct(block.shape, block.dtype),
        in_specs=[ANY] * (1 + len(gates)),
        out_specs=ANY,
        input_output_aliases={0: 0},
        compiler_params=SMALL,
        cost_estimate=pl.CostEstimate(flops=cost, bytes_accessed=cost // 256, transcendentals=0),
        name="relay",
    )(block, *gates)


def store_upper(out_ref, update, *others):
    half = update.shape[0] // 2
    quarter = half // 2
    left, right = update[:, :half], update[:, half:]
    lanes = lax.broadcasted_iota(jnp.int32, (quarter, half), 1)
    last = jnp.where(lanes < quarter, pltpu.roll(right[3 * quarter:], quarter, 1), left[quarter:half])
    tiles = [left[:quarter], right[:quarter], right[quarter:half], right[half:3 * quarter], last]
    for t, tile in enumerate(tiles):
        columns = pl.ds(t * half, half)
        for other in others:
            tile += other[:, columns].astype(jnp.float32)
        out_ref[:, columns] = tile.astype(jnp.bfloat16)


def share(turned, product):
    return dot(turned, product.astype(jnp.bfloat16))


def choose(slot, tops, out_ref):
    for t, top in enumerate(tops):
        @pl.when(slot == t)
        def _():
            out_ref[...] = top[...]


def near_kernel(n, slots_ref, *refs):
    tops, own, beside = refs[:n], refs[n], refs[n + 1:-4]
    partial_ref, turned_ref, update_ref, chosen_ref = refs[-4:]
    for s in range(PAIR):
        choose(slots_ref[s], tops, chosen_ref.at[s])
    turned = own[...].astype(jnp.float32).T.astype(jnp.bfloat16)
    turned_ref[...] = turned
    total = dot(chosen_ref[0], own[...]) + banded_dot(chosen_ref.at[1], beside)
    partial_ref[...] = total
    store_upper(update_ref, share(turned, total))


def near_product(tops, own, beside, slots):
    rows, width = own.shape
    return pl.pallas_call(
        functools.partial(near_kernel, len(tops)),
        out_shape=(
            jax.ShapeDtypeStruct((rows, width), jnp.float32),
            jax.ShapeDtypeStruct((width, rows), jnp.bfloat16),
            jax.ShapeDtypeStruct((width // 4, 5 * (width // 2)), jnp.bfloat16),
        ),
        in_specs=[SMEM] + [VMEM] * (len(tops) + 1 + len(beside)),
        out_specs=(VMEM, VMEM, VMEM),
        scratch_shapes=[pltpu.VMEM((PAIR,) + tops[0].shape, jnp.bfloat16)],
        compiler_params=PARAMS,
        name="near",
    )(slots, *tops, own, *beside)


def banded_dot(top, bands):
    height = bands[0].shape[0]
    total = dot(top[:, :height], bands[0][...])
    for b, band in enumerate(bands[1:], 1):
        total += dot(top[:, b * height:(b + 1) * height], band[...])
    return total


def far_kernel(n, blocks, slots_ref, partial_ref, turned_ref, *refs):
    count = n // 2 - 1
    tops, bands = refs[:n], refs[n:n + count * blocks]
    out_ref, chosen_ref, update_ref, crossing_ref = refs[n + count * blocks:]
    for d in range(count):
        choose(slots_ref[2 * d + 3], tops, crossing_ref.at[d])
        choose(slots_ref[2 * d + 2], tops, chosen_ref.at[d])
    total = banded_dot(crossing_ref.at[0], bands[:blocks])
    for d in range(1, count):
        total += banded_dot(crossing_ref.at[d], bands[d * blocks:(d + 1) * blocks])
    out_ref[...] = partial_ref[...] + total
    update = share(turned_ref[...], total)
    if count == 1:
        update += update.T
    store_upper(update_ref, update)


def far_product(tops, partial, turned, crossed, slots):
    n, blocks = len(tops), len(crossed[0])
    rows, width = partial.shape
    chosen = (n // 2 - 1,) + tops[0].shape
    bands = [band for bands in crossed for band in bands]
    return pl.pallas_call(
        functools.partial(far_kernel, n, blocks),
        out_shape=(
            jax.ShapeDtypeStruct((rows, width), jnp.float32),
            jax.ShapeDtypeStruct(chosen, jnp.bfloat16),
            jax.ShapeDtypeStruct((width // 4, 5 * (width // 2)), jnp.bfloat16),
        ),
        in_specs=[SMEM] + [VMEM] * (2 + n + len(bands)),
        out_specs=(VMEM, VMEM, VMEM),
        scratch_shapes=[pltpu.VMEM(chosen, jnp.bfloat16)],
        compiler_params=PARAMS,
        name="far",
    )(slots, partial, turned, *tops, *bands)


def last_kernel(count, blocks, partial_ref, chosen_ref, turned_ref, *refs):
    bands, others, (selected_ref, update_ref) = refs[:count * blocks], refs[count * blocks:-2], refs[-2:]
    total = banded_dot(chosen_ref.at[0], bands[:blocks])
    for d in range(1, count):
        total += banded_dot(chosen_ref.at[d], bands[d * blocks:(d + 1) * blocks])
    selected_ref[...] = partial_ref[...] + total
    update = share(turned_ref[...], total)
    if count == 1:
        update += update.T
    store_upper(update_ref, update, *others)


def last_product(partial, chosen, turned, swapped, others):
    rows, width = partial.shape
    bands = [band for bands in swapped for band in bands]
    return pl.pallas_call(
        functools.partial(last_kernel, len(swapped), len(swapped[0])),
        out_shape=(
            jax.ShapeDtypeStruct((rows, width), jnp.float32),
            jax.ShapeDtypeStruct((width // 4, 5 * (width // 2)), jnp.bfloat16),
        ),
        in_specs=[VMEM] * (3 + len(bands) + len(others)),
        out_specs=(VMEM, VMEM),
        compiler_params=PARAMS,
        name="last",
    )(partial, chosen, turned, *bands, *others)


def finish_kernel(diag_ref, *refs):
    out_ref = refs[-1]
    total = refs[0][...].astype(jnp.float32)
    for ref in refs[1:-1]:
        total += ref[...].astype(jnp.float32)
    quarter = total.shape[0]
    half = 2 * quarter
    tiles = [total[:, t * half:(t + 1) * half] for t in range(5)]
    rows = lax.broadcasted_iota(jnp.int32, (half, half), 0)
    columns = lax.broadcasted_iota(jnp.int32, (half, half), 1)
    mirrored = (rows >= quarter) & (columns < quarter)

    def corner(top, bottom):
        block = jnp.concatenate([top, bottom], axis=0)
        return jnp.where(mirrored, block.T, block)

    side = jnp.concatenate([tiles[1], tiles[2]], axis=0)
    out_ref[0, :half, :half] = diag_ref[0, :half, :half] + corner(tiles[0], tiles[4])
    out_ref[0, :half, half:] = diag_ref[0, :half, half:] + side
    out_ref[0, half:, :half] = diag_ref[0, half:, :half] + side.T
    out_ref[0, half:, half:] = diag_ref[0, half:, half:] + corner(tiles[3], pltpu.roll(tiles[4], quarter, 1))


def finish(diag_inverse, updates):
    return pl.pallas_call(
        finish_kernel,
        out_shape=jax.ShapeDtypeStruct(diag_inverse.shape, jnp.float32),
        in_specs=[VMEM] * (1 + len(updates)),
        out_specs=VMEM,
        compiler_params=PARAMS,
        name="finish",
    )(diag_inverse, *updates)


def on_device(n, inverse_top, diag_inverse, cross_blocks, pattern):
    pairs = n // PAIR
    row, col = lax.axis_index("prow"), lax.axis_index("pcol")

    def from_pair(block, axis, shift, flip):
        moves = [
            (((m + shift) % pairs) * PAIR + (b ^ flip), m * PAIR + b) for m in range(pairs) for b in range(PAIR)
        ]
        return lax.ppermute(block, axis, moves)

    def mate(block, axis):
        return from_pair(block, axis, 0, 1)

    near = [from_pair(inverse_top, "pcol", d, 0) for d in range(1, pairs)]
    factor_panel, inverse_top, *bands = build_panel(cross_blocks, diag_inverse, pattern, inverse_top)
    beside = [mate(band, "prow") for band in bands]
    crossed = [[from_pair(band, "prow", d, 1) for band in bands] for d in range(1, pairs)]
    crossed = [[after(held[0], factor_panel)] + held[1:] for held in crossed]
    near = [after(block, crossed[0][0], *beside) for block in near]
    crossed = [held[:1] + [after(band, near[0], cost=4 * HOP_COST) for band in held[1:]] for held in crossed]
    swapped = [[mate(band, "prow") for band in held] for held in crossed]

    tops = [inverse_top, mate(inverse_top, "pcol")]
    for block in near:
        tops += [block, mate(block, "pcol")]

    place = jnp.arange(n, dtype=jnp.int32)
    wanted_pair = (row // PAIR + place // PAIR) % pairs
    wanted_side = (row % PAIR) ^ (place % PAIR)
    slots = ((wanted_pair - col // PAIR) % pairs) * PAIR + (wanted_side ^ (col % PAIR))

    partial, turned, early = near_product(tops, factor_panel, beside, slots)
    partial, chosen, far = far_product(tops, partial, turned, crossed, slots)
    if pairs > 2:
        selected, update = last_product(partial, chosen, turned, swapped, [early, far])
        parts = [update] + [from_pair(update, "prow", d, 0) for d in range(1, pairs)]
        update = functools.reduce(jnp.add, [part.astype(jnp.float32) for part in parts]).astype(jnp.bfloat16)
    else:
        others = [early, after(from_pair(early, "prow", 1, 1), swapped[0][-1]), far]
        selected, update = last_product(partial, chosen, turned, swapped, others)
    return -selected, finish(diag_inverse, [update, mate(update, "prow")])


def solution(mesh):
    placed = (
        P(("pole", "prow"), "pcol"),
        P(("pole", "pcol"), None, None),
        P(("pole", "prow"), "pcol"),
        P("prow", "pcol"),
    )
    return jax.shard_map(
        functools.partial(on_device, mesh.shape["pcol"]),
        mesh=mesh,
        in_specs=placed,
        out_specs=(P(("pole", "prow"), "pcol"), P(("pole", "pcol"), None, None)),
        check_vma=False,
    )
```

```python
import functools
import jax
import jax.numpy as jnp
from jax import lax
from jax.experimental import pallas as pl
from jax.experimental.pallas import tpu as pltpu
from jax.sharding import PartitionSpec as P

PAIR = 2
HOP_COST = 10**10
VMEM_LIMIT = 40 * 1024 * 1024
PARAMS = pltpu.CompilerParams(vmem_limit_bytes=VMEM_LIMIT)
SMALL = pltpu.CompilerParams(vmem_limit_bytes=1024 * 1024)
SMEM = pl.BlockSpec(memory_space=pltpu.SMEM)
VMEM = pl.BlockSpec(memory_space=pltpu.VMEM)
ANY = pl.BlockSpec(memory_space=pl.ANY)
HBM = pl.BlockSpec(memory_space=pltpu.HBM)


def split(value):
    high = value.astype(jnp.bfloat16)
    return high, (value - high.astype(jnp.float32)).astype(jnp.bfloat16)


def dot(left, right):
    return jnp.dot(left, right, preferred_element_type=jnp.float32)


def token_kernel(out_ref):
    out_ref[...] = jnp.zeros_like(out_ref)


def token():
    return pl.pallas_call(
        token_kernel,
        out_shape=jax.ShapeDtypeStruct((8, 128), jnp.float32),
        out_specs=VMEM,
        compiler_params=SMALL,
        cost_estimate=pl.CostEstimate(flops=HOP_COST, bytes_accessed=0, transcendentals=0),
        name="token",
    )()


def panel_kernel(pattern_hbm, cross_ref, diag_ref, top_hbm, token_ref, panel_ref, top_ref, pattern_ref, sems):
    del token_ref
    width = diag_ref.shape[1]
    pattern_copy = pltpu.make_async_copy(pattern_hbm, pattern_ref, sems.at[0])
    pattern_copy.start()
    top_copy = pltpu.make_async_copy(top_hbm, top_ref, sems.at[1])
    top_copy.start()
    diag_high, diag_low = split(diag_ref[0])
    solved = []
    for a in range(pattern_hbm.shape[0]):
        high, low = split(cross_ref[pl.ds(a * width, width), :])
        solved.append(dot(high, diag_high) + (dot(high, diag_low) + dot(low, diag_high)))
    pattern_copy.wait()
    for a, block in enumerate(solved):
        kept = jnp.where(pattern_ref[a] != 0, block, 0.0)
        panel_ref[pl.ds(a * width, width), :] = kept.astype(jnp.bfloat16)
    top_copy.wait()


def build_panel(cross_blocks, diag_inverse, pattern, inverse_top):
    return pl.pallas_call(
        panel_kernel,
        out_shape=(
            pltpu.VMEM(cross_blocks.shape, jnp.bfloat16),
            pltpu.VMEM(inverse_top.shape, inverse_top.dtype),
        ),
        in_specs=[HBM, VMEM, VMEM, HBM, ANY],
        out_specs=(VMEM, VMEM),
        scratch_shapes=[pltpu.SMEM((pattern.size,), jnp.int32), pltpu.SemaphoreType.DMA((2,))],
        compiler_params=PARAMS,
        name="panel",
    )(
        pltpu.with_memory_space_constraint(pattern.reshape(-1), pltpu.HBM),
        cross_blocks,
        diag_inverse,
        pltpu.with_memory_space_constraint(inverse_top, pltpu.HBM),
        token(),
    )


def relay_kernel(*refs):
    del refs


def after(block, *gates, cost=0):
    return pl.pallas_call(
        relay_kernel,
        out_shape=jax.ShapeDtypeStruct(block.shape, block.dtype),
        in_specs=[ANY] * (1 + len(gates)),
        out_specs=ANY,
        input_output_aliases={0: 0},
        compiler_params=SMALL,
        cost_estimate=pl.CostEstimate(flops=cost, bytes_accessed=cost // 256, transcendentals=0),
        name="relay",
    )(block, *gates)


def store_upper(out_ref, update, *others):
    half = update.shape[0] // 2
    quarter = half // 2
    left, right = update[:, :half], update[:, half:]
    lanes = lax.broadcasted_iota(jnp.int32, (quarter, half), 1)
    last = jnp.where(lanes < quarter, pltpu.roll(right[3 * quarter:], quarter, 1), left[quarter:half])
    tiles = [left[:quarter], right[:quarter], right[quarter:half], right[half:3 * quarter], last]
    for t, tile in enumerate(tiles):
        columns = pl.ds(t * half, half)
        for other in others:
            tile += other[:, columns].astype(jnp.float32)
        out_ref[:, columns] = tile.astype(jnp.bfloat16)


def partial_kernel(n, slots_ref, *refs):
    tops, panels = refs[:n], refs[n:n + n // 2 + 1]
    partial_ref, chosen_ref, turned_ref, update_ref, panel_buf = refs[n + n // 2 + 1:]
    places = [0] + list(range(1, n, 2))
    for place, panel in zip(places, panels):
        panel_buf[slots_ref[place]] = panel[...]
    for d, place in enumerate(range(2, n, 2)):
        slot = slots_ref[place]
        panel_buf[slot] = jnp.zeros(panel_buf.shape[1:], panel_buf.dtype)
        for t in range(n):
            @pl.when(slot == t)
            def _():
                chosen_ref[d] = tops[t][...]
    total = dot(tops[0][...], panel_buf[0])
    for t in range(1, n):
        total += dot(tops[t][...], panel_buf[t])
    partial_ref[...] = total
    turned = panels[0][...].astype(jnp.float32).T.astype(jnp.bfloat16)
    turned_ref[...] = turned
    store_upper(update_ref, dot(turned, total.astype(jnp.bfloat16)))


def partial_product(tops, panels, slots):
    n = len(tops)
    rows, width = panels[0].shape
    return pl.pallas_call(
        functools.partial(partial_kernel, n),
        out_shape=(
            jax.ShapeDtypeStruct((rows, width), jnp.float32),
            jax.ShapeDtypeStruct((n // 2 - 1,) + tops[0].shape, jnp.bfloat16),
            jax.ShapeDtypeStruct((width, rows), jnp.bfloat16),
            jax.ShapeDtypeStruct((width // 4, 5 * (width // 2)), jnp.bfloat16),
        ),
        in_specs=[SMEM] + [VMEM] * (n + len(panels)),
        out_specs=(VMEM, VMEM, VMEM, VMEM),
        scratch_shapes=[pltpu.VMEM((n, rows, width), jnp.bfloat16)],
        compiler_params=PARAMS,
        cost_estimate=pl.CostEstimate(
            flops=2 * n * rows * rows * width, bytes_accessed=2 * n * rows * (rows + width), transcendentals=0
        ),
        name="partial",
    )(slots, *tops, *panels)


def product_kernel(count, alone, partial_ref, chosen_ref, turned_ref, *refs):
    panels, early, (selected_ref, update_ref) = refs[:count], refs[count:-2], refs[-2:]
    rest = dot(chosen_ref[0], panels[0][...])
    for d, panel in enumerate(panels[1:], 1):
        rest += dot(chosen_ref[d], panel[...])
    selected_ref[...] = partial_ref[...] + rest
    update = dot(turned_ref[...], rest.astype(jnp.bfloat16))
    if alone:
        update += update.T
    store_upper(update_ref, update, *early)


def products(partial, chosen, turned, panels, early):
    rows, width = panels[0].shape
    alone = len(panels) == 1
    return pl.pallas_call(
        functools.partial(product_kernel, len(panels), alone),
        out_shape=(
            jax.ShapeDtypeStruct((rows, width), jnp.float32),
            jax.ShapeDtypeStruct((width // 4, 5 * (width // 2)), jnp.bfloat16),
        ),
        in_specs=[VMEM] * (3 + len(panels) + len(early)),
        out_specs=(VMEM, VMEM),
        compiler_params=PARAMS,
        name="products",
    )(partial, chosen, turned, *panels, *early)


def finish_kernel(diag_ref, *refs):
    out_ref = refs[-1]
    total = refs[0][...].astype(jnp.float32)
    for ref in refs[1:-1]:
        total += ref[...].astype(jnp.float32)
    quarter = total.shape[0]
    half = 2 * quarter
    tiles = [total[:, t * half:(t + 1) * half] for t in range(5)]
    rows = lax.broadcasted_iota(jnp.int32, (half, half), 0)
    columns = lax.broadcasted_iota(jnp.int32, (half, half), 1)
    mirrored = (rows >= quarter) & (columns < quarter)

    def corner(top, bottom):
        block = jnp.concatenate([top, bottom], axis=0)
        return jnp.where(mirrored, block.T, block)

    side = jnp.concatenate([tiles[1], tiles[2]], axis=0)
    out_ref[0, :half, :half] = diag_ref[0, :half, :half] + corner(tiles[0], tiles[4])
    out_ref[0, :half, half:] = diag_ref[0, :half, half:] + side
    out_ref[0, half:, :half] = diag_ref[0, half:, :half] + side.T
    out_ref[0, half:, half:] = diag_ref[0, half:, half:] + corner(tiles[3], pltpu.roll(tiles[4], quarter, 1))


def finish(diag_inverse, updates):
    return pl.pallas_call(
        finish_kernel,
        out_shape=jax.ShapeDtypeStruct(diag_inverse.shape, jnp.float32),
        in_specs=[VMEM] * (1 + len(updates)),
        out_specs=VMEM,
        compiler_params=PARAMS,
        name="finish",
    )(diag_inverse, *updates)


def on_device(n, inverse_top, diag_inverse, cross_blocks, pattern):
    pairs = n // PAIR
    row, col = lax.axis_index("prow"), lax.axis_index("pcol")

    def from_pair(block, axis, shift, flip):
        moves = [
            (((m + shift) % pairs) * PAIR + (b ^ flip), m * PAIR + b) for m in range(pairs) for b in range(PAIR)
        ]
        return lax.ppermute(block, axis, moves)

    def mate(block, axis):
        return from_pair(block, axis, 0, 1)

    near = [from_pair(inverse_top, "pcol", d, 0) for d in range(1, pairs)]
    factor_panel, inverse_top = build_panel(cross_blocks, diag_inverse, pattern, inverse_top)
    beside = mate(factor_panel, "prow")
    crossed = [from_pair(factor_panel, "prow", d, 1) for d in range(1, pairs)]
    near = [after(block, factor_panel) for block in near]
    crossed = [after(block, near[0], beside, cost=HOP_COST) for block in crossed]
    swapped = [mate(block, "prow") for block in crossed]

    tops = [inverse_top, mate(inverse_top, "pcol")]
    for block in near:
        tops += [block, mate(block, "pcol")]

    place = jnp.arange(n, dtype=jnp.int32)
    wanted_pair = (row // PAIR + place // PAIR) % pairs
    wanted_side = (row % PAIR) ^ (place % PAIR)
    slots = ((wanted_pair - col // PAIR) % pairs) * PAIR + (wanted_side ^ (col % PAIR))

    partial, chosen, turned, early = partial_product(tops, [factor_panel, beside] + crossed, slots)
    if pairs > 2:
        selected, late = products(partial, chosen, turned, swapped, [])
        parts = [early, late] + [from_pair(part, "prow", d, 0) for part in (early, late) for d in range(1, pairs)]
        update = functools.reduce(jnp.add, [part.astype(jnp.float32) for part in parts]).astype(jnp.bfloat16)
        others = []
    else:
        others = [from_pair(early, "prow", 1, flip) for flip in (1, 0)]
        selected, update = products(partial, chosen, turned, swapped, [early])
    return -selected, finish(diag_inverse, [update, mate(update, "prow")] + others)


def solution(mesh):
    placed = (
        P(("pole", "prow"), "pcol"),
        P(("pole", "pcol"), None, None),
        P(("pole", "prow"), "pcol"),
        P("prow", "pcol"),
    )
    return jax.shard_map(
        functools.partial(on_device, mesh.shape["pcol"]),
        mesh=mesh,
        in_specs=placed,
        out_specs=(P(("pole", "prow"), "pcol"), P(("pole", "pcol"), None, None)),
        check_vma=False,
    )
```

```python
import functools
import jax
import jax.numpy as jnp
from jax import lax
from jax.experimental import pallas as pl
from jax.experimental.pallas import tpu as pltpu
from jax.sharding import PartitionSpec as P

PAIR = 2
HOP_COST = 10**10
VMEM_LIMIT = 40 * 1024 * 1024
PARAMS = pltpu.CompilerParams(vmem_limit_bytes=VMEM_LIMIT)
SMALL = pltpu.CompilerParams(vmem_limit_bytes=1024 * 1024)
SMEM = pl.BlockSpec(memory_space=pltpu.SMEM)
VMEM = pl.BlockSpec(memory_space=pltpu.VMEM)
ANY = pl.BlockSpec(memory_space=pl.ANY)
HBM = pl.BlockSpec(memory_space=pltpu.HBM)


def split(value):
    high = value.astype(jnp.bfloat16)
    return high, (value - high.astype(jnp.float32)).astype(jnp.bfloat16)


def dot(left, right):
    return jnp.dot(left, right, preferred_element_type=jnp.float32)


def token_kernel(out_ref):
    out_ref[...] = jnp.zeros_like(out_ref)


def token():
    return pl.pallas_call(
        token_kernel,
        out_shape=jax.ShapeDtypeStruct((8, 128), jnp.float32),
        out_specs=VMEM,
        compiler_params=SMALL,
        cost_estimate=pl.CostEstimate(flops=HOP_COST, bytes_accessed=0, transcendentals=0),
        name="token",
    )()


def panel_kernel(pattern_hbm, cross_ref, diag_ref, top_hbm, token_ref, panel_ref, top_ref, pattern_ref, sems):
    del token_ref
    width = diag_ref.shape[1]
    pattern_copy = pltpu.make_async_copy(pattern_hbm, pattern_ref, sems.at[0])
    pattern_copy.start()
    top_copy = pltpu.make_async_copy(top_hbm, top_ref, sems.at[1])
    top_copy.start()
    diag_high, diag_low = split(diag_ref[0])
    solved = []
    for a in range(pattern_hbm.shape[0]):
        high, low = split(cross_ref[pl.ds(a * width, width), :])
        solved.append(dot(high, diag_high) + (dot(high, diag_low) + dot(low, diag_high)))
    pattern_copy.wait()
    for a, block in enumerate(solved):
        kept = jnp.where(pattern_ref[a] != 0, block, 0.0)
        panel_ref[pl.ds(a * width, width), :] = kept.astype(jnp.bfloat16)
    top_copy.wait()


def build_panel(cross_blocks, diag_inverse, pattern, inverse_top):
    return pl.pallas_call(
        panel_kernel,
        out_shape=(
            pltpu.VMEM(cross_blocks.shape, jnp.bfloat16),
            pltpu.VMEM(inverse_top.shape, inverse_top.dtype),
        ),
        in_specs=[HBM, VMEM, VMEM, HBM, ANY],
        out_specs=(VMEM, VMEM),
        scratch_shapes=[pltpu.SMEM((pattern.size,), jnp.int32), pltpu.SemaphoreType.DMA((2,))],
        compiler_params=PARAMS,
        name="panel",
    )(
        pltpu.with_memory_space_constraint(pattern.reshape(-1), pltpu.HBM),
        cross_blocks,
        diag_inverse,
        pltpu.with_memory_space_constraint(inverse_top, pltpu.HBM),
        token(),
    )


def relay_kernel(*refs):
    del refs


def after(block, *gates, cost=0):
    return pl.pallas_call(
        relay_kernel,
        out_shape=jax.ShapeDtypeStruct(block.shape, block.dtype),
        in_specs=[ANY] * (1 + len(gates)),
        out_specs=ANY,
        input_output_aliases={0: 0},
        compiler_params=SMALL,
        cost_estimate=pl.CostEstimate(flops=cost, bytes_accessed=cost // 256, transcendentals=0),
        name="relay",
    )(block, *gates)


def store_upper(out_ref, update, *others):
    half = update.shape[0] // 2
    quarter = half // 2
    left, right = update[:, :half], update[:, half:]
    lanes = lax.broadcasted_iota(jnp.int32, (quarter, half), 1)
    last = jnp.where(lanes < quarter, pltpu.roll(right[3 * quarter:], quarter, 1), left[quarter:half])
    tiles = [left[:quarter], right[:quarter], right[quarter:half], right[half:3 * quarter], last]
    for t, tile in enumerate(tiles):
        columns = pl.ds(t * half, half)
        for other in others:
            tile += other[:, columns].astype(jnp.float32)
        out_ref[:, columns] = tile.astype(jnp.bfloat16)


def partial_kernel(n, slots_ref, *refs):
    tops, panels = refs[:n], refs[n:n + n // 2 + 1]
    partial_ref, chosen_ref, turned_ref, update_ref, panel_buf = refs[n + n // 2 + 1:]
    places = [0] + list(range(1, n, 2))
    for place, panel in zip(places, panels):
        panel_buf[slots_ref[place]] = panel[...]
    for d, place in enumerate(range(2, n, 2)):
        slot = slots_ref[place]
        panel_buf[slot] = jnp.zeros(panel_buf.shape[1:], panel_buf.dtype)
        for t in range(n):
            @pl.when(slot == t)
            def _():
                chosen_ref[d] = tops[t][...]
    total = dot(tops[0][...], panel_buf[0])
    for t in range(1, n):
        total += dot(tops[t][...], panel_buf[t])
    partial_ref[...] = total
    turned = panels[0][...].astype(jnp.float32).T.astype(jnp.bfloat16)
    turned_ref[...] = turned
    store_upper(update_ref, dot(turned, total.astype(jnp.bfloat16)))


def partial_product(tops, panels, slots):
    n = len(tops)
    rows, width = panels[0].shape
    return pl.pallas_call(
        functools.partial(partial_kernel, n),
        out_shape=(
            jax.ShapeDtypeStruct((rows, width), jnp.float32),
            jax.ShapeDtypeStruct((n // 2 - 1,) + tops[0].shape, jnp.bfloat16),
            jax.ShapeDtypeStruct((width, rows), jnp.bfloat16),
            jax.ShapeDtypeStruct((width // 4, 5 * (width // 2)), jnp.bfloat16),
        ),
        in_specs=[SMEM] + [VMEM] * (n + len(panels)),
        out_specs=(VMEM, VMEM, VMEM, VMEM),
        scratch_shapes=[pltpu.VMEM((n, rows, width), jnp.bfloat16)],
        compiler_params=PARAMS,
        cost_estimate=pl.CostEstimate(
            flops=2 * n * rows * rows * width, bytes_accessed=2 * n * rows * (rows + width), transcendentals=0
        ),
        name="partial",
    )(slots, *tops, *panels)


def product_kernel(count, alone, partial_ref, chosen_ref, turned_ref, *refs):
    panels, early, (selected_ref, update_ref) = refs[:count], refs[count:-2], refs[-2:]
    rest = dot(chosen_ref[0], panels[0][...])
    for d, panel in enumerate(panels[1:], 1):
        rest += dot(chosen_ref[d], panel[...])
    selected_ref[...] = partial_ref[...] + rest
    update = dot(turned_ref[...], rest.astype(jnp.bfloat16))
    if alone:
        update += update.T
    store_upper(update_ref, update, *early)


def products(partial, chosen, turned, panels, early):
    rows, width = panels[0].shape
    alone = len(panels) == 1
    return pl.pallas_call(
        functools.partial(product_kernel, len(panels), alone),
        out_shape=(
            jax.ShapeDtypeStruct((rows, width), jnp.float32),
            jax.ShapeDtypeStruct((width // 4, 5 * (width // 2)), jnp.bfloat16),
        ),
        in_specs=[VMEM] * (3 + len(panels) + len(early)),
        out_specs=(VMEM, VMEM),
        compiler_params=PARAMS,
        name="products",
    )(partial, chosen, turned, *panels, *early)


def finish_kernel(diag_ref, *refs):
    out_ref = refs[-1]
    total = refs[0][...].astype(jnp.float32)
    for ref in refs[1:-1]:
        total += ref[...].astype(jnp.float32)
    quarter = total.shape[0]
    half = 2 * quarter
    tiles = [total[:, t * half:(t + 1) * half] for t in range(5)]
    rows = lax.broadcasted_iota(jnp.int32, (half, half), 0)
    columns = lax.broadcasted_iota(jnp.int32, (half, half), 1)
    mirrored = (rows >= quarter) & (columns < quarter)

    def corner(top, bottom):
        block = jnp.concatenate([top, bottom], axis=0)
        return jnp.where(mirrored, block.T, block)

    side = jnp.concatenate([tiles[1], tiles[2]], axis=0)
    out_ref[0, :half, :half] = diag_ref[0, :half, :half] + corner(tiles[0], tiles[4])
    out_ref[0, :half, half:] = diag_ref[0, :half, half:] + side
    out_ref[0, half:, :half] = diag_ref[0, half:, :half] + side.T
    out_ref[0, half:, half:] = diag_ref[0, half:, half:] + corner(tiles[3], pltpu.roll(tiles[4], quarter, 1))


def finish(diag_inverse, updates):
    return pl.pallas_call(
        finish_kernel,
        out_shape=jax.ShapeDtypeStruct(diag_inverse.shape, jnp.float32),
        in_specs=[VMEM] * (1 + len(updates)),
        out_specs=VMEM,
        compiler_params=PARAMS,
        name="finish",
    )(diag_inverse, *updates)


def on_device(n, inverse_top, diag_inverse, cross_blocks, pattern):
    pairs = n // PAIR
    row, col = lax.axis_index("prow"), lax.axis_index("pcol")

    def from_pair(block, axis, shift, flip):
        moves = [
            (((m + shift) % pairs) * PAIR + (b ^ flip), m * PAIR + b) for m in range(pairs) for b in range(PAIR)
        ]
        return lax.ppermute(block, axis, moves)

    def mate(block, axis):
        return from_pair(block, axis, 0, 1)

    near = [from_pair(inverse_top, "pcol", d, 0) for d in range(1, pairs)]
    factor_panel, inverse_top = build_panel(cross_blocks, diag_inverse, pattern, inverse_top)
    beside = mate(factor_panel, "prow")
    crossed = [from_pair(factor_panel, "prow", d, 1) for d in range(1, pairs)]
    near = [after(block, factor_panel) for block in near]
    crossed = [after(block, near[0], beside, cost=HOP_COST) for block in crossed]
    swapped = [mate(block, "prow") for block in crossed]

    tops = [inverse_top, mate(inverse_top, "pcol")]
    for block in near:
        tops += [block, mate(block, "pcol")]

    place = jnp.arange(n, dtype=jnp.int32)
    wanted_pair = (row // PAIR + place // PAIR) % pairs
    wanted_side = (row % PAIR) ^ (place % PAIR)
    slots = ((wanted_pair - col // PAIR) % pairs) * PAIR + (wanted_side ^ (col % PAIR))

    partial, chosen, turned, early = partial_product(tops, [factor_panel, beside] + crossed, slots)
    if pairs > 2:
        selected, late = products(partial, chosen, turned, swapped, [])
        parts = [early, late] + [from_pair(part, "prow", d, 0) for part in (early, late) for d in range(1, pairs)]
        update = functools.reduce(jnp.add, [part.astype(jnp.float32) for part in parts]).astype(jnp.bfloat16)
        others = []
    else:
        others = [after(from_pair(early, "prow", 1, flip), early, cost=0) for flip in (1, 0)]
        selected, update = products(partial, chosen, turned, swapped, [early])
    return -selected, finish(diag_inverse, [update, mate(update, "prow")] + others)


def solution(mesh):
    placed = (
        P(("pole", "prow"), "pcol"),
        P(("pole", "pcol"), None, None),
        P(("pole", "prow"), "pcol"),
        P("prow", "pcol"),
    )
    return jax.shard_map(
        functools.partial(on_device, mesh.shape["pcol"]),
        mesh=mesh,
        in_specs=placed,
        out_specs=(P(("pole", "prow"), "pcol"), P(("pole", "pcol"), None, None)),
        check_vma=False,
    )
```

```python
import functools
import jax
import jax.numpy as jnp
from jax import lax
from jax.experimental import pallas as pl
from jax.experimental.pallas import tpu as pltpu
from jax.sharding import PartitionSpec as P

PAIR = 2
HOP_COST = 10**10
VMEM_LIMIT = 40 * 1024 * 1024
PARAMS = pltpu.CompilerParams(vmem_limit_bytes=VMEM_LIMIT)
SMALL = pltpu.CompilerParams(vmem_limit_bytes=1024 * 1024)
SMEM = pl.BlockSpec(memory_space=pltpu.SMEM)
VMEM = pl.BlockSpec(memory_space=pltpu.VMEM)
ANY = pl.BlockSpec(memory_space=pl.ANY)
HBM = pl.BlockSpec(memory_space=pltpu.HBM)


def split(value):
    high = value.astype(jnp.bfloat16)
    return high, (value - high.astype(jnp.float32)).astype(jnp.bfloat16)


def dot(left, right):
    return jnp.dot(left, right, preferred_element_type=jnp.float32)


def token_kernel(out_ref):
    out_ref[...] = jnp.zeros_like(out_ref)


def token():
    return pl.pallas_call(
        token_kernel,
        out_shape=jax.ShapeDtypeStruct((8, 128), jnp.float32),
        out_specs=VMEM,
        compiler_params=SMALL,
        cost_estimate=pl.CostEstimate(flops=HOP_COST, bytes_accessed=0, transcendentals=0),
        name="token",
    )()


def panel_kernel(pattern_hbm, cross_ref, diag_ref, top_hbm, token_ref, panel_ref, top_ref, pattern_ref, sems):
    del token_ref
    width = diag_ref.shape[1]
    pattern_copy = pltpu.make_async_copy(pattern_hbm, pattern_ref, sems.at[0])
    pattern_copy.start()
    top_copy = pltpu.make_async_copy(top_hbm, top_ref, sems.at[1])
    top_copy.start()
    diag_high, diag_low = split(diag_ref[0])
    solved = []
    for a in range(pattern_hbm.shape[0]):
        high, low = split(cross_ref[pl.ds(a * width, width), :])
        solved.append(dot(high, diag_high) + (dot(high, diag_low) + dot(low, diag_high)))
    pattern_copy.wait()
    for a, block in enumerate(solved):
        kept = jnp.where(pattern_ref[a] != 0, block, 0.0)
        panel_ref[pl.ds(a * width, width), :] = kept.astype(jnp.bfloat16)
    top_copy.wait()


def build_panel(cross_blocks, diag_inverse, pattern, inverse_top):
    return pl.pallas_call(
        panel_kernel,
        out_shape=(
            pltpu.VMEM(cross_blocks.shape, jnp.bfloat16),
            pltpu.VMEM(inverse_top.shape, inverse_top.dtype),
        ),
        in_specs=[HBM, VMEM, VMEM, HBM, ANY],
        out_specs=(VMEM, VMEM),
        scratch_shapes=[pltpu.SMEM((pattern.size,), jnp.int32), pltpu.SemaphoreType.DMA((2,))],
        compiler_params=PARAMS,
        name="panel",
    )(
        pltpu.with_memory_space_constraint(pattern.reshape(-1), pltpu.HBM),
        cross_blocks,
        diag_inverse,
        pltpu.with_memory_space_constraint(inverse_top, pltpu.HBM),
        token(),
    )


def relay_kernel(*refs):
    del refs


def after(block, *gates, cost=0):
    return pl.pallas_call(
        relay_kernel,
        out_shape=jax.ShapeDtypeStruct(block.shape, block.dtype),
        in_specs=[ANY] * (1 + len(gates)),
        out_specs=ANY,
        input_output_aliases={0: 0},
        compiler_params=SMALL,
        cost_estimate=pl.CostEstimate(flops=cost, bytes_accessed=cost // 256, transcendentals=0),
        name="relay",
    )(block, *gates)


def store_upper(out_ref, update, *others):
    half = update.shape[0] // 2
    quarter = half // 2
    left, right = update[:, :half], update[:, half:]
    lanes = lax.broadcasted_iota(jnp.int32, (quarter, half), 1)
    last = jnp.where(lanes < quarter, pltpu.roll(right[3 * quarter:], quarter, 1), left[quarter:half])
    tiles = [left[:quarter], right[:quarter], right[quarter:half], right[half:3 * quarter], last]
    for t, tile in enumerate(tiles):
        columns = pl.ds(t * half, half)
        for other in others:
            tile += other[:, columns].astype(jnp.float32)
        out_ref[:, columns] = tile.astype(jnp.bfloat16)


def partial_kernel(n, slots_ref, *refs):
    tops, panels = refs[:n], refs[n:n + n // 2 + 1]
    turned_ref, partial_ref, update_ref, panel_buf = refs[n + n // 2 + 1:]
    places = [0] + list(range(1, n, 2))
    for place, panel in zip(places, panels):
        panel_buf[slots_ref[place]] = panel[...]
    for place in range(2, n, 2):
        panel_buf[slots_ref[place]] = jnp.zeros(panel_buf.shape[1:], panel_buf.dtype)
    total = dot(tops[0][...], panel_buf[0])
    for t in range(1, n):
        total += dot(tops[t][...], panel_buf[t])
    partial_ref[...] = total
    store_upper(update_ref, dot(turned_ref[...], total.astype(jnp.bfloat16)))


def partial_product(tops, panels, turned, slots):
    n = len(tops)
    rows, width = panels[0].shape
    return pl.pallas_call(
        functools.partial(partial_kernel, n),
        out_shape=(
            jax.ShapeDtypeStruct((rows, width), jnp.float32),
            jax.ShapeDtypeStruct((width // 4, 5 * (width // 2)), jnp.bfloat16),
        ),
        in_specs=[SMEM] + [VMEM] * (n + len(panels) + 1),
        out_specs=(VMEM, VMEM),
        scratch_shapes=[pltpu.VMEM((n, rows, width), jnp.bfloat16)],
        compiler_params=PARAMS,
        cost_estimate=pl.CostEstimate(
            flops=2 * n * rows * rows * width, bytes_accessed=2 * n * rows * (rows + width), transcendentals=0
        ),
        name="partial",
    )(slots, *tops, *panels, turned)


def turn_kernel(panel_ref, turned_ref):
    turned_ref[...] = panel_ref[...].astype(jnp.float32).T.astype(jnp.bfloat16)


def turn(panel):
    return pl.pallas_call(
        turn_kernel,
        out_shape=jax.ShapeDtypeStruct(panel.shape[::-1], panel.dtype),
        in_specs=[VMEM],
        out_specs=VMEM,
        compiler_params=PARAMS,
        name="turn",
    )(panel)


def choose_kernel(n, slots_ref, *refs):
    tops, chosen_ref = refs[:n], refs[n]
    for d, place in enumerate(range(2, n, 2)):
        for t in range(n):
            @pl.when(slots_ref[place] == t)
            def _():
                chosen_ref[d] = tops[t][...]


def choose(tops, slots):
    n = len(tops)
    return pl.pallas_call(
        functools.partial(choose_kernel, n),
        out_shape=jax.ShapeDtypeStruct((n // 2 - 1,) + tops[0].shape, jnp.bfloat16),
        in_specs=[SMEM] + [VMEM] * n,
        out_specs=VMEM,
        compiler_params=PARAMS,
        name="choose",
    )(slots, *tops)


def product_kernel(count, alone, partial_ref, chosen_ref, turned_ref, *refs):
    panels, early, (selected_ref, update_ref) = refs[:count], refs[count:-2], refs[-2:]
    rest = dot(chosen_ref[0], panels[0][...])
    for d, panel in enumerate(panels[1:], 1):
        rest += dot(chosen_ref[d], panel[...])
    selected_ref[...] = partial_ref[...] + rest
    update = dot(turned_ref[...], rest.astype(jnp.bfloat16))
    if alone:
        update += update.T
    store_upper(update_ref, update, *early)


def products(partial, chosen, turned, panels, early):
    rows, width = panels[0].shape
    alone = len(panels) == 1
    return pl.pallas_call(
        functools.partial(product_kernel, len(panels), alone),
        out_shape=(
            jax.ShapeDtypeStruct((rows, width), jnp.float32),
            jax.ShapeDtypeStruct((width // 4, 5 * (width // 2)), jnp.bfloat16),
        ),
        in_specs=[VMEM] * (3 + len(panels) + len(early)),
        out_specs=(VMEM, VMEM),
        compiler_params=PARAMS,
        name="products",
    )(partial, chosen, turned, *panels, *early)


def finish_kernel(diag_ref, *refs):
    updates, (out_hbm, out_ref, sems) = refs[:-3], refs[-3:]
    total = updates[0][...].astype(jnp.float32)
    for ref in updates[1:]:
        total += ref[...].astype(jnp.float32)
    quarter = total.shape[0]
    half = 2 * quarter
    tiles = [total[:, t * half:(t + 1) * half] for t in range(5)]
    rows = lax.broadcasted_iota(jnp.int32, (half, half), 0)
    columns = lax.broadcasted_iota(jnp.int32, (half, half), 1)
    mirrored = (rows >= quarter) & (columns < quarter)
    stores = [
        pltpu.make_async_copy(out_ref.at[h], out_hbm.at[0, pl.ds(h * half, half)], sems.at[h]) for h in range(2)
    ]

    def corner(top, bottom):
        block = jnp.concatenate([top, bottom], axis=0)
        return jnp.where(mirrored, block.T, block)

    side = jnp.concatenate([tiles[1], tiles[2]], axis=0)
    out_ref[0, :, :half] = diag_ref[0, :half, :half] + corner(tiles[0], tiles[4])
    out_ref[0, :, half:] = diag_ref[0, :half, half:] + side
    stores[0].start()
    out_ref[1, :, :half] = diag_ref[0, half:, :half] + side.T
    out_ref[1, :, half:] = diag_ref[0, half:, half:] + corner(tiles[3], pltpu.roll(tiles[4], quarter, 1))
    stores[1].start()
    for store in stores:
        store.wait()


def finish(diag_inverse, updates):
    width = diag_inverse.shape[1]
    return pl.pallas_call(
        finish_kernel,
        out_shape=jax.ShapeDtypeStruct(diag_inverse.shape, jnp.float32),
        in_specs=[VMEM] * (1 + len(updates)),
        out_specs=ANY,
        scratch_shapes=[pltpu.VMEM((2, width // 2, width), jnp.float32), pltpu.SemaphoreType.DMA((2,))],
        compiler_params=PARAMS,
        name="finish",
    )(diag_inverse, *updates)


def on_device(n, inverse_top, diag_inverse, cross_blocks, pattern):
    pairs = n // PAIR
    row, col = lax.axis_index("prow"), lax.axis_index("pcol")

    def from_pair(block, axis, shift, flip):
        moves = [
            (((m + shift) % pairs) * PAIR + (b ^ flip), m * PAIR + b) for m in range(pairs) for b in range(PAIR)
        ]
        return lax.ppermute(block, axis, moves)

    def mate(block, axis):
        return from_pair(block, axis, 0, 1)

    near = [from_pair(inverse_top, "pcol", d, 0) for d in range(1, pairs)]
    factor_panel, inverse_top = build_panel(cross_blocks, diag_inverse, pattern, inverse_top)
    beside = mate(factor_panel, "prow")
    crossed = [from_pair(factor_panel, "prow", d, 1) for d in range(1, pairs)]
    turned = turn(factor_panel)
    near = [after(block, turned) for block in near]
    crossed = [after(block, near[0], cost=HOP_COST) for block in crossed]
    beside = after(beside, *crossed, cost=2 * HOP_COST)
    swapped = [mate(block, "prow") for block in crossed]

    tops = [inverse_top, mate(inverse_top, "pcol")]
    for block in near:
        tops += [block, mate(block, "pcol")]

    place = jnp.arange(n, dtype=jnp.int32)
    wanted_pair = (row // PAIR + place // PAIR) % pairs
    wanted_side = (row % PAIR) ^ (place % PAIR)
    slots = ((wanted_pair - col // PAIR) % pairs) * PAIR + (wanted_side ^ (col % PAIR))

    partial, early = partial_product(tops, [factor_panel, beside] + crossed, turned, slots)
    chosen = choose(tops, slots)
    early = [early] + [after(from_pair(early, "prow", d, 1), swapped[-1]) for d in range(1, pairs)]
    if pairs > 2:
        selected, late = products(partial, chosen, turned, swapped, [])
        parts = early + [late] + [from_pair(late, "prow", d, 0) for d in range(1, pairs)]
        update = functools.reduce(jnp.add, [part.astype(jnp.float32) for part in parts]).astype(jnp.bfloat16)
    else:
        selected, update = products(partial, chosen, turned, swapped, early)
    return -selected, finish(diag_inverse, [update, mate(update, "prow")])


def solution(mesh):
    placed = (
        P(("pole", "prow"), "pcol"),
        P(("pole", "pcol"), None, None),
        P(("pole", "prow"), "pcol"),
        P("prow", "pcol"),
    )
    return jax.shard_map(
        functools.partial(on_device, mesh.shape["pcol"]),
        mesh=mesh,
        in_specs=placed,
        out_specs=(P(("pole", "prow"), "pcol"), P(("pole", "pcol"), None, None)),
        check_vma=False,
    )
```

```python
import functools
import jax
import jax.numpy as jnp
from jax import lax
from jax.experimental import pallas as pl
from jax.experimental.pallas import tpu as pltpu
from jax.sharding import PartitionSpec as P

PAIR = 2
HOP_COST = 10**10
VMEM_LIMIT = 40 * 1024 * 1024
PARAMS = pltpu.CompilerParams(vmem_limit_bytes=VMEM_LIMIT)
SMALL = pltpu.CompilerParams(vmem_limit_bytes=1024 * 1024)
SMEM = pl.BlockSpec(memory_space=pltpu.SMEM)
VMEM = pl.BlockSpec(memory_space=pltpu.VMEM)
ANY = pl.BlockSpec(memory_space=pl.ANY)
HBM = pl.BlockSpec(memory_space=pltpu.HBM)


def split(value):
    high = value.astype(jnp.bfloat16)
    return high, (value - high.astype(jnp.float32)).astype(jnp.bfloat16)


def dot(left, right):
    return jnp.dot(left, right, preferred_element_type=jnp.float32)


def token_kernel(out_ref):
    out_ref[...] = jnp.zeros_like(out_ref)


def token():
    return pl.pallas_call(
        token_kernel,
        out_shape=jax.ShapeDtypeStruct((8, 128), jnp.float32),
        out_specs=VMEM,
        compiler_params=SMALL,
        cost_estimate=pl.CostEstimate(flops=HOP_COST, bytes_accessed=0, transcendentals=0),
        name="token",
    )()


def panel_kernel(pattern_hbm, cross_ref, diag_ref, top_hbm, token_ref, panel_ref, top_ref, pattern_ref, sems):
    del token_ref
    width = diag_ref.shape[1]
    pattern_copy = pltpu.make_async_copy(pattern_hbm, pattern_ref, sems.at[0])
    pattern_copy.start()
    top_copy = pltpu.make_async_copy(top_hbm, top_ref, sems.at[1])
    top_copy.start()
    diag_high, diag_low = split(diag_ref[0])
    solved = []
    for a in range(pattern_hbm.shape[0]):
        high, low = split(cross_ref[pl.ds(a * width, width), :])
        solved.append(dot(high, diag_high) + (dot(high, diag_low) + dot(low, diag_high)))
    pattern_copy.wait()
    for a, block in enumerate(solved):
        kept = jnp.where(pattern_ref[a] != 0, block, 0.0)
        panel_ref[pl.ds(a * width, width), :] = kept.astype(jnp.bfloat16)
    top_copy.wait()


def build_panel(cross_blocks, diag_inverse, pattern, inverse_top):
    return pl.pallas_call(
        panel_kernel,
        out_shape=(
            pltpu.VMEM(cross_blocks.shape, jnp.bfloat16),
            pltpu.VMEM(inverse_top.shape, inverse_top.dtype),
        ),
        in_specs=[HBM, VMEM, VMEM, HBM, ANY],
        out_specs=(VMEM, VMEM),
        scratch_shapes=[pltpu.SMEM((pattern.size,), jnp.int32), pltpu.SemaphoreType.DMA((2,))],
        compiler_params=PARAMS,
        name="panel",
    )(
        pltpu.with_memory_space_constraint(pattern.reshape(-1), pltpu.HBM),
        cross_blocks,
        diag_inverse,
        pltpu.with_memory_space_constraint(inverse_top, pltpu.HBM),
        token(),
    )


def relay_kernel(*refs):
    del refs


def after(block, *gates, cost=0):
    return pl.pallas_call(
        relay_kernel,
        out_shape=jax.ShapeDtypeStruct(block.shape, block.dtype),
        in_specs=[ANY] * (1 + len(gates)),
        out_specs=ANY,
        input_output_aliases={0: 0},
        compiler_params=SMALL,
        cost_estimate=pl.CostEstimate(flops=cost, bytes_accessed=cost // 256, transcendentals=0),
        name="relay",
    )(block, *gates)


def store_upper(out_ref, update, *others):
    half = update.shape[0] // 2
    quarter = half // 2
    left, right = update[:, :half], update[:, half:]
    lanes = lax.broadcasted_iota(jnp.int32, (quarter, half), 1)
    last = jnp.where(lanes < quarter, pltpu.roll(right[3 * quarter:], quarter, 1), left[quarter:half])
    tiles = [left[:quarter], right[:quarter], right[quarter:half], right[half:3 * quarter], last]
    for t, tile in enumerate(tiles):
        columns = pl.ds(t * half, half)
        for other in others:
            tile += other[:, columns].astype(jnp.float32)
        out_ref[:, columns] = tile.astype(out_ref.dtype)


def partial_kernel(n, slots_ref, *refs):
    tops, panels = refs[:n], refs[n:n + n // 2 + 1]
    turned_ref, partial_ref, update_ref, panel_buf = refs[n + n // 2 + 1:]

    def run(pairs):
        total = dot(*[ref[...] for ref in pairs[0]])
        for top, panel in pairs[1:]:
            total += dot(top[...], panel[...])
        partial_ref[...] = total
        store_upper(update_ref, dot(turned_ref[...], total.astype(jnp.bfloat16)))

    if n == 2 * PAIR:
        for own in range(n):
            pl.when(slots_ref[0] == own)(functools.partial(run, list(zip([tops[own ^ s] for s in (0, 1, 3)], panels))))
        return
    places = [0] + list(range(1, n, 2))
    for place, panel in zip(places, panels):
        panel_buf[slots_ref[place]] = panel[...]
    for place in range(2, n, 2):
        panel_buf[slots_ref[place]] = jnp.zeros(panel_buf.shape[1:], panel_buf.dtype)
    run([(tops[t], panel_buf.at[t]) for t in range(n)])


def partial_product(tops, panels, turned, slots):
    n = len(tops)
    rows, width = panels[0].shape
    return pl.pallas_call(
        functools.partial(partial_kernel, n),
        out_shape=(
            jax.ShapeDtypeStruct((rows, width), jnp.float32),
            jax.ShapeDtypeStruct((width // 4, 5 * (width // 2)), jnp.bfloat16),
        ),
        in_specs=[SMEM] + [VMEM] * (n + len(panels) + 1),
        out_specs=(VMEM, VMEM),
        scratch_shapes=[pltpu.VMEM((n, rows, width), jnp.bfloat16)],
        compiler_params=PARAMS,
        cost_estimate=pl.CostEstimate(
            flops=2 * n * rows * rows * width, bytes_accessed=2 * n * rows * (rows + width), transcendentals=0
        ),
        name="partial",
    )(slots, *tops, *panels, turned)


def turn_kernel(panel_ref, turned_ref):
    turned_ref[...] = panel_ref[...].astype(jnp.float32).T.astype(jnp.bfloat16)


def turn(panel):
    return pl.pallas_call(
        turn_kernel,
        out_shape=jax.ShapeDtypeStruct(panel.shape[::-1], panel.dtype),
        in_specs=[VMEM],
        out_specs=VMEM,
        compiler_params=PARAMS,
        name="turn",
    )(panel)


def choose_kernel(n, slots_ref, *refs):
    tops, chosen_ref = refs[:n], refs[n]
    for d, place in enumerate(range(2, n, 2)):
        for t in range(n):
            @pl.when(slots_ref[place] == t)
            def _():
                chosen_ref[d] = tops[t][...]


def choose(tops, slots):
    n = len(tops)
    return pl.pallas_call(
        functools.partial(choose_kernel, n),
        out_shape=jax.ShapeDtypeStruct((n // 2 - 1,) + tops[0].shape, jnp.bfloat16),
        in_specs=[SMEM] + [VMEM] * n,
        out_specs=VMEM,
        compiler_params=PARAMS,
        name="choose",
    )(slots, *tops)


def product_kernel(count, alone, partial_ref, chosen_ref, turned_ref, *refs):
    panels, early, (selected_ref, update_ref) = refs[:count], refs[count:-2], refs[-2:]
    rest = dot(chosen_ref[0], panels[0][...])
    for d, panel in enumerate(panels[1:], 1):
        rest += dot(chosen_ref[d], panel[...])
    selected_ref[...] = partial_ref[...] + rest
    update = dot(turned_ref[...], rest.astype(jnp.bfloat16))
    if alone:
        update += update.T
    store_upper(update_ref, update, *early)


def products(partial, chosen, turned, panels, early):
    rows, width = panels[0].shape
    alone = len(panels) == 1
    return pl.pallas_call(
        functools.partial(product_kernel, len(panels), alone),
        out_shape=(
            jax.ShapeDtypeStruct((rows, width), jnp.float32),
            jax.ShapeDtypeStruct((width // 4, 5 * (width // 2)), jnp.float32),
        ),
        in_specs=[VMEM] * (3 + len(panels) + len(early)),
        out_specs=(VMEM, VMEM),
        compiler_params=PARAMS,
        name="products",
    )(partial, chosen, turned, *panels, *early)


def finish_kernel(diag_ref, *refs):
    updates, (out_hbm, out_ref, sems) = refs[:-3], refs[-3:]
    total = updates[0][...].astype(jnp.float32)
    for ref in updates[1:]:
        total += ref[...].astype(jnp.float32)
    quarter = total.shape[0]
    half = 2 * quarter
    tiles = [total[:, t * half:(t + 1) * half] for t in range(5)]
    rows = lax.broadcasted_iota(jnp.int32, (half, half), 0)
    columns = lax.broadcasted_iota(jnp.int32, (half, half), 1)
    mirrored = (rows >= quarter) & (columns < quarter)
    stores = [
        pltpu.make_async_copy(out_ref.at[h], out_hbm.at[0, pl.ds(h * half, half)], sems.at[h]) for h in range(2)
    ]

    def corner(top, bottom):
        block = jnp.concatenate([top, bottom], axis=0)
        return jnp.where(mirrored, block.T, block)

    side = jnp.concatenate([tiles[1], tiles[2]], axis=0)
    out_ref[0, :, :half] = diag_ref[0, :half, :half] + corner(tiles[0], tiles[4])
    out_ref[0, :, half:] = diag_ref[0, :half, half:] + side
    stores[0].start()
    out_ref[1, :, :half] = diag_ref[0, half:, :half] + side.T
    out_ref[1, :, half:] = diag_ref[0, half:, half:] + corner(tiles[3], pltpu.roll(tiles[4], quarter, 1))
    stores[1].start()
    for store in stores:
        store.wait()


def finish(diag_inverse, updates):
    width = diag_inverse.shape[1]
    return pl.pallas_call(
        finish_kernel,
        out_shape=jax.ShapeDtypeStruct(diag_inverse.shape, jnp.float32),
        in_specs=[VMEM] * (1 + len(updates)),
        out_specs=ANY,
        scratch_shapes=[pltpu.VMEM((2, width // 2, width), jnp.float32), pltpu.SemaphoreType.DMA((2,))],
        compiler_params=PARAMS,
        name="finish",
    )(diag_inverse, *updates)


def on_device(n, inverse_top, diag_inverse, cross_blocks, pattern):
    pairs = n // PAIR
    row, col = lax.axis_index("prow"), lax.axis_index("pcol")

    def from_pair(block, axis, shift, flip):
        moves = [
            (((m + shift) % pairs) * PAIR + (b ^ flip), m * PAIR + b) for m in range(pairs) for b in range(PAIR)
        ]
        return lax.ppermute(block, axis, moves)

    def mate(block, axis):
        return from_pair(block, axis, 0, 1)

    near = [from_pair(inverse_top, "pcol", d, 0) for d in range(1, pairs)]
    factor_panel, inverse_top = build_panel(cross_blocks, diag_inverse, pattern, inverse_top)
    beside = mate(factor_panel, "prow")
    crossed = [from_pair(factor_panel, "prow", d, 1) for d in range(1, pairs)]
    turned = turn(factor_panel)
    near = [after(block, turned) for block in near]
    crossed = [after(block, near[0], cost=HOP_COST) for block in crossed]
    beside = after(beside, *crossed, cost=2 * HOP_COST)
    swapped = [mate(block, "prow") for block in crossed]

    tops = [inverse_top, mate(inverse_top, "pcol")]
    for block in near:
        tops += [block, mate(block, "pcol")]

    place = jnp.arange(n, dtype=jnp.int32)
    wanted_pair = (row // PAIR + place // PAIR) % pairs
    wanted_side = (row % PAIR) ^ (place % PAIR)
    slots = ((wanted_pair - col // PAIR) % pairs) * PAIR + (wanted_side ^ (col % PAIR))

    partial, early = partial_product(tops, [factor_panel, beside] + crossed, turned, slots)
    chosen = choose(tops, slots)
    crossing = [after(from_pair(early, "prow", d, 1), swapped[-1]) for d in range(1, pairs)]
    selected, late = products(partial, chosen, turned, swapped, [early])
    parts = [late] + crossing
    if pairs > 2:
        rest = (late - early.astype(jnp.float32)).astype(jnp.bfloat16)
        parts += [from_pair(rest, "prow", d, 0) for d in range(1, pairs)]
    update = functools.reduce(jnp.add, [part.astype(jnp.float32) for part in parts]).astype(jnp.bfloat16)
    return -selected, finish(diag_inverse, [update, mate(update, "prow")])


def solution(mesh):
    placed = (
        P(("pole", "prow"), "pcol"),
        P(("pole", "pcol"), None, None),
        P(("pole", "prow"), "pcol"),
        P("prow", "pcol"),
    )
    return jax.shard_map(
        functools.partial(on_device, mesh.shape["pcol"]),
        mesh=mesh,
        in_specs=placed,
        out_specs=(P(("pole", "prow"), "pcol"), P(("pole", "pcol"), None, None)),
        check_vma=False,
    )
```

```python
import functools
import jax
import jax.numpy as jnp
from jax import lax
from jax.experimental import pallas as pl
from jax.experimental.pallas import tpu as pltpu
from jax.sharding import PartitionSpec as P

PAIR = 2
HOP_COST = 10**10
VMEM_LIMIT = 40 * 1024 * 1024
PARAMS = pltpu.CompilerParams(vmem_limit_bytes=VMEM_LIMIT)
SMALL = pltpu.CompilerParams(vmem_limit_bytes=1024 * 1024)
VMEM = pl.BlockSpec(memory_space=pltpu.VMEM)
ANY = pl.BlockSpec(memory_space=pl.ANY)
HBM = pl.BlockSpec(memory_space=pltpu.HBM)


def split(value):
    high = value.astype(jnp.bfloat16)
    return high, (value - high.astype(jnp.float32)).astype(jnp.bfloat16)


def dot(left, right):
    return jnp.dot(left, right, preferred_element_type=jnp.float32)


def token_kernel(out_ref):
    out_ref[...] = jnp.zeros_like(out_ref)


def token():
    return pl.pallas_call(
        token_kernel,
        out_shape=jax.ShapeDtypeStruct((8, 128), jnp.float32),
        out_specs=VMEM,
        compiler_params=SMALL,
        cost_estimate=pl.CostEstimate(flops=HOP_COST, bytes_accessed=0, transcendentals=0),
        name="token",
    )()


def panel_kernel(pattern_hbm, cross_ref, diag_ref, token_ref, panel_ref, pattern_ref, sem):
    del token_ref
    width = diag_ref.shape[1]
    pattern_copy = pltpu.make_async_copy(pattern_hbm, pattern_ref, sem)
    pattern_copy.start()
    diag_high, diag_low = split(diag_ref[0])
    solved = []
    for a in range(pattern_hbm.shape[0]):
        high, low = split(cross_ref[pl.ds(a * width, width), :])
        solved.append(dot(high, diag_high) + (dot(high, diag_low) + dot(low, diag_high)))
    pattern_copy.wait()
    for a, block in enumerate(solved):
        kept = jnp.where(pattern_ref[a] != 0, block, 0.0)
        panel_ref[pl.ds(a * width, width), :] = kept.astype(jnp.bfloat16)


def build_panel(cross_blocks, diag_inverse, pattern):
    return pl.pallas_call(
        panel_kernel,
        out_shape=pltpu.VMEM(cross_blocks.shape, jnp.bfloat16),
        in_specs=[HBM, VMEM, VMEM, ANY],
        out_specs=VMEM,
        scratch_shapes=[pltpu.SMEM((pattern.size,), jnp.int32), pltpu.SemaphoreType.DMA],
        compiler_params=PARAMS,
        name="panel",
    )(
        pltpu.with_memory_space_constraint(pattern.reshape(-1), pltpu.HBM),
        cross_blocks,
        diag_inverse,
        token(),
    )


def relay_kernel(*refs):
    del refs


def after(block, *gates, cost=0):
    return pl.pallas_call(
        relay_kernel,
        out_shape=jax.ShapeDtypeStruct(block.shape, block.dtype),
        in_specs=[ANY] * (1 + len(gates)),
        out_specs=ANY,
        input_output_aliases={0: 0},
        compiler_params=SMALL,
        cost_estimate=pl.CostEstimate(flops=cost, bytes_accessed=cost // 256, transcendentals=0),
        name="relay",
    )(block, *gates)


def store_upper(out_ref, update, *others):
    half = update.shape[0] // 2
    quarter = half // 2
    left, right = update[:, :half], update[:, half:]
    lanes = lax.broadcasted_iota(jnp.int32, (quarter, half), 1)
    last = jnp.where(lanes < quarter, pltpu.roll(right[3 * quarter:], quarter, 1), left[quarter:half])
    tiles = [left[:quarter], right[:quarter], right[quarter:half], right[half:3 * quarter], last]
    for t, tile in enumerate(tiles):
        columns = pl.ds(t * half, half)
        for other in others:
            tile += other[:, columns].astype(jnp.float32)
        out_ref[:, columns] = tile.astype(out_ref.dtype)


def place_of(n, d, f):
    pairs = n // PAIR
    row, col = lax.axis_index("prow"), lax.axis_index("pcol")
    pair = (row // PAIR + d + pairs - col // PAIR) % pairs
    side = (row + f + col) % PAIR
    return pair * PAIR + side


def partial_kernel(n, *refs):
    tops, panels = refs[:n], refs[n:n + n // 2 + 1]
    turned_ref, partial_ref, update_ref, panel_buf = refs[n + n // 2 + 1:]

    def run(pairs):
        total = dot(*[ref[...] for ref in pairs[0]])
        for top, panel in pairs[1:]:
            total += dot(top[...], panel[...])
        partial_ref[...] = total
        store_upper(update_ref, dot(turned_ref[...], total.astype(jnp.bfloat16)))

    if n == 2 * PAIR:
        place = place_of(n, 0, 0)
        for own in range(n):
            pl.when(place == own)(functools.partial(run, list(zip([tops[own ^ s] for s in (0, 1, 3)], panels))))
        return
    pairs = n // PAIR
    held = [(0, 0)] + [(d, 1) for d in range(pairs)]
    for (d, f), panel in zip(held, panels):
        panel_buf[place_of(n, d, f)] = panel[...]
    for d in range(1, pairs):
        panel_buf[place_of(n, d, 0)] = jnp.zeros(panel_buf.shape[1:], panel_buf.dtype)
    run([(tops[t], panel_buf.at[t]) for t in range(n)])


def partial_product(tops, panels, turned):
    n = len(tops)
    rows, width = panels[0].shape
    return pl.pallas_call(
        functools.partial(partial_kernel, n),
        out_shape=(
            jax.ShapeDtypeStruct((rows, width), jnp.float32),
            jax.ShapeDtypeStruct((width // 4, 5 * (width // 2)), jnp.bfloat16),
        ),
        in_specs=[VMEM] * (n + len(panels) + 1),
        out_specs=(VMEM, VMEM),
        scratch_shapes=[pltpu.VMEM((n, rows, width), jnp.bfloat16)],
        compiler_params=PARAMS,
        cost_estimate=pl.CostEstimate(
            flops=2 * n * rows * rows * width, bytes_accessed=2 * n * rows * (rows + width), transcendentals=0
        ),
        name="partial",
    )(*tops, *panels, turned)


def stage_kernel(panel_ref, top_hbm, turned_ref, top_ref, sem):
    copy = pltpu.make_async_copy(top_hbm, top_ref, sem)
    copy.start()
    turned_ref[...] = panel_ref[...].astype(jnp.float32).T.astype(jnp.bfloat16)
    copy.wait()


def stage(panel, inverse_top):
    return pl.pallas_call(
        stage_kernel,
        out_shape=(pltpu.VMEM(panel.shape[::-1], panel.dtype), pltpu.VMEM(inverse_top.shape, inverse_top.dtype)),
        in_specs=[VMEM, HBM],
        out_specs=(VMEM, VMEM),
        scratch_shapes=[pltpu.SemaphoreType.DMA],
        compiler_params=PARAMS,
        name="stage",
    )(panel, pltpu.with_memory_space_constraint(inverse_top, pltpu.HBM))


def choose_kernel(n, *refs):
    tops, chosen_ref = refs[:n], refs[n]
    for d in range(1, n // PAIR):
        place = place_of(n, d, 0)
        for t in range(n):
            @pl.when(place == t)
            def _():
                chosen_ref[d - 1] = tops[t][...]


def choose(tops):
    n = len(tops)
    return pl.pallas_call(
        functools.partial(choose_kernel, n),
        out_shape=jax.ShapeDtypeStruct((n // 2 - 1,) + tops[0].shape, jnp.bfloat16),
        in_specs=[VMEM] * n,
        out_specs=VMEM,
        compiler_params=PARAMS,
        name="choose",
    )(*tops)


def product_kernel(count, alone, partial_ref, chosen_ref, turned_ref, *refs):
    panels, early, (selected_ref, update_ref) = refs[:count], refs[count:-2], refs[-2:]
    rest = dot(chosen_ref[0], panels[0][...])
    for d, panel in enumerate(panels[1:], 1):
        rest += dot(chosen_ref[d], panel[...])
    selected_ref[...] = partial_ref[...] + rest
    update = dot(turned_ref[...], rest.astype(jnp.bfloat16))
    if alone:
        update += update.T
    store_upper(update_ref, update, *early)


def products(partial, chosen, turned, panels, early):
    rows, width = panels[0].shape
    alone = len(panels) == 1
    return pl.pallas_call(
        functools.partial(product_kernel, len(panels), alone),
        out_shape=(
            jax.ShapeDtypeStruct((rows, width), jnp.float32),
            jax.ShapeDtypeStruct((width // 4, 5 * (width // 2)), jnp.float32),
        ),
        in_specs=[VMEM] * (3 + len(panels) + len(early)),
        out_specs=(VMEM, VMEM),
        compiler_params=PARAMS,
        name="products",
    )(partial, chosen, turned, *panels, *early)


def finish_kernel(diag_ref, *refs):
    updates, (out_hbm, out_ref, sems) = refs[:-3], refs[-3:]
    total = updates[0][...].astype(jnp.float32)
    for ref in updates[1:]:
        total += ref[...].astype(jnp.float32)
    quarter = total.shape[0]
    half = 2 * quarter
    tiles = [total[:, t * half:(t + 1) * half] for t in range(5)]
    rows = lax.broadcasted_iota(jnp.int32, (half, half), 0)
    columns = lax.broadcasted_iota(jnp.int32, (half, half), 1)
    mirrored = (rows >= quarter) & (columns < quarter)
    stores = [
        pltpu.make_async_copy(out_ref.at[h], out_hbm.at[0, pl.ds(h * half, half)], sems.at[h]) for h in range(2)
    ]

    def corner(top, bottom):
        block = jnp.concatenate([top, bottom], axis=0)
        return jnp.where(mirrored, block.T, block)

    side = jnp.concatenate([tiles[1], tiles[2]], axis=0)
    out_ref[0, :, :half] = diag_ref[0, :half, :half] + corner(tiles[0], tiles[4])
    out_ref[0, :, half:] = diag_ref[0, :half, half:] + side
    stores[0].start()
    out_ref[1, :, :half] = diag_ref[0, half:, :half] + side.T
    out_ref[1, :, half:] = diag_ref[0, half:, half:] + corner(tiles[3], pltpu.roll(tiles[4], quarter, 1))
    stores[1].start()
    for store in stores:
        store.wait()


def finish(diag_inverse, updates):
    width = diag_inverse.shape[1]
    return pl.pallas_call(
        finish_kernel,
        out_shape=jax.ShapeDtypeStruct(diag_inverse.shape, jnp.float32),
        in_specs=[VMEM] * (1 + len(updates)),
        out_specs=ANY,
        scratch_shapes=[pltpu.VMEM((2, width // 2, width), jnp.float32), pltpu.SemaphoreType.DMA((2,))],
        compiler_params=PARAMS,
        name="finish",
    )(diag_inverse, *updates)


def on_device(n, inverse_top, diag_inverse, cross_blocks, pattern):
    pairs = n // PAIR

    def from_pair(block, axis, shift, flip):
        moves = [
            (((m + shift) % pairs) * PAIR + (b ^ flip), m * PAIR + b) for m in range(pairs) for b in range(PAIR)
        ]
        return lax.ppermute(block, axis, moves)

    def mate(block, axis):
        return from_pair(block, axis, 0, 1)

    near = [from_pair(inverse_top, "pcol", d, 0) for d in range(1, pairs)]
    factor_panel = build_panel(cross_blocks, diag_inverse, pattern)
    beside = mate(factor_panel, "prow")
    crossed = [from_pair(factor_panel, "prow", d, 1) for d in range(1, pairs)]
    turned, inverse_top = stage(factor_panel, inverse_top)
    near = [after(block, turned) for block in near]
    crossed = [after(block, near[0], cost=HOP_COST) for block in crossed]
    beside = after(beside, *crossed, cost=2 * HOP_COST)
    swapped = [mate(block, "prow") for block in crossed]

    tops = [inverse_top, mate(inverse_top, "pcol")]
    for block in near:
        tops += [block, mate(block, "pcol")]

    partial, early = partial_product(tops, [factor_panel, beside] + crossed, turned)
    chosen = choose(tops)
    crossing = [after(from_pair(early, "prow", d, 1), swapped[-1]) for d in range(1, pairs)]
    selected, late = products(partial, chosen, turned, swapped, [early])
    parts = [late] + crossing
    if pairs > 2:
        rest = (late - early.astype(jnp.float32)).astype(jnp.bfloat16)
        parts += [from_pair(rest, "prow", d, 0) for d in range(1, pairs)]
    update = functools.reduce(jnp.add, [part.astype(jnp.float32) for part in parts]).astype(jnp.bfloat16)
    return -selected, finish(diag_inverse, [update, mate(update, "prow")])


def solution(mesh):
    placed = (
        P(("pole", "prow"), "pcol"),
        P(("pole", "pcol"), None, None),
        P(("pole", "prow"), "pcol"),
        P("prow", "pcol"),
    )
    return jax.shard_map(
        functools.partial(on_device, mesh.shape["pcol"]),
        mesh=mesh,
        in_specs=placed,
        out_specs=(P(("pole", "prow"), "pcol"), P(("pole", "pcol"), None, None)),
        check_vma=False,
    )
```

```python
import functools
import jax
import jax.numpy as jnp
from jax import lax
from jax.experimental import pallas as pl
from jax.experimental.pallas import tpu as pltpu
from jax.sharding import PartitionSpec as P

PAIR = 2
HOP_COST = 10**10
VMEM_LIMIT = 40 * 1024 * 1024
PARAMS = pltpu.CompilerParams(vmem_limit_bytes=VMEM_LIMIT)
SMALL = pltpu.CompilerParams(vmem_limit_bytes=1024 * 1024)
VMEM = pl.BlockSpec(memory_space=pltpu.VMEM)
ANY = pl.BlockSpec(memory_space=pl.ANY)
HBM = pl.BlockSpec(memory_space=pltpu.HBM)


def split(value):
    high = value.astype(jnp.bfloat16)
    return high, (value - high.astype(jnp.float32)).astype(jnp.bfloat16)


def dot(left, right):
    return jnp.dot(left, right, preferred_element_type=jnp.float32)


def token_kernel(out_ref):
    out_ref[...] = jnp.zeros_like(out_ref)


def token():
    return pl.pallas_call(
        token_kernel,
        out_shape=jax.ShapeDtypeStruct((8, 128), jnp.float32),
        out_specs=VMEM,
        compiler_params=SMALL,
        cost_estimate=pl.CostEstimate(flops=HOP_COST, bytes_accessed=0, transcendentals=0),
        name="token",
    )()


def panel_kernel(pattern_hbm, cross_ref, diag_ref, token_ref, panel_ref, pattern_ref, sem):
    del token_ref
    width = diag_ref.shape[1]
    pattern_copy = pltpu.make_async_copy(pattern_hbm, pattern_ref, sem)
    pattern_copy.start()
    diag_high, diag_low = split(diag_ref[0])
    solved = []
    for a in range(pattern_hbm.shape[0]):
        high, low = split(cross_ref[pl.ds(a * width, width), :])
        solved.append(dot(high, diag_high) + (dot(high, diag_low) + dot(low, diag_high)))
    pattern_copy.wait()
    for a, block in enumerate(solved):
        kept = jnp.where(pattern_ref[a] != 0, block, 0.0)
        panel_ref[pl.ds(a * width, width), :] = kept.astype(jnp.bfloat16)


def build_panel(cross_blocks, diag_inverse, pattern):
    return pl.pallas_call(
        panel_kernel,
        out_shape=pltpu.VMEM(cross_blocks.shape, jnp.bfloat16),
        in_specs=[HBM, VMEM, VMEM, ANY],
        out_specs=VMEM,
        scratch_shapes=[pltpu.SMEM((pattern.size,), jnp.int32), pltpu.SemaphoreType.DMA],
        compiler_params=PARAMS,
        name="panel",
    )(
        pltpu.with_memory_space_constraint(pattern.reshape(-1), pltpu.HBM),
        cross_blocks,
        diag_inverse,
        token(),
    )


def relay_kernel(*refs):
    del refs


def after(block, *gates, cost=0):
    return pl.pallas_call(
        relay_kernel,
        out_shape=jax.ShapeDtypeStruct(block.shape, block.dtype),
        in_specs=[ANY] * (1 + len(gates)),
        out_specs=ANY,
        input_output_aliases={0: 0},
        compiler_params=SMALL,
        cost_estimate=pl.CostEstimate(flops=cost, bytes_accessed=cost // 256, transcendentals=0),
        name="relay",
    )(block, *gates)


def store_upper(out_ref, update, *others):
    half = update.shape[0] // 2
    quarter = half // 2
    left, right = update[:, :half], update[:, half:]
    lanes = lax.broadcasted_iota(jnp.int32, (quarter, half), 1)
    last = jnp.where(lanes < quarter, pltpu.roll(right[3 * quarter:], quarter, 1), left[quarter:half])
    tiles = [left[:quarter], right[:quarter], right[quarter:half], right[half:3 * quarter], last]
    for t, tile in enumerate(tiles):
        columns = pl.ds(t * half, half)
        for other in others:
            tile += other[:, columns].astype(jnp.float32)
        out_ref[:, columns] = tile.astype(out_ref.dtype)


def place_of(n, d, f):
    pairs = n // PAIR
    row, col = lax.axis_index("prow"), lax.axis_index("pcol")
    pair = (row // PAIR + d + pairs - col // PAIR) % pairs
    side = (row + f + col) % PAIR
    return pair * PAIR + side


def partial_kernel(n, *refs):
    tops, panels = refs[:n], refs[n:n + n // 2 + 1]
    turned_ref, partial_ref, update_ref, copy_ref, panel_buf = refs[n + n // 2 + 1:]

    def run(pairs):
        total = dot(*[ref[...] for ref in pairs[0]])
        for top, panel in pairs[1:]:
            total += dot(top[...], panel[...])
        partial_ref[...] = total
        store_upper(update_ref, dot(turned_ref[...], total.astype(jnp.bfloat16)))
        copy_ref[...] = update_ref[...]

    if n == 2 * PAIR:
        place = place_of(n, 0, 0)
        for own in range(n):
            pl.when(place == own)(functools.partial(run, list(zip([tops[own ^ s] for s in (0, 1, 3)], panels))))
        return
    pairs = n // PAIR
    held = [(0, 0)] + [(d, 1) for d in range(pairs)]
    for (d, f), panel in zip(held, panels):
        panel_buf[place_of(n, d, f)] = panel[...]
    for d in range(1, pairs):
        panel_buf[place_of(n, d, 0)] = jnp.zeros(panel_buf.shape[1:], panel_buf.dtype)
    run([(tops[t], panel_buf.at[t]) for t in range(n)])


def partial_product(tops, panels, turned):
    n = len(tops)
    rows, width = panels[0].shape
    share = jax.ShapeDtypeStruct((width // 4, 5 * (width // 2)), jnp.bfloat16)
    return pl.pallas_call(
        functools.partial(partial_kernel, n),
        out_shape=(
            jax.ShapeDtypeStruct((rows, width), jnp.float32),
            share,
            share,
        ),
        in_specs=[VMEM] * (n + len(panels) + 1),
        out_specs=(VMEM, VMEM, VMEM),
        scratch_shapes=[pltpu.VMEM((n, rows, width), jnp.bfloat16)],
        compiler_params=PARAMS,
        cost_estimate=pl.CostEstimate(
            flops=2 * n * rows * rows * width, bytes_accessed=2 * n * rows * (rows + width), transcendentals=0
        ),
        name="partial",
    )(*tops, *panels, turned)


def stage_kernel(panel_ref, top_hbm, turned_ref, top_ref, sem):
    copy = pltpu.make_async_copy(top_hbm, top_ref, sem)
    copy.start()
    turned_ref[...] = panel_ref[...].astype(jnp.float32).T.astype(jnp.bfloat16)
    copy.wait()


def stage(panel, inverse_top):
    return pl.pallas_call(
        stage_kernel,
        out_shape=(pltpu.VMEM(panel.shape[::-1], panel.dtype), pltpu.VMEM(inverse_top.shape, inverse_top.dtype)),
        in_specs=[VMEM, HBM],
        out_specs=(VMEM, VMEM),
        scratch_shapes=[pltpu.SemaphoreType.DMA],
        compiler_params=PARAMS,
        name="stage",
    )(panel, pltpu.with_memory_space_constraint(inverse_top, pltpu.HBM))


def choose_kernel(n, *refs):
    tops, chosen_ref = refs[:n], refs[n]
    for d in range(1, n // PAIR):
        place = place_of(n, d, 0)
        for t in range(n):
            @pl.when(place == t)
            def _():
                chosen_ref[d - 1] = tops[t][...]


def choose(tops):
    n = len(tops)
    return pl.pallas_call(
        functools.partial(choose_kernel, n),
        out_shape=jax.ShapeDtypeStruct((n // 2 - 1,) + tops[0].shape, jnp.bfloat16),
        in_specs=[VMEM] * n,
        out_specs=VMEM,
        compiler_params=PARAMS,
        name="choose",
    )(*tops)


def product_kernel(count, alone, partial_ref, chosen_ref, turned_ref, *refs):
    panels, early, (selected_ref, update_ref) = refs[:count], refs[count:-2], refs[-2:]
    rest = dot(chosen_ref[0], panels[0][...])
    for d, panel in enumerate(panels[1:], 1):
        rest += dot(chosen_ref[d], panel[...])
    selected_ref[...] = partial_ref[...] + rest
    update = dot(turned_ref[...], rest.astype(jnp.bfloat16))
    if alone:
        update += update.T
    store_upper(update_ref, update, *early)


def products(partial, chosen, turned, panels, early):
    rows, width = panels[0].shape
    alone = len(panels) == 1
    return pl.pallas_call(
        functools.partial(product_kernel, len(panels), alone),
        out_shape=(
            jax.ShapeDtypeStruct((rows, width), jnp.float32),
            jax.ShapeDtypeStruct((width // 4, 5 * (width // 2)), jnp.float32),
        ),
        in_specs=[VMEM] * (3 + len(panels) + len(early)),
        out_specs=(VMEM, VMEM),
        compiler_params=PARAMS,
        name="products",
    )(partial, chosen, turned, *panels, *early)


def finish_kernel(diag_ref, *refs):
    updates, (out_hbm, out_ref, sems) = refs[:-3], refs[-3:]
    total = updates[0][...].astype(jnp.float32)
    for ref in updates[1:]:
        total += ref[...].astype(jnp.float32)
    quarter = total.shape[0]
    half = 2 * quarter
    tiles = [total[:, t * half:(t + 1) * half] for t in range(5)]
    rows = lax.broadcasted_iota(jnp.int32, (half, half), 0)
    columns = lax.broadcasted_iota(jnp.int32, (half, half), 1)
    mirrored = (rows >= quarter) & (columns < quarter)
    stores = [
        pltpu.make_async_copy(out_ref.at[h], out_hbm.at[0, pl.ds(h * half, half)], sems.at[h]) for h in range(2)
    ]

    def corner(top, bottom):
        block = jnp.concatenate([top, bottom], axis=0)
        return jnp.where(mirrored, block.T, block)

    side = jnp.concatenate([tiles[1], tiles[2]], axis=0)
    out_ref[0, :, :half] = diag_ref[0, :half, :half] + corner(tiles[0], tiles[4])
    out_ref[0, :, half:] = diag_ref[0, :half, half:] + side
    stores[0].start()
    out_ref[1, :, :half] = diag_ref[0, half:, :half] + side.T
    out_ref[1, :, half:] = diag_ref[0, half:, half:] + corner(tiles[3], pltpu.roll(tiles[4], quarter, 1))
    stores[1].start()
    for store in stores:
        store.wait()


def finish(diag_inverse, updates):
    width = diag_inverse.shape[1]
    return pl.pallas_call(
        finish_kernel,
        out_shape=jax.ShapeDtypeStruct(diag_inverse.shape, jnp.float32),
        in_specs=[VMEM] * (1 + len(updates)),
        out_specs=ANY,
        scratch_shapes=[pltpu.VMEM((2, width // 2, width), jnp.float32), pltpu.SemaphoreType.DMA((2,))],
        compiler_params=PARAMS,
        name="finish",
    )(diag_inverse, *updates)


def on_device(n, inverse_top, diag_inverse, cross_blocks, pattern):
    pairs = n // PAIR

    def from_pair(block, axis, shift, flip):
        moves = [
            (((m + shift) % pairs) * PAIR + (b ^ flip), m * PAIR + b) for m in range(pairs) for b in range(PAIR)
        ]
        return lax.ppermute(block, axis, moves)

    def across(block, shift, side):
        moves = [
            ((((m + shift) % pairs * PAIR + (b ^ 1)) * n + col), (m * PAIR + b) * n + col)
            for m in range(pairs)
            for b in range(PAIR)
            for col in range(side, n, PAIR)
        ]
        return lax.ppermute(block, ("prow", "pcol"), moves)

    def mate(block, axis):
        return from_pair(block, axis, 0, 1)

    near = [from_pair(inverse_top, "pcol", d, 0) for d in range(1, pairs)]
    factor_panel = build_panel(cross_blocks, diag_inverse, pattern)
    beside = mate(factor_panel, "prow")
    crossed = [from_pair(factor_panel, "prow", d, 1) for d in range(1, pairs)]
    turned, inverse_top = stage(factor_panel, inverse_top)
    near = [after(block, turned) for block in near]
    crossed = [after(block, near[0], cost=HOP_COST) for block in crossed]
    beside = after(beside, *crossed, cost=2 * HOP_COST)
    swapped = [mate(block, "prow") for block in crossed]

    tops = [inverse_top, mate(inverse_top, "pcol")]
    for block in near:
        tops += [block, mate(block, "pcol")]

    partial, early, again = partial_product(tops, [factor_panel, beside] + crossed, turned)
    chosen = choose(tops)
    again = after(again, swapped[-1], cost=HOP_COST)
    crossing = [after(across(early, d, 0), again, cost=0) for d in range(1, pairs)]
    crossing += [after(across(again, d, 1), crossing[0], cost=0) for d in range(1, pairs)]
    selected, late = products(partial, chosen, turned, swapped, [early])
    parts = [late] + crossing
    if pairs > 2:
        rest = (late - early.astype(jnp.float32)).astype(jnp.bfloat16)
        parts += [from_pair(rest, "prow", d, 0) for d in range(1, pairs)]
    update = functools.reduce(jnp.add, [part.astype(jnp.float32) for part in parts]).astype(jnp.bfloat16)
    return -selected, finish(diag_inverse, [update, mate(update, "prow")])


def solution(mesh):
    placed = (
        P(("pole", "prow"), "pcol"),
        P(("pole", "pcol"), None, None),
        P(("pole", "prow"), "pcol"),
        P("prow", "pcol"),
    )
    return jax.shard_map(
        functools.partial(on_device, mesh.shape["pcol"]),
        mesh=mesh,
        in_specs=placed,
        out_specs=(P(("pole", "prow"), "pcol"), P(("pole", "pcol"), None, None)),
        check_vma=False,
    )
```

```python
import functools
import jax
import jax.numpy as jnp
from jax import lax
from jax.experimental import pallas as pl
from jax.experimental.pallas import tpu as pltpu
from jax.sharding import PartitionSpec as P

PAIR = 2
HOP_COST = 10**10
VMEM_LIMIT = 40 * 1024 * 1024
PARAMS = pltpu.CompilerParams(vmem_limit_bytes=VMEM_LIMIT)
SMALL = pltpu.CompilerParams(vmem_limit_bytes=1024 * 1024)
VMEM = pl.BlockSpec(memory_space=pltpu.VMEM)
ANY = pl.BlockSpec(memory_space=pl.ANY)
HBM = pl.BlockSpec(memory_space=pltpu.HBM)


def split(value):
    high = value.astype(jnp.bfloat16)
    return high, (value - high.astype(jnp.float32)).astype(jnp.bfloat16)


def dot(left, right):
    return jnp.dot(left, right, preferred_element_type=jnp.float32)


def token_kernel(out_ref):
    out_ref[...] = jnp.zeros_like(out_ref)


def token():
    return pl.pallas_call(
        token_kernel,
        out_shape=jax.ShapeDtypeStruct((8, 128), jnp.float32),
        out_specs=VMEM,
        compiler_params=SMALL,
        cost_estimate=pl.CostEstimate(flops=HOP_COST, bytes_accessed=0, transcendentals=0),
        name="token",
    )()


def panel_kernel(pattern_hbm, cross_ref, diag_ref, token_ref, panel_ref, pattern_ref, sem):
    del token_ref
    width = diag_ref.shape[1]
    pattern_copy = pltpu.make_async_copy(pattern_hbm, pattern_ref, sem)
    pattern_copy.start()
    diag_high, diag_low = split(diag_ref[0])
    solved = []
    for a in range(pattern_hbm.shape[0]):
        high, low = split(cross_ref[pl.ds(a * width, width), :])
        solved.append(dot(high, diag_high) + (dot(high, diag_low) + dot(low, diag_high)))
    pattern_copy.wait()
    for a, block in enumerate(solved):
        kept = jnp.where(pattern_ref[a] != 0, block, 0.0)
        panel_ref[pl.ds(a * width, width), :] = kept.astype(jnp.bfloat16)


def build_panel(cross_blocks, diag_inverse, pattern):
    return pl.pallas_call(
        panel_kernel,
        out_shape=pltpu.VMEM(cross_blocks.shape, jnp.bfloat16),
        in_specs=[HBM, VMEM, VMEM, ANY],
        out_specs=VMEM,
        scratch_shapes=[pltpu.SMEM((pattern.size,), jnp.int32), pltpu.SemaphoreType.DMA],
        compiler_params=PARAMS,
        name="panel",
    )(
        pltpu.with_memory_space_constraint(pattern.reshape(-1), pltpu.HBM),
        cross_blocks,
        diag_inverse,
        token(),
    )


def relay_kernel(*refs):
    del refs


def after(block, *gates, cost=0):
    return pl.pallas_call(
        relay_kernel,
        out_shape=jax.ShapeDtypeStruct(block.shape, block.dtype),
        in_specs=[ANY] * (1 + len(gates)),
        out_specs=ANY,
        input_output_aliases={0: 0},
        compiler_params=SMALL,
        cost_estimate=pl.CostEstimate(flops=cost, bytes_accessed=cost // 256, transcendentals=0),
        name="relay",
    )(block, *gates)


def store_upper(out_ref, update, *others):
    half = update.shape[0] // 2
    quarter = half // 2
    left, right = update[:, :half], update[:, half:]
    lanes = lax.broadcasted_iota(jnp.int32, (quarter, half), 1)
    last = jnp.where(lanes < quarter, pltpu.roll(right[3 * quarter:], quarter, 1), left[quarter:half])
    tiles = [left[:quarter], right[:quarter], right[quarter:half], right[half:3 * quarter], last]
    for t, tile in enumerate(tiles):
        columns = pl.ds(t * half, half)
        for other in others:
            tile += other[:, columns].astype(jnp.float32)
        out_ref[:, columns] = tile.astype(out_ref.dtype)


def place_of(n, d, f):
    pairs = n // PAIR
    row, col = lax.axis_index("prow"), lax.axis_index("pcol")
    pair = (row // PAIR + d + pairs - col // PAIR) % pairs
    side = (row + f + col) % PAIR
    return pair * PAIR + side


def partial_kernel(n, *refs):
    tops, panels = refs[:n], refs[n:n + n // 2 + 1]
    turned_ref, partial_ref, update_ref, panel_buf = refs[n + n // 2 + 1:]

    def run(pairs):
        total = dot(*[ref[...] for ref in pairs[0]])
        for top, panel in pairs[1:]:
            total += dot(top[...], panel[...])
        partial_ref[...] = total
        store_upper(update_ref, dot(turned_ref[...], total.astype(jnp.bfloat16)))

    if n == 2 * PAIR:
        place = place_of(n, 0, 0)
        for own in range(n):
            pl.when(place == own)(functools.partial(run, list(zip([tops[own ^ s] for s in (0, 1, 3)], panels))))
        return
    pairs = n // PAIR
    held = [(0, 0)] + [(d, 1) for d in range(pairs)]
    for (d, f), panel in zip(held, panels):
        panel_buf[place_of(n, d, f)] = panel[...]
    for d in range(1, pairs):
        panel_buf[place_of(n, d, 0)] = jnp.zeros(panel_buf.shape[1:], panel_buf.dtype)
    run([(tops[t], panel_buf.at[t]) for t in range(n)])


def partial_product(tops, panels, turned):
    n = len(tops)
    rows, width = panels[0].shape
    return pl.pallas_call(
        functools.partial(partial_kernel, n),
        out_shape=(
            jax.ShapeDtypeStruct((rows, width), jnp.float32),
            jax.ShapeDtypeStruct((width // 4, 5 * (width // 2)), jnp.bfloat16),
        ),
        in_specs=[VMEM] * (n + len(panels) + 1),
        out_specs=(VMEM, VMEM),
        scratch_shapes=[pltpu.VMEM((n, rows, width), jnp.bfloat16)],
        compiler_params=PARAMS,
        cost_estimate=pl.CostEstimate(
            flops=2 * n * rows * rows * width, bytes_accessed=2 * n * rows * (rows + width), transcendentals=0
        ),
        name="partial",
    )(*tops, *panels, turned)


def stage_kernel(panel_ref, top_hbm, turned_ref, top_ref, sem):
    copy = pltpu.make_async_copy(top_hbm, top_ref, sem)
    copy.start()
    turned_ref[...] = panel_ref[...].astype(jnp.float32).T.astype(jnp.bfloat16)
    copy.wait()


def stage(panel, inverse_top):
    return pl.pallas_call(
        stage_kernel,
        out_shape=(pltpu.VMEM(panel.shape[::-1], panel.dtype), pltpu.VMEM(inverse_top.shape, inverse_top.dtype)),
        in_specs=[VMEM, HBM],
        out_specs=(VMEM, VMEM),
        scratch_shapes=[pltpu.SemaphoreType.DMA],
        compiler_params=PARAMS,
        name="stage",
    )(panel, pltpu.with_memory_space_constraint(inverse_top, pltpu.HBM))


def choose_kernel(n, *refs):
    tops, chosen_ref = refs[:n], refs[n]
    for d in range(1, n // PAIR):
        place = place_of(n, d, 0)
        for t in range(n):
            @pl.when(place == t)
            def _():
                chosen_ref[d - 1] = tops[t][...]


def choose(tops):
    n = len(tops)
    return pl.pallas_call(
        functools.partial(choose_kernel, n),
        out_shape=jax.ShapeDtypeStruct((n // 2 - 1,) + tops[0].shape, jnp.bfloat16),
        in_specs=[VMEM] * n,
        out_specs=VMEM,
        compiler_params=PARAMS,
        name="choose",
    )(*tops)


def product_kernel(count, alone, partial_ref, chosen_ref, turned_ref, *refs):
    panels, early, (selected_ref, update_ref) = refs[:count], refs[count:-2], refs[-2:]
    rest = dot(chosen_ref[0], panels[0][...])
    for d, panel in enumerate(panels[1:], 1):
        rest += dot(chosen_ref[d], panel[...])
    selected_ref[...] = partial_ref[...] + rest
    update = dot(turned_ref[...], rest.astype(jnp.bfloat16))
    if alone:
        update += update.T
    store_upper(update_ref, update, *early)


def products(partial, chosen, turned, panels, early):
    rows, width = panels[0].shape
    alone = len(panels) == 1
    return pl.pallas_call(
        functools.partial(product_kernel, len(panels), alone),
        out_shape=(
            jax.ShapeDtypeStruct((rows, width), jnp.float32),
            jax.ShapeDtypeStruct((width // 4, 5 * (width // 2)), jnp.float32),
        ),
        in_specs=[VMEM] * (3 + len(panels) + len(early)),
        out_specs=(VMEM, VMEM),
        compiler_params=PARAMS,
        name="products",
    )(partial, chosen, turned, *panels, *early)


def finish_kernel(diag_ref, *refs):
    updates, (out_hbm, out_ref, sems) = refs[:-3], refs[-3:]
    total = updates[0][...].astype(jnp.float32)
    for ref in updates[1:]:
        total += ref[...].astype(jnp.float32)
    quarter = total.shape[0]
    half = 2 * quarter
    tiles = [total[:, t * half:(t + 1) * half] for t in range(5)]
    rows = lax.broadcasted_iota(jnp.int32, (half, half), 0)
    columns = lax.broadcasted_iota(jnp.int32, (half, half), 1)
    mirrored = (rows >= quarter) & (columns < quarter)
    stores = [
        pltpu.make_async_copy(out_ref.at[h], out_hbm.at[0, pl.ds(h * half, half)], sems.at[h]) for h in range(2)
    ]

    def corner(top, bottom):
        block = jnp.concatenate([top, bottom], axis=0)
        return jnp.where(mirrored, block.T, block)

    side = jnp.concatenate([tiles[1], tiles[2]], axis=0)
    out_ref[0, :, :half] = diag_ref[0, :half, :half] + corner(tiles[0], tiles[4])
    out_ref[0, :, half:] = diag_ref[0, :half, half:] + side
    stores[0].start()
    out_ref[1, :, :half] = diag_ref[0, half:, :half] + side.T
    out_ref[1, :, half:] = diag_ref[0, half:, half:] + corner(tiles[3], pltpu.roll(tiles[4], quarter, 1))
    stores[1].start()
    for store in stores:
        store.wait()


def finish(diag_inverse, updates):
    width = diag_inverse.shape[1]
    return pl.pallas_call(
        finish_kernel,
        out_shape=jax.ShapeDtypeStruct(diag_inverse.shape, jnp.float32),
        in_specs=[VMEM] * (1 + len(updates)),
        out_specs=ANY,
        scratch_shapes=[pltpu.VMEM((2, width // 2, width), jnp.float32), pltpu.SemaphoreType.DMA((2,))],
        compiler_params=PARAMS,
        name="finish",
    )(diag_inverse, *updates)


def on_device(n, inverse_top, diag_inverse, cross_blocks, pattern):
    pairs = n // PAIR

    def from_pair(block, axis, shift, flip):
        moves = [
            (((m + shift) % pairs) * PAIR + (b ^ flip), m * PAIR + b) for m in range(pairs) for b in range(PAIR)
        ]
        return lax.ppermute(block, axis, moves)

    def mate(block, axis):
        return from_pair(block, axis, 0, 1)

    near = [from_pair(inverse_top, "pcol", d, 0) for d in range(1, pairs)]
    factor_panel = build_panel(cross_blocks, diag_inverse, pattern)
    beside = mate(factor_panel, "prow")
    crossed = [from_pair(factor_panel, "prow", d, 1) for d in range(1, pairs)]
    turned, inverse_top = stage(factor_panel, inverse_top)
    near = [after(block, turned) for block in near]
    crossed = [after(block, near[0], beside, cost=HOP_COST) for block in crossed]
    swapped = [mate(block, "prow") for block in crossed]

    tops = [inverse_top, mate(inverse_top, "pcol")]
    for block in near:
        tops += [block, mate(block, "pcol")]

    partial, early = partial_product(tops, [factor_panel, beside] + crossed, turned)
    chosen = choose(tops)
    crossing = [after(from_pair(early, "prow", d, 1), swapped[-1]) for d in range(1, pairs)]
    selected, late = products(partial, chosen, turned, swapped, [early])
    parts = [late] + crossing
    if pairs > 2:
        rest = (late - early.astype(jnp.float32)).astype(jnp.bfloat16)
        parts += [from_pair(rest, "prow", d, 0) for d in range(1, pairs)]
    update = functools.reduce(jnp.add, [part.astype(jnp.float32) for part in parts]).astype(jnp.bfloat16)
    return -selected, finish(diag_inverse, [update, mate(update, "prow")])


def solution(mesh):
    placed = (
        P(("pole", "prow"), "pcol"),
        P(("pole", "pcol"), None, None),
        P(("pole", "prow"), "pcol"),
        P("prow", "pcol"),
    )
    return jax.shard_map(
        functools.partial(on_device, mesh.shape["pcol"]),
        mesh=mesh,
        in_specs=placed,
        out_specs=(P(("pole", "prow"), "pcol"), P(("pole", "pcol"), None, None)),
        check_vma=False,
    )
```

```python
import functools
import jax
import jax.numpy as jnp
from jax import lax
from jax.experimental import pallas as pl
from jax.experimental.pallas import tpu as pltpu
from jax.sharding import PartitionSpec as P

PAIR = 2
HOP_COST = 10**10
VMEM_LIMIT = 40 * 1024 * 1024
PARAMS = pltpu.CompilerParams(vmem_limit_bytes=VMEM_LIMIT)
SMALL = pltpu.CompilerParams(vmem_limit_bytes=1024 * 1024)
VMEM = pl.BlockSpec(memory_space=pltpu.VMEM)
ANY = pl.BlockSpec(memory_space=pl.ANY)
HBM = pl.BlockSpec(memory_space=pltpu.HBM)


def split(value):
    high = value.astype(jnp.bfloat16)
    return high, (value - high.astype(jnp.float32)).astype(jnp.bfloat16)


def dot(left, right):
    return jnp.dot(left, right, preferred_element_type=jnp.float32)


def token_kernel(out_ref):
    out_ref[...] = jnp.zeros_like(out_ref)


def token():
    return pl.pallas_call(
        token_kernel,
        out_shape=jax.ShapeDtypeStruct((8, 128), jnp.float32),
        out_specs=VMEM,
        compiler_params=SMALL,
        cost_estimate=pl.CostEstimate(flops=HOP_COST, bytes_accessed=0, transcendentals=0),
        name="token",
    )()


def stage_work(panel_ref, top_hbm, turned_ref, top_ref, sem):
    copy = pltpu.make_async_copy(top_hbm, top_ref, sem)
    copy.start()
    turned_ref[...] = panel_ref[...].astype(jnp.float32).T.astype(jnp.bfloat16)
    copy.wait()


def on_side(side):
    return pl.when(lax.axis_index("pcol") % PAIR == side)


def stage_kernel(panel_ref, top_hbm, turned_in, top_in, turned_ref, top_ref, sem):
    del turned_in, top_in

    @on_side(0)
    def _():
        stage_work(panel_ref, top_hbm, turned_ref, top_ref, sem)


def stage(panel, inverse_top, turned, top):
    return pl.pallas_call(
        stage_kernel,
        out_shape=(pltpu.VMEM(turned.shape, turned.dtype), pltpu.VMEM(top.shape, top.dtype)),
        in_specs=[VMEM, HBM, VMEM, VMEM],
        out_specs=(VMEM, VMEM),
        input_output_aliases={2: 0, 3: 1},
        scratch_shapes=[pltpu.SemaphoreType.DMA],
        compiler_params=PARAMS,
        name="stage",
    )(panel, pltpu.with_memory_space_constraint(inverse_top, pltpu.HBM), turned, top)


def panel_kernel(
    pattern_hbm, cross_ref, diag_ref, top_hbm, token_ref, panel_ref, turned_ref, top_ref, pattern_ref, sem, top_sem
):
    del token_ref
    width = diag_ref.shape[1]
    pattern_copy = pltpu.make_async_copy(pattern_hbm, pattern_ref, sem)
    pattern_copy.start()
    diag_high, diag_low = split(diag_ref[0])
    solved = []
    for a in range(pattern_hbm.shape[0]):
        high, low = split(cross_ref[pl.ds(a * width, width), :])
        solved.append(dot(high, diag_high) + (dot(high, diag_low) + dot(low, diag_high)))
    pattern_copy.wait()
    for a, block in enumerate(solved):
        kept = jnp.where(pattern_ref[a] != 0, block, 0.0)
        panel_ref[pl.ds(a * width, width), :] = kept.astype(jnp.bfloat16)

    @on_side(1)
    def _():
        stage_work(panel_ref, top_hbm, turned_ref, top_ref, top_sem)


def build_panel(cross_blocks, diag_inverse, pattern, inverse_top):
    shape = cross_blocks.shape
    return pl.pallas_call(
        panel_kernel,
        out_shape=(
            pltpu.VMEM(shape, jnp.bfloat16),
            pltpu.VMEM(shape[::-1], jnp.bfloat16),
            pltpu.VMEM(inverse_top.shape, inverse_top.dtype),
        ),
        in_specs=[HBM, VMEM, VMEM, HBM, ANY],
        out_specs=(VMEM, VMEM, VMEM),
        scratch_shapes=[
            pltpu.SMEM((pattern.size,), jnp.int32),
            pltpu.SemaphoreType.DMA,
            pltpu.SemaphoreType.DMA,
        ],
        compiler_params=PARAMS,
        name="panel",
    )(
        pltpu.with_memory_space_constraint(pattern.reshape(-1), pltpu.HBM),
        cross_blocks,
        diag_inverse,
        pltpu.with_memory_space_constraint(inverse_top, pltpu.HBM),
        token(),
    )


def relay_kernel(*refs):
    del refs


def after(block, *gates, cost=0):
    return pl.pallas_call(
        relay_kernel,
        out_shape=jax.ShapeDtypeStruct(block.shape, block.dtype),
        in_specs=[ANY] * (1 + len(gates)),
        out_specs=ANY,
        input_output_aliases={0: 0},
        compiler_params=SMALL,
        cost_estimate=pl.CostEstimate(flops=cost, bytes_accessed=cost // 256, transcendentals=0),
        name="relay",
    )(block, *gates)


def store_upper(out_ref, update, *others):
    half = update.shape[0] // 2
    quarter = half // 2
    left, right = update[:, :half], update[:, half:]
    lanes = lax.broadcasted_iota(jnp.int32, (quarter, half), 1)
    last = jnp.where(lanes < quarter, pltpu.roll(right[3 * quarter:], quarter, 1), left[quarter:half])
    tiles = [left[:quarter], right[:quarter], right[quarter:half], right[half:3 * quarter], last]
    for t, tile in enumerate(tiles):
        columns = pl.ds(t * half, half)
        for other in others:
            tile += other[:, columns].astype(jnp.float32)
        out_ref[:, columns] = tile.astype(out_ref.dtype)


def place_of(n, d, f):
    pairs = n // PAIR
    row, col = lax.axis_index("prow"), lax.axis_index("pcol")
    pair = (row // PAIR + d + pairs - col // PAIR) % pairs
    side = (row + f + col) % PAIR
    return pair * PAIR + side


def partial_kernel(n, *refs):
    tops, panels = refs[:n], refs[n:n + n // 2 + 1]
    turned_ref, partial_ref, update_ref, panel_buf = refs[n + n // 2 + 1:]

    def run(pairs):
        total = dot(*[ref[...] for ref in pairs[0]])
        for top, panel in pairs[1:]:
            total += dot(top[...], panel[...])
        partial_ref[...] = total
        store_upper(update_ref, dot(turned_ref[...], total.astype(jnp.bfloat16)))

    if n == 2 * PAIR:
        place = place_of(n, 0, 0)
        for own in range(n):
            pl.when(place == own)(functools.partial(run, list(zip([tops[own ^ s] for s in (0, 1, 3)], panels))))
        return
    pairs = n // PAIR
    held = [(0, 0)] + [(d, 1) for d in range(pairs)]
    for (d, f), panel in zip(held, panels):
        panel_buf[place_of(n, d, f)] = panel[...]
    for d in range(1, pairs):
        panel_buf[place_of(n, d, 0)] = jnp.zeros(panel_buf.shape[1:], panel_buf.dtype)
    run([(tops[t], panel_buf.at[t]) for t in range(n)])


def partial_product(tops, panels, turned):
    n = len(tops)
    rows, width = panels[0].shape
    return pl.pallas_call(
        functools.partial(partial_kernel, n),
        out_shape=(
            jax.ShapeDtypeStruct((rows, width), jnp.float32),
            jax.ShapeDtypeStruct((width // 4, 5 * (width // 2)), jnp.bfloat16),
        ),
        in_specs=[VMEM] * (n + len(panels) + 1),
        out_specs=(VMEM, VMEM),
        scratch_shapes=[pltpu.VMEM((n, rows, width), jnp.bfloat16)],
        compiler_params=PARAMS,
        cost_estimate=pl.CostEstimate(
            flops=2 * n * rows * rows * width, bytes_accessed=2 * n * rows * (rows + width), transcendentals=0
        ),
        name="partial",
    )(*tops, *panels, turned)


def choose_kernel(n, *refs):
    tops, chosen_ref = refs[:n], refs[n]
    for d in range(1, n // PAIR):
        place = place_of(n, d, 0)
        for t in range(n):
            @pl.when(place == t)
            def _():
                chosen_ref[d - 1] = tops[t][...]


def choose(tops):
    n = len(tops)
    return pl.pallas_call(
        functools.partial(choose_kernel, n),
        out_shape=jax.ShapeDtypeStruct((n // 2 - 1,) + tops[0].shape, jnp.bfloat16),
        in_specs=[VMEM] * n,
        out_specs=VMEM,
        compiler_params=PARAMS,
        name="choose",
    )(*tops)


def product_kernel(count, alone, partial_ref, chosen_ref, turned_ref, *refs):
    panels, early, (selected_ref, update_ref) = refs[:count], refs[count:-2], refs[-2:]
    rest = dot(chosen_ref[0], panels[0][...])
    for d, panel in enumerate(panels[1:], 1):
        rest += dot(chosen_ref[d], panel[...])
    selected_ref[...] = partial_ref[...] + rest
    update = dot(turned_ref[...], rest.astype(jnp.bfloat16))
    if alone:
        update += update.T
    store_upper(update_ref, update, *early)


def products(partial, chosen, turned, panels, early):
    rows, width = panels[0].shape
    alone = len(panels) == 1
    return pl.pallas_call(
        functools.partial(product_kernel, len(panels), alone),
        out_shape=(
            jax.ShapeDtypeStruct((rows, width), jnp.float32),
            jax.ShapeDtypeStruct((width // 4, 5 * (width // 2)), jnp.float32),
        ),
        in_specs=[VMEM] * (3 + len(panels) + len(early)),
        out_specs=(VMEM, VMEM),
        compiler_params=PARAMS,
        name="products",
    )(partial, chosen, turned, *panels, *early)


def finish_kernel(diag_ref, *refs):
    updates, (out_hbm, out_ref, sems) = refs[:-3], refs[-3:]
    total = updates[0][...].astype(jnp.float32)
    for ref in updates[1:]:
        total += ref[...].astype(jnp.float32)
    quarter = total.shape[0]
    half = 2 * quarter
    tiles = [total[:, t * half:(t + 1) * half] for t in range(5)]
    rows = lax.broadcasted_iota(jnp.int32, (half, half), 0)
    columns = lax.broadcasted_iota(jnp.int32, (half, half), 1)
    mirrored = (rows >= quarter) & (columns < quarter)
    stores = [
        pltpu.make_async_copy(out_ref.at[h], out_hbm.at[0, pl.ds(h * half, half)], sems.at[h]) for h in range(2)
    ]

    def corner(top, bottom):
        block = jnp.concatenate([top, bottom], axis=0)
        return jnp.where(mirrored, block.T, block)

    side = jnp.concatenate([tiles[1], tiles[2]], axis=0)
    out_ref[0, :, :half] = diag_ref[0, :half, :half] + corner(tiles[0], tiles[4])
    out_ref[0, :, half:] = diag_ref[0, :half, half:] + side
    stores[0].start()
    out_ref[1, :, :half] = diag_ref[0, half:, :half] + side.T
    out_ref[1, :, half:] = diag_ref[0, half:, half:] + corner(tiles[3], pltpu.roll(tiles[4], quarter, 1))
    stores[1].start()
    for store in stores:
        store.wait()


def finish(diag_inverse, updates):
    width = diag_inverse.shape[1]
    return pl.pallas_call(
        finish_kernel,
        out_shape=jax.ShapeDtypeStruct(diag_inverse.shape, jnp.float32),
        in_specs=[VMEM] * (1 + len(updates)),
        out_specs=ANY,
        scratch_shapes=[pltpu.VMEM((2, width // 2, width), jnp.float32), pltpu.SemaphoreType.DMA((2,))],
        compiler_params=PARAMS,
        name="finish",
    )(diag_inverse, *updates)


def on_device(n, inverse_top, diag_inverse, cross_blocks, pattern):
    pairs = n // PAIR

    def from_pair(block, axis, shift, flip):
        moves = [
            (((m + shift) % pairs) * PAIR + (b ^ flip), m * PAIR + b) for m in range(pairs) for b in range(PAIR)
        ]
        return lax.ppermute(block, axis, moves)

    def mate(block, axis):
        return from_pair(block, axis, 0, 1)

    near = [from_pair(inverse_top, "pcol", d, 0) for d in range(1, pairs)]
    factor_panel, turned, top = build_panel(cross_blocks, diag_inverse, pattern, inverse_top)
    beside = mate(factor_panel, "prow")
    crossed = [from_pair(factor_panel, "prow", d, 1) for d in range(1, pairs)]
    turned, inverse_top = stage(factor_panel, inverse_top, turned, top)
    near = [after(block, turned) for block in near]
    crossed = [after(block, near[0], beside, cost=HOP_COST) for block in crossed]
    swapped = [mate(block, "prow") for block in crossed]

    tops = [inverse_top, mate(inverse_top, "pcol")]
    for block in near:
        tops += [block, mate(block, "pcol")]

    partial, early = partial_product(tops, [factor_panel, beside] + crossed, turned)
    chosen = choose(tops)
    crossing = [after(from_pair(early, "prow", d, 1), swapped[-1]) for d in range(1, pairs)]
    selected, late = products(partial, chosen, turned, swapped, [early])
    parts = [late] + crossing
    if pairs > 2:
        rest = (late - early.astype(jnp.float32)).astype(jnp.bfloat16)
        parts += [from_pair(rest, "prow", d, 0) for d in range(1, pairs)]
    update = functools.reduce(jnp.add, [part.astype(jnp.float32) for part in parts]).astype(jnp.bfloat16)
    return -selected, finish(diag_inverse, [update, mate(update, "prow")])


def solution(mesh):
    placed = (
        P(("pole", "prow"), "pcol"),
        P(("pole", "pcol"), None, None),
        P(("pole", "prow"), "pcol"),
        P("prow", "pcol"),
    )
    return jax.shard_map(
        functools.partial(on_device, mesh.shape["pcol"]),
        mesh=mesh,
        in_specs=placed,
        out_specs=(P(("pole", "prow"), "pcol"), P(("pole", "pcol"), None, None)),
        check_vma=False,
    )
```

```python
import functools
import jax
import jax.numpy as jnp
from jax import lax
from jax.experimental import pallas as pl
from jax.experimental.pallas import tpu as pltpu
from jax.sharding import PartitionSpec as P

PAIR = 2
HOP_COST = 10**10
VMEM_LIMIT = 40 * 1024 * 1024
PARAMS = pltpu.CompilerParams(vmem_limit_bytes=VMEM_LIMIT)
SMALL = pltpu.CompilerParams(vmem_limit_bytes=1024 * 1024)
VMEM = pl.BlockSpec(memory_space=pltpu.VMEM)
ANY = pl.BlockSpec(memory_space=pl.ANY)
HBM = pl.BlockSpec(memory_space=pltpu.HBM)


def split(value):
    high = value.astype(jnp.bfloat16)
    return high, (value - high.astype(jnp.float32)).astype(jnp.bfloat16)


def dot(left, right):
    return jnp.dot(left, right, preferred_element_type=jnp.float32)


def token_kernel(out_ref):
    out_ref[...] = jnp.zeros_like(out_ref)


def token():
    return pl.pallas_call(
        token_kernel,
        out_shape=jax.ShapeDtypeStruct((8, 128), jnp.float32),
        out_specs=VMEM,
        compiler_params=SMALL,
        cost_estimate=pl.CostEstimate(flops=HOP_COST, bytes_accessed=0, transcendentals=0),
        name="token",
    )()


def panel_kernel(pattern_hbm, cross_ref, diag_ref, token_ref, panel_ref, pattern_ref, sem):
    del token_ref
    width = diag_ref.shape[1]
    pattern_copy = pltpu.make_async_copy(pattern_hbm, pattern_ref, sem)
    pattern_copy.start()
    diag_high, diag_low = split(diag_ref[0])
    solved = []
    for a in range(pattern_hbm.shape[0]):
        high, low = split(cross_ref[pl.ds(a * width, width), :])
        solved.append(dot(high, diag_high) + (dot(high, diag_low) + dot(low, diag_high)))
    pattern_copy.wait()
    for a, block in enumerate(solved):
        kept = jnp.where(pattern_ref[a] != 0, block, 0.0)
        panel_ref[pl.ds(a * width, width), :] = kept.astype(jnp.bfloat16)


def build_panel(cross_blocks, diag_inverse, pattern):
    return pl.pallas_call(
        panel_kernel,
        out_shape=pltpu.VMEM(cross_blocks.shape, jnp.bfloat16),
        in_specs=[HBM, VMEM, VMEM, ANY],
        out_specs=VMEM,
        scratch_shapes=[pltpu.SMEM((pattern.size,), jnp.int32), pltpu.SemaphoreType.DMA],
        compiler_params=PARAMS,
        name="panel",
    )(
        pltpu.with_memory_space_constraint(pattern.reshape(-1), pltpu.HBM),
        cross_blocks,
        diag_inverse,
        token(),
    )


def relay_kernel(*refs):
    del refs


def after(block, *gates, cost=0):
    return pl.pallas_call(
        relay_kernel,
        out_shape=jax.ShapeDtypeStruct(block.shape, block.dtype),
        in_specs=[ANY] * (1 + len(gates)),
        out_specs=ANY,
        input_output_aliases={0: 0},
        compiler_params=SMALL,
        cost_estimate=pl.CostEstimate(flops=cost, bytes_accessed=cost // 256, transcendentals=0),
        name="relay",
    )(block, *gates)


def store_upper(out_ref, update, *others):
    half = update.shape[0] // 2
    quarter = half // 2
    left, right = update[:, :half], update[:, half:]
    lanes = lax.broadcasted_iota(jnp.int32, (quarter, half), 1)
    last = jnp.where(lanes < quarter, pltpu.roll(right[3 * quarter:], quarter, 1), left[quarter:half])
    tiles = [left[:quarter], right[:quarter], right[quarter:half], right[half:3 * quarter], last]
    for t, tile in enumerate(tiles):
        columns = pl.ds(t * half, half)
        for other in others:
            tile += other[:, columns].astype(jnp.float32)
        out_ref[:, columns] = tile.astype(out_ref.dtype)


def place_of(n, d, f):
    pairs = n // PAIR
    row, col = lax.axis_index("prow"), lax.axis_index("pcol")
    pair = (row // PAIR + d + pairs - col // PAIR) % pairs
    side = (row + f + col) % PAIR
    return pair * PAIR + side


def partial_kernel(n, *refs):
    tops, panels = refs[:n], refs[n:n + n // 2 + 1]
    turned_ref, partial_ref, update_ref, panel_buf = refs[n + n // 2 + 1:]

    def run(pairs):
        total = dot(*[ref[...] for ref in pairs[0]])
        for top, panel in pairs[1:]:
            total += dot(top[...], panel[...])
        partial_ref[...] = total
        store_upper(update_ref, dot(turned_ref[...], total.astype(jnp.bfloat16)))

    if n == 2 * PAIR:
        place = place_of(n, 0, 0)
        for own in range(n):
            pl.when(place == own)(functools.partial(run, list(zip([tops[own ^ s] for s in (0, 1, 3)], panels))))
        return
    pairs = n // PAIR
    held = [(0, 0)] + [(d, 1) for d in range(pairs)]
    for (d, f), panel in zip(held, panels):
        panel_buf[place_of(n, d, f)] = panel[...]
    for d in range(1, pairs):
        panel_buf[place_of(n, d, 0)] = jnp.zeros(panel_buf.shape[1:], panel_buf.dtype)
    run([(tops[t], panel_buf.at[t]) for t in range(n)])


def partial_product(tops, panels, turned):
    n = len(tops)
    rows, width = panels[0].shape
    return pl.pallas_call(
        functools.partial(partial_kernel, n),
        out_shape=(
            jax.ShapeDtypeStruct((rows, width), jnp.float32),
            jax.ShapeDtypeStruct((width // 4, 5 * (width // 2)), jnp.bfloat16),
        ),
        in_specs=[VMEM] * (n + len(panels) + 1),
        out_specs=(VMEM, VMEM),
        scratch_shapes=[pltpu.VMEM((n, rows, width), jnp.bfloat16)],
        compiler_params=PARAMS,
        cost_estimate=pl.CostEstimate(
            flops=2 * n * rows * rows * width, bytes_accessed=2 * n * rows * (rows + width), transcendentals=0
        ),
        name="partial",
    )(*tops, *panels, turned)


def stage_kernel(panel_ref, top_hbm, turned_ref, top_ref, sem):
    copy = pltpu.make_async_copy(top_hbm, top_ref, sem)
    copy.start()
    turned_ref[...] = panel_ref[...].astype(jnp.float32).T.astype(jnp.bfloat16)
    copy.wait()


def stage(panel, inverse_top):
    return pl.pallas_call(
        stage_kernel,
        out_shape=(pltpu.VMEM(panel.shape[::-1], panel.dtype), pltpu.VMEM(inverse_top.shape, inverse_top.dtype)),
        in_specs=[VMEM, HBM],
        out_specs=(VMEM, VMEM),
        scratch_shapes=[pltpu.SemaphoreType.DMA],
        compiler_params=PARAMS,
        name="stage",
    )(panel, pltpu.with_memory_space_constraint(inverse_top, pltpu.HBM))


def choose_kernel(n, *refs):
    tops, chosen_ref = refs[:n], refs[n]
    for d in range(1, n // PAIR):
        place = place_of(n, d, 0)
        for t in range(n):
            @pl.when(place == t)
            def _():
                chosen_ref[d - 1] = tops[t][...]


def choose(tops):
    n = len(tops)
    return pl.pallas_call(
        functools.partial(choose_kernel, n),
        out_shape=jax.ShapeDtypeStruct((n // 2 - 1,) + tops[0].shape, jnp.bfloat16),
        in_specs=[VMEM] * n,
        out_specs=VMEM,
        compiler_params=PARAMS,
        name="choose",
    )(*tops)


def product_kernel(count, alone, chosen_ref, turned_ref, *refs):
    panels, early, (rest_ref, update_ref) = refs[:count], refs[count:-2], refs[-2:]
    rest = dot(chosen_ref[0], panels[0][...])
    for d, panel in enumerate(panels[1:], 1):
        rest += dot(chosen_ref[d], panel[...])
    rest_ref[...] = rest
    update = dot(turned_ref[...], rest.astype(jnp.bfloat16))
    if alone:
        update += update.T
    store_upper(update_ref, update, *early)


def products(chosen, turned, panels, early):
    rows, width = panels[0].shape
    alone = len(panels) == 1
    return pl.pallas_call(
        functools.partial(product_kernel, len(panels), alone),
        out_shape=(
            jax.ShapeDtypeStruct((rows, width), jnp.float32),
            jax.ShapeDtypeStruct((width // 4, 5 * (width // 2)), jnp.float32),
        ),
        in_specs=[VMEM] * (2 + len(panels) + len(early)),
        out_specs=(VMEM, VMEM),
        compiler_params=PARAMS,
        name="products",
    )(chosen, turned, *panels, *early)


def finish_kernel(diag_ref, *refs):
    updates, (out_hbm, out_ref, sems) = refs[:-3], refs[-3:]
    total = updates[0][...].astype(jnp.float32)
    for ref in updates[1:]:
        total += ref[...].astype(jnp.float32)
    quarter = total.shape[0]
    half = 2 * quarter
    tiles = [total[:, t * half:(t + 1) * half] for t in range(5)]
    rows = lax.broadcasted_iota(jnp.int32, (half, half), 0)
    columns = lax.broadcasted_iota(jnp.int32, (half, half), 1)
    mirrored = (rows >= quarter) & (columns < quarter)
    stores = [
        pltpu.make_async_copy(out_ref.at[h], out_hbm.at[0, pl.ds(h * half, half)], sems.at[h]) for h in range(2)
    ]

    def corner(top, bottom):
        block = jnp.concatenate([top, bottom], axis=0)
        return jnp.where(mirrored, block.T, block)

    side = jnp.concatenate([tiles[1], tiles[2]], axis=0)
    out_ref[0, :, :half] = diag_ref[0, :half, :half] + corner(tiles[0], tiles[4])
    out_ref[0, :, half:] = diag_ref[0, :half, half:] + side
    stores[0].start()
    out_ref[1, :, :half] = diag_ref[0, half:, :half] + side.T
    out_ref[1, :, half:] = diag_ref[0, half:, half:] + corner(tiles[3], pltpu.roll(tiles[4], quarter, 1))
    stores[1].start()
    for store in stores:
        store.wait()


def finish(diag_inverse, updates):
    width = diag_inverse.shape[1]
    return pl.pallas_call(
        finish_kernel,
        out_shape=jax.ShapeDtypeStruct(diag_inverse.shape, jnp.float32),
        in_specs=[VMEM] * (1 + len(updates)),
        out_specs=ANY,
        scratch_shapes=[pltpu.VMEM((2, width // 2, width), jnp.float32), pltpu.SemaphoreType.DMA((2,))],
        compiler_params=PARAMS,
        name="finish",
    )(diag_inverse, *updates)


def on_device(n, inverse_top, diag_inverse, cross_blocks, pattern):
    pairs = n // PAIR

    def from_pair(block, axis, shift, flip):
        moves = [
            (((m + shift) % pairs) * PAIR + (b ^ flip), m * PAIR + b) for m in range(pairs) for b in range(PAIR)
        ]
        return lax.ppermute(block, axis, moves)

    def mate(block, axis):
        return from_pair(block, axis, 0, 1)

    near = [from_pair(inverse_top, "pcol", d, 0) for d in range(1, pairs)]
    factor_panel = build_panel(cross_blocks, diag_inverse, pattern)
    beside = mate(factor_panel, "prow")
    crossed = [from_pair(factor_panel, "prow", d, 1) for d in range(1, pairs)]
    turned, inverse_top = stage(factor_panel, inverse_top)
    near = [after(block, turned) for block in near]
    crossed = [after(block, near[0], beside, cost=HOP_COST) for block in crossed]
    swapped = [mate(block, "prow") for block in crossed]

    tops = [inverse_top, mate(inverse_top, "pcol")]
    for block in near:
        tops += [block, mate(block, "pcol")]

    partial, early = partial_product(tops, [factor_panel, beside] + crossed, turned)
    chosen = choose(tops)
    crossing = [after(from_pair(early, "prow", d, 0), swapped[-1]) for d in range(1, pairs)]
    rest, late = products(chosen, turned, swapped, [early])
    parts = [late] + crossing
    if pairs > 2:
        share = (late - early.astype(jnp.float32)).astype(jnp.bfloat16)
        parts += [from_pair(share, "prow", d, 0) for d in range(1, pairs)]
    update = functools.reduce(jnp.add, [part.astype(jnp.float32) for part in parts]).astype(jnp.bfloat16)
    return -(partial + rest), finish(diag_inverse, [update, mate(update, "prow")])


def solution(mesh):
    placed = (
        P(("pole", "prow"), "pcol"),
        P(("pole", "pcol"), None, None),
        P(("pole", "prow"), "pcol"),
        P("prow", "pcol"),
    )
    return jax.shard_map(
        functools.partial(on_device, mesh.shape["pcol"]),
        mesh=mesh,
        in_specs=placed,
        out_specs=(P(("pole", "prow"), "pcol"), P(("pole", "pcol"), None, None)),
        check_vma=False,
    )
```

```python
import functools
import jax
import jax.numpy as jnp
from jax import lax
from jax.experimental import pallas as pl
from jax.experimental.pallas import tpu as pltpu
from jax.sharding import PartitionSpec as P

PAIR = 2
HOP_COST = 10**10
VMEM_LIMIT = 40 * 1024 * 1024
PARAMS = pltpu.CompilerParams(vmem_limit_bytes=VMEM_LIMIT)
SMALL = pltpu.CompilerParams(vmem_limit_bytes=1024 * 1024)
VMEM = pl.BlockSpec(memory_space=pltpu.VMEM)
ANY = pl.BlockSpec(memory_space=pl.ANY)
HBM = pl.BlockSpec(memory_space=pltpu.HBM)


def split(value):
    high = value.astype(jnp.bfloat16)
    return high, (value - high.astype(jnp.float32)).astype(jnp.bfloat16)


def dot(left, right):
    return jnp.dot(left, right, preferred_element_type=jnp.float32)


def token_kernel(out_ref):
    out_ref[...] = jnp.zeros_like(out_ref)


def token():
    return pl.pallas_call(
        token_kernel,
        out_shape=jax.ShapeDtypeStruct((8, 128), jnp.float32),
        out_specs=VMEM,
        compiler_params=SMALL,
        cost_estimate=pl.CostEstimate(flops=HOP_COST, bytes_accessed=0, transcendentals=0),
        name="token",
    )()


def panel_kernel(pattern_hbm, cross_ref, diag_ref, token_ref, panel_ref, pattern_ref, sem):
    del token_ref
    width = diag_ref.shape[1]
    pattern_copy = pltpu.make_async_copy(pattern_hbm, pattern_ref, sem)
    pattern_copy.start()
    diag_high, diag_low = split(diag_ref[0])
    solved = []
    for a in range(pattern_hbm.shape[0]):
        high, low = split(cross_ref[pl.ds(a * width, width), :])
        solved.append(dot(high, diag_high) + (dot(high, diag_low) + dot(low, diag_high)))
    pattern_copy.wait()
    for a, block in enumerate(solved):
        kept = jnp.where(pattern_ref[a] != 0, block, 0.0)
        panel_ref[pl.ds(a * width, width), :] = kept.astype(jnp.bfloat16)


def build_panel(cross_blocks, diag_inverse, pattern):
    return pl.pallas_call(
        panel_kernel,
        out_shape=pltpu.VMEM(cross_blocks.shape, jnp.bfloat16),
        in_specs=[HBM, VMEM, VMEM, ANY],
        out_specs=VMEM,
        scratch_shapes=[pltpu.SMEM((pattern.size,), jnp.int32), pltpu.SemaphoreType.DMA],
        compiler_params=PARAMS,
        name="panel",
    )(
        pltpu.with_memory_space_constraint(pattern.reshape(-1), pltpu.HBM),
        cross_blocks,
        diag_inverse,
        token(),
    )


def relay_kernel(*refs):
    del refs


def after(block, *gates, cost=0):
    return pl.pallas_call(
        relay_kernel,
        out_shape=jax.ShapeDtypeStruct(block.shape, block.dtype),
        in_specs=[ANY] * (1 + len(gates)),
        out_specs=ANY,
        input_output_aliases={0: 0},
        compiler_params=SMALL,
        cost_estimate=pl.CostEstimate(flops=cost, bytes_accessed=cost // 256, transcendentals=0),
        name="relay",
    )(block, *gates)


def store_upper(out_ref, update, *others):
    half = update.shape[0] // 2
    quarter = half // 2
    left, right = update[:, :half], update[:, half:]
    lanes = lax.broadcasted_iota(jnp.int32, (quarter, half), 1)
    last = jnp.where(lanes < quarter, pltpu.roll(right[3 * quarter:], quarter, 1), left[quarter:half])
    tiles = [left[:quarter], right[:quarter], right[quarter:half], right[half:3 * quarter], last]
    for t, tile in enumerate(tiles):
        columns = pl.ds(t * half, half)
        for other in others:
            tile += other[:, columns].astype(jnp.float32)
        out_ref[:, columns] = tile.astype(out_ref.dtype)


def place_of(n, d, f):
    pairs = n // PAIR
    row, col = lax.axis_index("prow"), lax.axis_index("pcol")
    pair = (row // PAIR + d + pairs - col // PAIR) % pairs
    side = (row + f + col) % PAIR
    return pair * PAIR + side


def partial_kernel(n, *refs):
    tops, panels = refs[:n], refs[n:n + n // 2 + 1]
    turned_ref, partial_ref, update_ref, panel_buf = refs[n + n // 2 + 1:]

    def run(pairs):
        total = dot(*[ref[...] for ref in pairs[0]])
        for top, panel in pairs[1:]:
            total += dot(top[...], panel[...])
        partial_ref[...] = total
        store_upper(update_ref, dot(turned_ref[...], total.astype(jnp.bfloat16)))

    if n == 2 * PAIR:
        place = place_of(n, 0, 0)
        for own in range(n):
            pl.when(place == own)(functools.partial(run, list(zip([tops[own ^ s] for s in (0, 1, 3)], panels))))
        return
    pairs = n // PAIR
    held = [(0, 0)] + [(d, 1) for d in range(pairs)]
    for (d, f), panel in zip(held, panels):
        panel_buf[place_of(n, d, f)] = panel[...]
    for d in range(1, pairs):
        panel_buf[place_of(n, d, 0)] = jnp.zeros(panel_buf.shape[1:], panel_buf.dtype)
    run([(tops[t], panel_buf.at[t]) for t in range(n)])


def partial_product(tops, panels, turned):
    n = len(tops)
    rows, width = panels[0].shape
    return pl.pallas_call(
        functools.partial(partial_kernel, n),
        out_shape=(
            jax.ShapeDtypeStruct((rows, width), jnp.float32),
            jax.ShapeDtypeStruct((width // 4, 5 * (width // 2)), jnp.bfloat16),
        ),
        in_specs=[VMEM] * (n + len(panels) + 1),
        out_specs=(VMEM, VMEM),
        scratch_shapes=[pltpu.VMEM((n, rows, width), jnp.bfloat16)],
        compiler_params=PARAMS,
        cost_estimate=pl.CostEstimate(
            flops=2 * n * rows * rows * width, bytes_accessed=2 * n * rows * (rows + width), transcendentals=0
        ),
        name="partial",
    )(*tops, *panels, turned)


def stage_kernel(panel_ref, top_hbm, turned_ref, top_ref, sem):
    copy = pltpu.make_async_copy(top_hbm, top_ref, sem)
    copy.start()
    turned_ref[...] = panel_ref[...].astype(jnp.float32).T.astype(jnp.bfloat16)
    copy.wait()


def stage(panel, inverse_top):
    return pl.pallas_call(
        stage_kernel,
        out_shape=(pltpu.VMEM(panel.shape[::-1], panel.dtype), pltpu.VMEM(inverse_top.shape, inverse_top.dtype)),
        in_specs=[VMEM, HBM],
        out_specs=(VMEM, VMEM),
        scratch_shapes=[pltpu.SemaphoreType.DMA],
        compiler_params=PARAMS,
        name="stage",
    )(panel, pltpu.with_memory_space_constraint(inverse_top, pltpu.HBM))


def choose_kernel(n, *refs):
    tops, chosen_ref = refs[:n], refs[n]
    for d in range(1, n // PAIR):
        place = place_of(n, d, 0)
        for t in range(n):
            @pl.when(place == t)
            def _():
                chosen_ref[d - 1] = tops[t][...]


def choose(tops):
    n = len(tops)
    return pl.pallas_call(
        functools.partial(choose_kernel, n),
        out_shape=jax.ShapeDtypeStruct((n // 2 - 1,) + tops[0].shape, jnp.bfloat16),
        in_specs=[VMEM] * n,
        out_specs=VMEM,
        compiler_params=PARAMS,
        name="choose",
    )(*tops)


def last_terms(chosen_ref, panels):
    total = dot(chosen_ref[0], panels[0][...])
    for d, panel in enumerate(panels[1:], 1):
        total += dot(chosen_ref[d], panel[...])
    return total


def late_kernel(chosen_ref, turned_ref, early_ref, *refs):
    panels, update_ref = refs[:-1], refs[-1]
    update = dot(turned_ref[...], last_terms(chosen_ref, panels).astype(jnp.bfloat16))
    if len(panels) == 1:
        update += update.T
    store_upper(update_ref, update, early_ref)


def late_share(chosen, turned, panels, early):
    return pl.pallas_call(
        late_kernel,
        out_shape=jax.ShapeDtypeStruct(early.shape, jnp.float32),
        in_specs=[VMEM] * (3 + len(panels)),
        out_specs=VMEM,
        compiler_params=PARAMS,
        name="late",
    )(chosen, turned, early, *panels)


def cross_kernel(partial_ref, chosen_ref, *refs):
    refs[-1][...] = -(partial_ref[...] + last_terms(chosen_ref, refs[:-1]))


def cross_result(partial, chosen, panels):
    rows, width = partial.shape
    return pl.pallas_call(
        cross_kernel,
        out_shape=jax.ShapeDtypeStruct(partial.shape, jnp.float32),
        in_specs=[VMEM] * (2 + len(panels)),
        out_specs=VMEM,
        compiler_params=PARAMS,
        cost_estimate=pl.CostEstimate(
            flops=2 * len(panels) * rows * rows * width, bytes_accessed=8 * rows * width, transcendentals=0
        ),
        name="cross",
    )(partial, chosen, *panels)


def finish_kernel(diag_ref, *refs):
    updates, (out_hbm, out_ref, sems) = refs[:-3], refs[-3:]
    total = updates[0][...].astype(jnp.float32)
    for ref in updates[1:]:
        total += ref[...].astype(jnp.float32)
    quarter = total.shape[0]
    half = 2 * quarter
    tiles = [total[:, t * half:(t + 1) * half] for t in range(5)]
    rows = lax.broadcasted_iota(jnp.int32, (half, half), 0)
    columns = lax.broadcasted_iota(jnp.int32, (half, half), 1)
    mirrored = (rows >= quarter) & (columns < quarter)
    stores = [
        pltpu.make_async_copy(out_ref.at[h], out_hbm.at[0, pl.ds(h * half, half)], sems.at[h]) for h in range(2)
    ]

    def corner(top, bottom):
        block = jnp.concatenate([top, bottom], axis=0)
        return jnp.where(mirrored, block.T, block)

    side = jnp.concatenate([tiles[1], tiles[2]], axis=0)
    out_ref[0, :, :half] = diag_ref[0, :half, :half] + corner(tiles[0], tiles[4])
    out_ref[0, :, half:] = diag_ref[0, :half, half:] + side
    stores[0].start()
    out_ref[1, :, :half] = diag_ref[0, half:, :half] + side.T
    out_ref[1, :, half:] = diag_ref[0, half:, half:] + corner(tiles[3], pltpu.roll(tiles[4], quarter, 1))
    stores[1].start()
    for store in stores:
        store.wait()


def finish(diag_inverse, updates):
    width = diag_inverse.shape[1]
    return pl.pallas_call(
        finish_kernel,
        out_shape=jax.ShapeDtypeStruct(diag_inverse.shape, jnp.float32),
        in_specs=[VMEM] * (1 + len(updates)),
        out_specs=ANY,
        scratch_shapes=[pltpu.VMEM((2, width // 2, width), jnp.float32), pltpu.SemaphoreType.DMA((2,))],
        compiler_params=PARAMS,
        name="finish",
    )(diag_inverse, *updates)


def on_device(n, inverse_top, diag_inverse, cross_blocks, pattern):
    pairs = n // PAIR

    def from_pair(block, axis, shift, flip):
        moves = [
            (((m + shift) % pairs) * PAIR + (b ^ flip), m * PAIR + b) for m in range(pairs) for b in range(PAIR)
        ]
        return lax.ppermute(block, axis, moves)

    def mate(block, axis):
        return from_pair(block, axis, 0, 1)

    near = [from_pair(inverse_top, "pcol", d, 0) for d in range(1, pairs)]
    factor_panel = build_panel(cross_blocks, diag_inverse, pattern)
    beside = mate(factor_panel, "prow")
    crossed = [from_pair(factor_panel, "prow", d, 1) for d in range(1, pairs)]
    turned, inverse_top = stage(factor_panel, inverse_top)
    near = [after(block, turned) for block in near]
    crossed = [after(block, near[0], beside, cost=HOP_COST) for block in crossed]
    swapped = [mate(block, "prow") for block in crossed]

    tops = [inverse_top, mate(inverse_top, "pcol")]
    for block in near:
        tops += [block, mate(block, "pcol")]

    partial, early = partial_product(tops, [factor_panel, beside] + crossed, turned)
    chosen = choose(tops)
    crossing = [after(from_pair(early, "prow", d, 1), swapped[-1]) for d in range(1, pairs)]
    late = late_share(chosen, turned, swapped, early)
    parts = [late] + crossing
    if pairs > 2:
        rest = (late - early.astype(jnp.float32)).astype(jnp.bfloat16)
        parts += [from_pair(rest, "prow", d, 0) for d in range(1, pairs)]
    update = functools.reduce(jnp.add, [part.astype(jnp.float32) for part in parts]).astype(jnp.bfloat16)
    return cross_result(partial, chosen, swapped), finish(diag_inverse, [update, mate(update, "prow")])


def solution(mesh):
    placed = (
        P(("pole", "prow"), "pcol"),
        P(("pole", "pcol"), None, None),
        P(("pole", "prow"), "pcol"),
        P("prow", "pcol"),
    )
    return jax.shard_map(
        functools.partial(on_device, mesh.shape["pcol"]),
        mesh=mesh,
        in_specs=placed,
        out_specs=(P(("pole", "prow"), "pcol"), P(("pole", "pcol"), None, None)),
        check_vma=False,
    )
```

```python
import functools
import jax
import jax.numpy as jnp
from jax import lax
from jax.experimental import pallas as pl
from jax.experimental.pallas import tpu as pltpu
from jax.sharding import PartitionSpec as P

PAIR = 2
HOP_COST = 10**10
VMEM_LIMIT = 40 * 1024 * 1024
PARAMS = pltpu.CompilerParams(vmem_limit_bytes=VMEM_LIMIT)
SMALL = pltpu.CompilerParams(vmem_limit_bytes=1024 * 1024)
VMEM = pl.BlockSpec(memory_space=pltpu.VMEM)
ANY = pl.BlockSpec(memory_space=pl.ANY)
HBM = pl.BlockSpec(memory_space=pltpu.HBM)


def split(value):
    high = value.astype(jnp.bfloat16)
    return high, (value - high.astype(jnp.float32)).astype(jnp.bfloat16)


def dot(left, right):
    return jnp.dot(left, right, preferred_element_type=jnp.float32)


def token_kernel(out_ref):
    out_ref[...] = jnp.zeros_like(out_ref)


def token():
    return pl.pallas_call(
        token_kernel,
        out_shape=jax.ShapeDtypeStruct((8, 128), jnp.float32),
        out_specs=VMEM,
        compiler_params=SMALL,
        cost_estimate=pl.CostEstimate(flops=HOP_COST, bytes_accessed=0, transcendentals=0),
        name="token",
    )()


def panel_kernel(pattern_hbm, cross_ref, diag_ref, token_ref, panel_ref, pattern_ref, sem):
    del token_ref
    width = diag_ref.shape[1]
    pattern_copy = pltpu.make_async_copy(pattern_hbm, pattern_ref, sem)
    pattern_copy.start()
    diag_high, diag_low = split(diag_ref[0])
    solved = []
    for a in range(pattern_hbm.shape[0]):
        high, low = split(cross_ref[pl.ds(a * width, width), :])
        solved.append(dot(high, diag_high) + (dot(high, diag_low) + dot(low, diag_high)))
    pattern_copy.wait()
    for a, block in enumerate(solved):
        kept = jnp.where(pattern_ref[a] != 0, block, 0.0)
        panel_ref[pl.ds(a * width, width), :] = kept.astype(jnp.bfloat16)


def build_panel(cross_blocks, diag_inverse, pattern):
    return pl.pallas_call(
        panel_kernel,
        out_shape=pltpu.VMEM(cross_blocks.shape, jnp.bfloat16),
        in_specs=[HBM, VMEM, VMEM, ANY],
        out_specs=VMEM,
        scratch_shapes=[pltpu.SMEM((pattern.size,), jnp.int32), pltpu.SemaphoreType.DMA],
        compiler_params=PARAMS,
        name="panel",
    )(
        pltpu.with_memory_space_constraint(pattern.reshape(-1), pltpu.HBM),
        cross_blocks,
        diag_inverse,
        token(),
    )


def relay_kernel(*refs):
    del refs


def after(block, *gates, cost=0):
    return pl.pallas_call(
        relay_kernel,
        out_shape=jax.ShapeDtypeStruct(block.shape, block.dtype),
        in_specs=[ANY] * (1 + len(gates)),
        out_specs=ANY,
        input_output_aliases={0: 0},
        compiler_params=SMALL,
        cost_estimate=pl.CostEstimate(flops=cost, bytes_accessed=cost // 256, transcendentals=0),
        name="relay",
    )(block, *gates)


def store_upper(out_ref, update, *others):
    half = update.shape[0] // 2
    quarter = half // 2
    left, right = update[:, :half], update[:, half:]
    lanes = lax.broadcasted_iota(jnp.int32, (quarter, half), 1)
    last = jnp.where(lanes < quarter, pltpu.roll(right[3 * quarter:], quarter, 1), left[quarter:half])
    tiles = [left[:quarter], right[:quarter], right[quarter:half], right[half:3 * quarter], last]
    for t, tile in enumerate(tiles):
        columns = pl.ds(t * half, half)
        for other in others:
            tile += other[:, columns].astype(jnp.float32)
        out_ref[:, columns] = tile.astype(out_ref.dtype)


def place_of(n, d, f):
    pairs = n // PAIR
    row, col = lax.axis_index("prow"), lax.axis_index("pcol")
    pair = (row // PAIR + d + pairs - col // PAIR) % pairs
    side = (row + f + col) % PAIR
    return pair * PAIR + side


def matched(n, tops, panels, panel_buf, run):
    if n == 2 * PAIR:
        place = place_of(n, 0, 0)
        for own in range(n):
            pl.when(place == own)(functools.partial(run, list(zip([tops[own ^ s] for s in (0, 1, 3)], panels))))
        return
    pairs = n // PAIR
    held = [(0, 0)] + [(d, 1) for d in range(pairs)]
    for (d, f), panel in zip(held, panels):
        panel_buf[place_of(n, d, f)] = panel[...]
    for d in range(1, pairs):
        panel_buf[place_of(n, d, 0)] = jnp.zeros(panel_buf.shape[1:], panel_buf.dtype)
    run([(tops[t], panel_buf.at[t]) for t in range(n)])


def product(pairs):
    total = dot(*[ref[...] for ref in pairs[0]])
    for top, panel in pairs[1:]:
        total += dot(top[...], panel[...])
    return total


def early_kernel(n, *refs):
    tops, panels = refs[:n], refs[n:n + n // 2 + 1]
    turned_ref, update_ref, panel_buf = refs[n + n // 2 + 1:]

    def run(pairs):
        store_upper(update_ref, dot(turned_ref[...], product(pairs).astype(jnp.bfloat16)))

    matched(n, tops, panels, panel_buf, run)


def early_share(tops, panels, turned):
    n = len(tops)
    rows, width = panels[0].shape
    return pl.pallas_call(
        functools.partial(early_kernel, n),
        out_shape=jax.ShapeDtypeStruct((width // 4, 5 * (width // 2)), jnp.bfloat16),
        in_specs=[VMEM] * (n + len(panels) + 1),
        out_specs=VMEM,
        scratch_shapes=[pltpu.VMEM((n, rows, width), jnp.bfloat16)],
        compiler_params=PARAMS,
        cost_estimate=pl.CostEstimate(
            flops=2 * n * rows * rows * width, bytes_accessed=2 * n * rows * (rows + width), transcendentals=0
        ),
        name="early",
    )(*tops, *panels, turned)


def stage_kernel(panel_ref, top_hbm, turned_ref, top_ref, sem):
    copy = pltpu.make_async_copy(top_hbm, top_ref, sem)
    copy.start()
    turned_ref[...] = panel_ref[...].astype(jnp.float32).T.astype(jnp.bfloat16)
    copy.wait()


def stage(panel, inverse_top):
    return pl.pallas_call(
        stage_kernel,
        out_shape=(pltpu.VMEM(panel.shape[::-1], panel.dtype), pltpu.VMEM(inverse_top.shape, inverse_top.dtype)),
        in_specs=[VMEM, HBM],
        out_specs=(VMEM, VMEM),
        scratch_shapes=[pltpu.SemaphoreType.DMA],
        compiler_params=PARAMS,
        name="stage",
    )(panel, pltpu.with_memory_space_constraint(inverse_top, pltpu.HBM))


def choose_kernel(n, *refs):
    tops, chosen_ref = refs[:n], refs[n]
    for d in range(1, n // PAIR):
        place = place_of(n, d, 0)
        for t in range(n):
            @pl.when(place == t)
            def _():
                chosen_ref[d - 1] = tops[t][...]


def choose(tops):
    n = len(tops)
    return pl.pallas_call(
        functools.partial(choose_kernel, n),
        out_shape=jax.ShapeDtypeStruct((n // 2 - 1,) + tops[0].shape, jnp.bfloat16),
        in_specs=[VMEM] * n,
        out_specs=VMEM,
        compiler_params=PARAMS,
        name="choose",
    )(*tops)


def last_terms(chosen_ref, panels):
    total = dot(chosen_ref[0], panels[0][...])
    for d, panel in enumerate(panels[1:], 1):
        total += dot(chosen_ref[d], panel[...])
    return total


def late_kernel(chosen_ref, turned_ref, early_ref, *refs):
    panels, update_ref = refs[:-1], refs[-1]
    update = dot(turned_ref[...], last_terms(chosen_ref, panels).astype(jnp.bfloat16))
    if len(panels) == 1:
        update += update.T
    store_upper(update_ref, update, early_ref)


def late_share(chosen, turned, panels, early):
    return pl.pallas_call(
        late_kernel,
        out_shape=jax.ShapeDtypeStruct(early.shape, jnp.float32),
        in_specs=[VMEM] * (3 + len(panels)),
        out_specs=VMEM,
        compiler_params=PARAMS,
        name="late",
    )(chosen, turned, early, *panels)


def cross_kernel(n, *refs):
    tops, panels = refs[:n], refs[n:n + n // 2 + 1]
    chosen_ref, *swapped, out_ref, panel_buf = refs[n + n // 2 + 1:]

    def run(pairs):
        out_ref[...] = -(product(pairs) + last_terms(chosen_ref, swapped))

    matched(n, tops, panels, panel_buf, run)


def cross_result(tops, panels, chosen, swapped):
    n = len(tops)
    rows, width = panels[0].shape
    return pl.pallas_call(
        functools.partial(cross_kernel, n),
        out_shape=jax.ShapeDtypeStruct((rows, width), jnp.float32),
        in_specs=[VMEM] * (n + len(panels) + 1 + len(swapped)),
        out_specs=VMEM,
        scratch_shapes=[pltpu.VMEM((n, rows, width), jnp.bfloat16)],
        compiler_params=PARAMS,
        cost_estimate=pl.CostEstimate(
            flops=2 * n * rows * rows * width, bytes_accessed=4 * rows * width, transcendentals=0
        ),
        name="cross",
    )(*tops, *panels, chosen, *swapped)


def finish_kernel(diag_ref, *refs):
    updates, (out_hbm, out_ref, sems) = refs[:-3], refs[-3:]
    total = updates[0][...].astype(jnp.float32)
    for ref in updates[1:]:
        total += ref[...].astype(jnp.float32)
    quarter = total.shape[0]
    half = 2 * quarter
    tiles = [total[:, t * half:(t + 1) * half] for t in range(5)]
    rows = lax.broadcasted_iota(jnp.int32, (half, half), 0)
    columns = lax.broadcasted_iota(jnp.int32, (half, half), 1)
    mirrored = (rows >= quarter) & (columns < quarter)
    stores = [
        pltpu.make_async_copy(out_ref.at[h], out_hbm.at[0, pl.ds(h * half, half)], sems.at[h]) for h in range(2)
    ]

    def corner(top, bottom):
        block = jnp.concatenate([top, bottom], axis=0)
        return jnp.where(mirrored, block.T, block)

    side = jnp.concatenate([tiles[1], tiles[2]], axis=0)
    out_ref[0, :, :half] = diag_ref[0, :half, :half] + corner(tiles[0], tiles[4])
    out_ref[0, :, half:] = diag_ref[0, :half, half:] + side
    stores[0].start()
    out_ref[1, :, :half] = diag_ref[0, half:, :half] + side.T
    out_ref[1, :, half:] = diag_ref[0, half:, half:] + corner(tiles[3], pltpu.roll(tiles[4], quarter, 1))
    stores[1].start()
    for store in stores:
        store.wait()


def finish(diag_inverse, updates):
    width = diag_inverse.shape[1]
    return pl.pallas_call(
        finish_kernel,
        out_shape=jax.ShapeDtypeStruct(diag_inverse.shape, jnp.float32),
        in_specs=[VMEM] * (1 + len(updates)),
        out_specs=ANY,
        scratch_shapes=[pltpu.VMEM((2, width // 2, width), jnp.float32), pltpu.SemaphoreType.DMA((2,))],
        compiler_params=PARAMS,
        name="finish",
    )(diag_inverse, *updates)


def on_device(n, inverse_top, diag_inverse, cross_blocks, pattern):
    pairs = n // PAIR

    def from_pair(block, axis, shift, flip):
        moves = [
            (((m + shift) % pairs) * PAIR + (b ^ flip), m * PAIR + b) for m in range(pairs) for b in range(PAIR)
        ]
        return lax.ppermute(block, axis, moves)

    def mate(block, axis):
        return from_pair(block, axis, 0, 1)

    near = [from_pair(inverse_top, "pcol", d, 0) for d in range(1, pairs)]
    factor_panel = build_panel(cross_blocks, diag_inverse, pattern)
    beside = mate(factor_panel, "prow")
    crossed = [from_pair(factor_panel, "prow", d, 1) for d in range(1, pairs)]
    turned, inverse_top = stage(factor_panel, inverse_top)
    near = [after(block, turned) for block in near]
    crossed = [after(block, near[0], beside, cost=HOP_COST) for block in crossed]
    swapped = [mate(block, "prow") for block in crossed]

    tops = [inverse_top, mate(inverse_top, "pcol")]
    for block in near:
        tops += [block, mate(block, "pcol")]

    panels = [factor_panel, beside] + crossed
    early = early_share(tops, panels, turned)
    chosen = choose(tops)
    crossing = [after(from_pair(early, "prow", d, 1), swapped[-1]) for d in range(1, pairs)]
    late = late_share(chosen, turned, swapped, early)
    parts = [late] + crossing
    if pairs > 2:
        rest = (late - early.astype(jnp.float32)).astype(jnp.bfloat16)
        parts += [from_pair(rest, "prow", d, 0) for d in range(1, pairs)]
    update = functools.reduce(jnp.add, [part.astype(jnp.float32) for part in parts]).astype(jnp.bfloat16)
    return cross_result(tops, panels, chosen, swapped), finish(diag_inverse, [update, mate(update, "prow")])


def solution(mesh):
    placed = (
        P(("pole", "prow"), "pcol"),
        P(("pole", "pcol"), None, None),
        P(("pole", "prow"), "pcol"),
        P("prow", "pcol"),
    )
    return jax.shard_map(
        functools.partial(on_device, mesh.shape["pcol"]),
        mesh=mesh,
        in_specs=placed,
        out_specs=(P(("pole", "prow"), "pcol"), P(("pole", "pcol"), None, None)),
        check_vma=False,
    )
```

```python
import functools
import jax
import jax.numpy as jnp
from jax import lax
from jax.experimental import pallas as pl
from jax.experimental.pallas import tpu as pltpu
from jax.sharding import PartitionSpec as P

PAIR = 2
HOP_COST = 10**10
VMEM_LIMIT = 40 * 1024 * 1024
PARAMS = pltpu.CompilerParams(vmem_limit_bytes=VMEM_LIMIT)
SMALL = pltpu.CompilerParams(vmem_limit_bytes=1024 * 1024)
VMEM = pl.BlockSpec(memory_space=pltpu.VMEM)
ANY = pl.BlockSpec(memory_space=pl.ANY)
HBM = pl.BlockSpec(memory_space=pltpu.HBM)


def split(value):
    high = value.astype(jnp.bfloat16)
    return high, (value - high.astype(jnp.float32)).astype(jnp.bfloat16)


def dot(left, right):
    return jnp.dot(left, right, preferred_element_type=jnp.float32)


def token_kernel(out_ref):
    out_ref[...] = jnp.zeros_like(out_ref)


def token():
    return pl.pallas_call(
        token_kernel,
        out_shape=jax.ShapeDtypeStruct((8, 128), jnp.float32),
        out_specs=VMEM,
        compiler_params=SMALL,
        cost_estimate=pl.CostEstimate(flops=HOP_COST, bytes_accessed=0, transcendentals=0),
        name="token",
    )()


def panel_kernel(pattern_hbm, cross_ref, diag_ref, token_ref, panel_ref, pattern_ref, sem):
    del token_ref
    width = diag_ref.shape[1]
    pattern_copy = pltpu.make_async_copy(pattern_hbm, pattern_ref, sem)
    pattern_copy.start()
    diag_high, diag_low = split(diag_ref[0])
    solved = []
    for a in range(pattern_hbm.shape[0]):
        high, low = split(cross_ref[pl.ds(a * width, width), :])
        solved.append(dot(high, diag_high) + (dot(high, diag_low) + dot(low, diag_high)))
    pattern_copy.wait()
    for a, block in enumerate(solved):
        kept = jnp.where(pattern_ref[a] != 0, block, 0.0)
        panel_ref[pl.ds(a * width, width), :] = kept.astype(jnp.bfloat16)


def build_panel(cross_blocks, diag_inverse, pattern):
    return pl.pallas_call(
        panel_kernel,
        out_shape=pltpu.VMEM(cross_blocks.shape, jnp.bfloat16),
        in_specs=[HBM, VMEM, VMEM, ANY],
        out_specs=VMEM,
        scratch_shapes=[pltpu.SMEM((pattern.size,), jnp.int32), pltpu.SemaphoreType.DMA],
        compiler_params=PARAMS,
        name="panel",
    )(
        pltpu.with_memory_space_constraint(pattern.reshape(-1), pltpu.HBM),
        cross_blocks,
        diag_inverse,
        token(),
    )


def relay_kernel(*refs):
    del refs


def after(block, *gates, cost=0):
    return pl.pallas_call(
        relay_kernel,
        out_shape=jax.ShapeDtypeStruct(block.shape, block.dtype),
        in_specs=[ANY] * (1 + len(gates)),
        out_specs=ANY,
        input_output_aliases={0: 0},
        compiler_params=SMALL,
        cost_estimate=pl.CostEstimate(flops=cost, bytes_accessed=cost // 256, transcendentals=0),
        name="relay",
    )(block, *gates)


def store_upper(out_ref, update, *others):
    half = update.shape[0] // 2
    quarter = half // 2
    left, right = update[:, :half], update[:, half:]
    lanes = lax.broadcasted_iota(jnp.int32, (quarter, half), 1)
    last = jnp.where(lanes < quarter, pltpu.roll(right[3 * quarter:], quarter, 1), left[quarter:half])
    tiles = [left[:quarter], right[:quarter], right[quarter:half], right[half:3 * quarter], last]
    for t, tile in enumerate(tiles):
        columns = pl.ds(t * half, half)
        for other in others:
            tile += other[:, columns].astype(jnp.float32)
        out_ref[:, columns] = tile.astype(out_ref.dtype)


def place_of(n, d, f):
    pairs = n // PAIR
    row, col = lax.axis_index("prow"), lax.axis_index("pcol")
    pair = (row // PAIR + d + pairs - col // PAIR) % pairs
    side = (row + f + col) % PAIR
    return pair * PAIR + side


def partial_kernel(n, *refs):
    tops, panels = refs[:n], refs[n:n + n // 2 + 1]
    turned_ref, partial_ref, update_ref, panel_buf = refs[n + n // 2 + 1:]

    def run(pairs):
        total = dot(*[ref[...] for ref in pairs[0]])
        for top, panel in pairs[1:]:
            total += dot(top[...], panel[...])
        partial_ref[...] = total
        store_upper(update_ref, dot(turned_ref[...], total.astype(jnp.bfloat16)))

    if n == 2 * PAIR:
        place = place_of(n, 0, 0)
        for own in range(n):
            pl.when(place == own)(functools.partial(run, list(zip([tops[own ^ s] for s in (0, 1, 3)], panels))))
        return
    pairs = n // PAIR
    held = [(0, 0)] + [(d, 1) for d in range(pairs)]
    for (d, f), panel in zip(held, panels):
        panel_buf[place_of(n, d, f)] = panel[...]
    for d in range(1, pairs):
        panel_buf[place_of(n, d, 0)] = jnp.zeros(panel_buf.shape[1:], panel_buf.dtype)
    run([(tops[t], panel_buf.at[t]) for t in range(n)])


def partial_product(tops, panels, turned):
    n = len(tops)
    rows, width = panels[0].shape
    return pl.pallas_call(
        functools.partial(partial_kernel, n),
        out_shape=(
            jax.ShapeDtypeStruct((rows, width), jnp.float32),
            jax.ShapeDtypeStruct((width // 4, 5 * (width // 2)), jnp.bfloat16),
        ),
        in_specs=[VMEM] * (n + len(panels) + 1),
        out_specs=(VMEM, VMEM),
        scratch_shapes=[pltpu.VMEM((n, rows, width), jnp.bfloat16)],
        compiler_params=PARAMS,
        cost_estimate=pl.CostEstimate(
            flops=2 * n * rows * rows * width, bytes_accessed=2 * n * rows * (rows + width), transcendentals=0
        ),
        name="partial",
    )(*tops, *panels, turned)


def stage_kernel(panel_ref, top_hbm, turned_ref, top_ref, sem):
    copy = pltpu.make_async_copy(top_hbm, top_ref, sem)
    copy.start()
    turned_ref[...] = panel_ref[...].astype(jnp.float32).T.astype(jnp.bfloat16)
    copy.wait()


def stage(panel, inverse_top):
    return pl.pallas_call(
        stage_kernel,
        out_shape=(pltpu.VMEM(panel.shape[::-1], panel.dtype), pltpu.VMEM(inverse_top.shape, inverse_top.dtype)),
        in_specs=[VMEM, HBM],
        out_specs=(VMEM, VMEM),
        scratch_shapes=[pltpu.SemaphoreType.DMA],
        compiler_params=PARAMS,
        name="stage",
    )(panel, pltpu.with_memory_space_constraint(inverse_top, pltpu.HBM))


def choose_kernel(n, *refs):
    tops, chosen_ref = refs[:n], refs[n]
    for d in range(1, n // PAIR):
        place = place_of(n, d, 0)
        for t in range(n):
            @pl.when(place == t)
            def _():
                chosen_ref[d - 1] = tops[t][...]


def choose(tops):
    n = len(tops)
    return pl.pallas_call(
        functools.partial(choose_kernel, n),
        out_shape=jax.ShapeDtypeStruct((n // 2 - 1,) + tops[0].shape, jnp.bfloat16),
        in_specs=[VMEM] * n,
        out_specs=VMEM,
        compiler_params=PARAMS,
        name="choose",
    )(*tops)


def last_terms(chosen_ref, panels):
    total = dot(chosen_ref[0], panels[0][...])
    for d, panel in enumerate(panels[1:], 1):
        total += dot(chosen_ref[d], panel[...])
    return total


def late_kernel(chosen_ref, turned_ref, early_ref, *refs):
    panels, update_ref = refs[:-1], refs[-1]
    update = dot(turned_ref[...], last_terms(chosen_ref, panels).astype(jnp.bfloat16))
    if len(panels) == 1:
        update += update.T
    store_upper(update_ref, update, early_ref)


def late_share(chosen, turned, panels, early):
    return pl.pallas_call(
        late_kernel,
        out_shape=jax.ShapeDtypeStruct(early.shape, jnp.float32),
        in_specs=[VMEM] * (3 + len(panels)),
        out_specs=VMEM,
        compiler_params=PARAMS,
        name="late",
    )(chosen, turned, early, *panels)


def cross_kernel(partial_ref, chosen_ref, *refs):
    refs[-1][...] = -(partial_ref[...] + last_terms(chosen_ref, refs[:-1]))


def cross_result(partial, chosen, panels):
    rows, width = partial.shape
    return pl.pallas_call(
        cross_kernel,
        out_shape=jax.ShapeDtypeStruct(partial.shape, jnp.float32),
        in_specs=[VMEM] * (2 + len(panels)),
        out_specs=VMEM,
        compiler_params=PARAMS,
        cost_estimate=pl.CostEstimate(
            flops=2 * len(panels) * rows * rows * width, bytes_accessed=8 * rows * width, transcendentals=0
        ),
        name="cross",
    )(partial, chosen, *panels)


def finish_kernel(diag_ref, *refs):
    updates, (out_hbm, out_ref, sems) = refs[:-3], refs[-3:]
    total = updates[0][...].astype(jnp.float32)
    for ref in updates[1:]:
        total += ref[...].astype(jnp.float32)
    quarter = total.shape[0]
    half = 2 * quarter
    tiles = [total[:, t * half:(t + 1) * half] for t in range(5)]
    rows = lax.broadcasted_iota(jnp.int32, (half, half), 0)
    columns = lax.broadcasted_iota(jnp.int32, (half, half), 1)
    mirrored = (rows >= quarter) & (columns < quarter)
    stores = [
        pltpu.make_async_copy(out_ref.at[h], out_hbm.at[0, pl.ds(h * half, half)], sems.at[h]) for h in range(2)
    ]

    def corner(top, bottom):
        block = jnp.concatenate([top, bottom], axis=0)
        return jnp.where(mirrored, block.T, block)

    side = jnp.concatenate([tiles[1], tiles[2]], axis=0)
    out_ref[0, :, :half] = diag_ref[0, :half, :half] + corner(tiles[0], tiles[4])
    out_ref[0, :, half:] = diag_ref[0, :half, half:] + side
    stores[0].start()
    out_ref[1, :, :half] = diag_ref[0, half:, :half] + side.T
    out_ref[1, :, half:] = diag_ref[0, half:, half:] + corner(tiles[3], pltpu.roll(tiles[4], quarter, 1))
    stores[1].start()
    for store in stores:
        store.wait()


def finish(diag_inverse, updates):
    width = diag_inverse.shape[1]
    return pl.pallas_call(
        finish_kernel,
        out_shape=jax.ShapeDtypeStruct(diag_inverse.shape, jnp.float32),
        in_specs=[VMEM] * (1 + len(updates)),
        out_specs=ANY,
        scratch_shapes=[pltpu.VMEM((2, width // 2, width), jnp.float32), pltpu.SemaphoreType.DMA((2,))],
        compiler_params=PARAMS,
        name="finish",
    )(diag_inverse, *updates)


def on_device(n, inverse_top, diag_inverse, cross_blocks, pattern):
    pairs = n // PAIR

    def from_pair(block, axis, shift, flip):
        moves = [
            (((m + shift) % pairs) * PAIR + (b ^ flip), m * PAIR + b) for m in range(pairs) for b in range(PAIR)
        ]
        return lax.ppermute(block, axis, moves)

    def mate(block, axis):
        return from_pair(block, axis, 0, 1)

    near = [from_pair(inverse_top, "pcol", d, 0) for d in range(1, pairs)]
    factor_panel = build_panel(cross_blocks, diag_inverse, pattern)
    beside = mate(factor_panel, "prow")
    crossed = [from_pair(factor_panel, "prow", d, 1) for d in range(1, pairs)]
    turned, inverse_top = stage(factor_panel, inverse_top)
    near = [after(block, turned) for block in near]
    beside = after(beside, factor_panel, cost=HOP_COST // 2)
    crossed = [after(block, near[0], beside, cost=HOP_COST) for block in crossed]
    swapped = [mate(block, "prow") for block in crossed]

    tops = [inverse_top, mate(inverse_top, "pcol")]
    for block in near:
        tops += [block, mate(block, "pcol")]

    partial, early = partial_product(tops, [factor_panel, beside] + crossed, turned)
    chosen = choose(tops)
    crossing = [after(from_pair(early, "prow", d, 1), swapped[-1]) for d in range(1, pairs)]
    late = late_share(chosen, turned, swapped, early)
    parts = [late] + crossing
    if pairs > 2:
        rest = (late - early.astype(jnp.float32)).astype(jnp.bfloat16)
        parts += [from_pair(rest, "prow", d, 0) for d in range(1, pairs)]
    update = functools.reduce(jnp.add, [part.astype(jnp.float32) for part in parts]).astype(jnp.bfloat16)
    return cross_result(partial, chosen, swapped), finish(diag_inverse, [update, mate(update, "prow")])


def solution(mesh):
    placed = (
        P(("pole", "prow"), "pcol"),
        P(("pole", "pcol"), None, None),
        P(("pole", "prow"), "pcol"),
        P("prow", "pcol"),
    )
    return jax.shard_map(
        functools.partial(on_device, mesh.shape["pcol"]),
        mesh=mesh,
        in_specs=placed,
        out_specs=(P(("pole", "prow"), "pcol"), P(("pole", "pcol"), None, None)),
        check_vma=False,
    )
```

```python
import functools
import jax
import jax.numpy as jnp
from jax import lax
from jax.experimental import pallas as pl
from jax.experimental.pallas import tpu as pltpu
from jax.sharding import PartitionSpec as P

PAIR = 2
HOP_COST = 10**10
VMEM_LIMIT = 40 * 1024 * 1024
PARAMS = pltpu.CompilerParams(vmem_limit_bytes=VMEM_LIMIT)
SMALL = pltpu.CompilerParams(vmem_limit_bytes=1024 * 1024)
VMEM = pl.BlockSpec(memory_space=pltpu.VMEM)
ANY = pl.BlockSpec(memory_space=pl.ANY)
HBM = pl.BlockSpec(memory_space=pltpu.HBM)


def split(value):
    high = value.astype(jnp.bfloat16)
    return high, (value - high.astype(jnp.float32)).astype(jnp.bfloat16)


def dot(left, right):
    return jnp.dot(left, right, preferred_element_type=jnp.float32)


def token_kernel(out_ref):
    out_ref[...] = jnp.zeros_like(out_ref)


def token():
    return pl.pallas_call(
        token_kernel,
        out_shape=jax.ShapeDtypeStruct((8, 128), jnp.float32),
        out_specs=VMEM,
        compiler_params=SMALL,
        cost_estimate=pl.CostEstimate(flops=HOP_COST, bytes_accessed=0, transcendentals=0),
        name="token",
    )()


def panel_kernel(pattern_hbm, cross_ref, diag_ref, token_ref, panel_ref, pattern_ref, sem):
    del token_ref
    width = diag_ref.shape[1]
    pattern_copy = pltpu.make_async_copy(pattern_hbm, pattern_ref, sem)
    pattern_copy.start()
    diag_high, diag_low = split(diag_ref[0])
    solved = []
    for a in range(pattern_hbm.shape[0]):
        high, low = split(cross_ref[pl.ds(a * width, width), :])
        solved.append(dot(high, diag_high) + (dot(high, diag_low) + dot(low, diag_high)))
    pattern_copy.wait()
    for a, block in enumerate(solved):
        kept = jnp.where(pattern_ref[a] != 0, block, 0.0)
        panel_ref[pl.ds(a * width, width), :] = kept.astype(jnp.bfloat16)


def build_panel(cross_blocks, diag_inverse, pattern):
    return pl.pallas_call(
        panel_kernel,
        out_shape=pltpu.VMEM(cross_blocks.shape, jnp.bfloat16),
        in_specs=[HBM, VMEM, VMEM, ANY],
        out_specs=VMEM,
        scratch_shapes=[pltpu.SMEM((pattern.size,), jnp.int32), pltpu.SemaphoreType.DMA],
        compiler_params=PARAMS,
        name="panel",
    )(
        pltpu.with_memory_space_constraint(pattern.reshape(-1), pltpu.HBM),
        cross_blocks,
        diag_inverse,
        token(),
    )


def relay_kernel(*refs):
    del refs


def after(block, *gates, cost=0):
    return pl.pallas_call(
        relay_kernel,
        out_shape=jax.ShapeDtypeStruct(block.shape, block.dtype),
        in_specs=[ANY] * (1 + len(gates)),
        out_specs=ANY,
        input_output_aliases={0: 0},
        compiler_params=SMALL,
        cost_estimate=pl.CostEstimate(flops=cost, bytes_accessed=cost // 256, transcendentals=0),
        name="relay",
    )(block, *gates)


def store_upper(out_ref, update, *others):
    half = update.shape[0] // 2
    quarter = half // 2
    left, right = update[:, :half], update[:, half:]
    lanes = lax.broadcasted_iota(jnp.int32, (quarter, half), 1)
    last = jnp.where(lanes < quarter, pltpu.roll(right[3 * quarter:], quarter, 1), left[quarter:half])
    tiles = [left[:quarter], right[:quarter], right[quarter:half], right[half:3 * quarter], last]
    for t, tile in enumerate(tiles):
        columns = pl.ds(t * half, half)
        for other in others:
            tile += other[:, columns].astype(jnp.float32)
        out_ref[:, columns] = tile.astype(out_ref.dtype)


def place_of(n, d, f):
    pairs = n // PAIR
    row, col = lax.axis_index("prow"), lax.axis_index("pcol")
    pair = (row // PAIR + d + pairs - col // PAIR) % pairs
    side = (row + f + col) % PAIR
    return pair * PAIR + side


def partial_kernel(n, *refs):
    tops, panels = refs[:n], refs[n:n + n // 2 + 1]
    turned_ref, partial_ref, update_ref, panel_buf = refs[n + n // 2 + 1:]

    def run(pairs):
        total = dot(*[ref[...] for ref in pairs[0]])
        for top, panel in pairs[1:]:
            total += dot(top[...], panel[...])
        partial_ref[...] = total
        store_upper(update_ref, dot(turned_ref[...], total.astype(jnp.bfloat16)))

    if n == 2 * PAIR:
        place = place_of(n, 0, 0)
        for own in range(n):
            pl.when(place == own)(functools.partial(run, list(zip([tops[own ^ s] for s in (0, 1, 3)], panels))))
        return
    pairs = n // PAIR
    held = [(0, 0)] + [(d, 1) for d in range(pairs)]
    for (d, f), panel in zip(held, panels):
        panel_buf[place_of(n, d, f)] = panel[...]
    for d in range(1, pairs):
        panel_buf[place_of(n, d, 0)] = jnp.zeros(panel_buf.shape[1:], panel_buf.dtype)
    run([(tops[t], panel_buf.at[t]) for t in range(n)])


def partial_product(tops, panels, turned):
    n = len(tops)
    rows, width = panels[0].shape
    return pl.pallas_call(
        functools.partial(partial_kernel, n),
        out_shape=(
            jax.ShapeDtypeStruct((rows, width), jnp.float32),
            jax.ShapeDtypeStruct((width // 4, 5 * (width // 2)), jnp.bfloat16),
        ),
        in_specs=[VMEM] * (n + len(panels) + 1),
        out_specs=(VMEM, VMEM),
        scratch_shapes=[pltpu.VMEM((n, rows, width), jnp.bfloat16)],
        compiler_params=PARAMS,
        cost_estimate=pl.CostEstimate(
            flops=2 * n * rows * rows * width, bytes_accessed=2 * n * rows * (rows + width), transcendentals=0
        ),
        name="partial",
    )(*tops, *panels, turned)


def stage_kernel(panel_ref, top_hbm, turned_ref, top_ref, sem):
    copy = pltpu.make_async_copy(top_hbm, top_ref, sem)
    copy.start()
    turned_ref[...] = panel_ref[...].astype(jnp.float32).T.astype(jnp.bfloat16)
    copy.wait()


def stage(panel, inverse_top):
    return pl.pallas_call(
        stage_kernel,
        out_shape=(pltpu.VMEM(panel.shape[::-1], panel.dtype), pltpu.VMEM(inverse_top.shape, inverse_top.dtype)),
        in_specs=[VMEM, HBM],
        out_specs=(VMEM, VMEM),
        scratch_shapes=[pltpu.SemaphoreType.DMA],
        compiler_params=PARAMS,
        name="stage",
    )(panel, pltpu.with_memory_space_constraint(inverse_top, pltpu.HBM))


def choose_kernel(n, *refs):
    tops, chosen_ref = refs[:n], refs[n]
    for d in range(1, n // PAIR):
        place = place_of(n, d, 0)
        for t in range(n):
            @pl.when(place == t)
            def _():
                chosen_ref[d - 1] = tops[t][...]


def choose(tops):
    n = len(tops)
    return pl.pallas_call(
        functools.partial(choose_kernel, n),
        out_shape=jax.ShapeDtypeStruct((n // 2 - 1,) + tops[0].shape, jnp.bfloat16),
        in_specs=[VMEM] * n,
        out_specs=VMEM,
        compiler_params=PARAMS,
        name="choose",
    )(*tops)


def last_terms(chosen_ref, panels):
    total = dot(chosen_ref[0], panels[0][...])
    for d, panel in enumerate(panels[1:], 1):
        total += dot(chosen_ref[d], panel[...])
    return total


def late_kernel(chosen_ref, turned_ref, early_ref, *refs):
    panels, update_ref = refs[:-1], refs[-1]
    update = dot(turned_ref[...], last_terms(chosen_ref, panels).astype(jnp.bfloat16))
    if len(panels) == 1:
        update += update.T
    store_upper(update_ref, update, early_ref)


def late_share(chosen, turned, panels, early):
    return pl.pallas_call(
        late_kernel,
        out_shape=jax.ShapeDtypeStruct(early.shape, jnp.float32),
        in_specs=[VMEM] * (3 + len(panels)),
        out_specs=VMEM,
        compiler_params=PARAMS,
        name="late",
    )(chosen, turned, early, *panels)


def cross_kernel(partial_ref, chosen_ref, *refs):
    refs[-1][...] = -(partial_ref[...] + last_terms(chosen_ref, refs[:-1]))


def cross_result(partial, chosen, panels):
    rows, width = partial.shape
    return pl.pallas_call(
        cross_kernel,
        out_shape=jax.ShapeDtypeStruct(partial.shape, jnp.float32),
        in_specs=[VMEM] * (2 + len(panels)),
        out_specs=VMEM,
        compiler_params=PARAMS,
        cost_estimate=pl.CostEstimate(
            flops=2 * len(panels) * rows * rows * width, bytes_accessed=8 * rows * width, transcendentals=0
        ),
        name="cross",
    )(partial, chosen, *panels)


def finish_kernel(diag_ref, *refs):
    updates, (out_hbm, out_ref, sems) = refs[:-3], refs[-3:]
    total = updates[0][...].astype(jnp.float32)
    for ref in updates[1:]:
        total += ref[...].astype(jnp.float32)
    quarter = total.shape[0]
    half = 2 * quarter
    tiles = [total[:, t * half:(t + 1) * half] for t in range(5)]
    rows = lax.broadcasted_iota(jnp.int32, (half, half), 0)
    columns = lax.broadcasted_iota(jnp.int32, (half, half), 1)
    mirrored = (rows >= quarter) & (columns < quarter)
    stores = [
        pltpu.make_async_copy(out_ref.at[h], out_hbm.at[0, pl.ds(h * half, half)], sems.at[h]) for h in range(2)
    ]

    def corner(top, bottom):
        block = jnp.concatenate([top, bottom], axis=0)
        return jnp.where(mirrored, block.T, block)

    side = jnp.concatenate([tiles[1], tiles[2]], axis=0)
    out_ref[0, :, :half] = diag_ref[0, :half, :half] + corner(tiles[0], tiles[4])
    out_ref[0, :, half:] = diag_ref[0, :half, half:] + side
    stores[0].start()
    out_ref[1, :, :half] = diag_ref[0, half:, :half] + side.T
    out_ref[1, :, half:] = diag_ref[0, half:, half:] + corner(tiles[3], pltpu.roll(tiles[4], quarter, 1))
    stores[1].start()
    for store in stores:
        store.wait()


def finish(diag_inverse, updates):
    width = diag_inverse.shape[1]
    return pl.pallas_call(
        finish_kernel,
        out_shape=jax.ShapeDtypeStruct(diag_inverse.shape, jnp.float32),
        in_specs=[VMEM] * (1 + len(updates)),
        out_specs=ANY,
        scratch_shapes=[pltpu.VMEM((2, width // 2, width), jnp.float32), pltpu.SemaphoreType.DMA((2,))],
        compiler_params=PARAMS,
        name="finish",
    )(diag_inverse, *updates)


def on_device(n, inverse_top, diag_inverse, cross_blocks, pattern):
    pairs = n // PAIR

    def from_pair(block, axis, shift, flip):
        moves = [
            (((m + shift) % pairs) * PAIR + (b ^ flip), m * PAIR + b) for m in range(pairs) for b in range(PAIR)
        ]
        return lax.ppermute(block, axis, moves)

    def mate(block, axis):
        return from_pair(block, axis, 0, 1)

    near = [from_pair(inverse_top, "pcol", d, 0) for d in range(1, pairs)]
    factor_panel = build_panel(cross_blocks, diag_inverse, pattern)
    beside = mate(factor_panel, "prow")
    crossed = [from_pair(factor_panel, "prow", d, 1) for d in range(1, pairs)]
    turned, inverse_top = stage(factor_panel, inverse_top)
    near = [after(block, turned) for block in near]
    crossed = [after(block, near[0], cost=HOP_COST) for block in crossed]
    beside = after(beside, *crossed, cost=2 * HOP_COST)
    swapped = [mate(block, "prow") for block in crossed]

    tops = [inverse_top, mate(inverse_top, "pcol")]
    for block in near:
        tops += [block, mate(block, "pcol")]

    partial, early = partial_product(tops, [factor_panel, beside] + crossed, turned)
    chosen = choose(tops)
    crossing = [after(from_pair(early, "prow", d, 0), swapped[-1]) for d in range(1, pairs)]
    late = late_share(chosen, turned, swapped, early)
    parts = [late] + crossing
    if pairs > 2:
        rest = (late - early.astype(jnp.float32)).astype(jnp.bfloat16)
        parts += [from_pair(rest, "prow", d, 0) for d in range(1, pairs)]
    update = functools.reduce(jnp.add, [part.astype(jnp.float32) for part in parts]).astype(jnp.bfloat16)
    return cross_result(partial, chosen, swapped), finish(diag_inverse, [update, mate(update, "prow")])


def solution(mesh):
    placed = (
        P(("pole", "prow"), "pcol"),
        P(("pole", "pcol"), None, None),
        P(("pole", "prow"), "pcol"),
        P("prow", "pcol"),
    )
    return jax.shard_map(
        functools.partial(on_device, mesh.shape["pcol"]),
        mesh=mesh,
        in_specs=placed,
        out_specs=(P(("pole", "prow"), "pcol"), P(("pole", "pcol"), None, None)),
        check_vma=False,
    )
```

```python
import functools
import jax
import jax.numpy as jnp
from jax import lax
from jax.experimental import pallas as pl
from jax.experimental.pallas import tpu as pltpu
from jax.sharding import PartitionSpec as P

PAIR = 2
HOP_COST = 10**10
VMEM_LIMIT = 40 * 1024 * 1024
PARAMS = pltpu.CompilerParams(vmem_limit_bytes=VMEM_LIMIT)
SMALL = pltpu.CompilerParams(vmem_limit_bytes=1024 * 1024)
VMEM = pl.BlockSpec(memory_space=pltpu.VMEM)
ANY = pl.BlockSpec(memory_space=pl.ANY)
HBM = pl.BlockSpec(memory_space=pltpu.HBM)


def split(value):
    high = value.astype(jnp.bfloat16)
    return high, (value - high.astype(jnp.float32)).astype(jnp.bfloat16)


def dot(left, right):
    return jnp.dot(left, right, preferred_element_type=jnp.float32)


def token_kernel(out_ref):
    out_ref[...] = jnp.zeros_like(out_ref)


def token():
    return pl.pallas_call(
        token_kernel,
        out_shape=jax.ShapeDtypeStruct((8, 128), jnp.float32),
        out_specs=VMEM,
        compiler_params=SMALL,
        cost_estimate=pl.CostEstimate(flops=HOP_COST, bytes_accessed=0, transcendentals=0),
        name="token",
    )()


def panel_kernel(pattern_hbm, cross_ref, diag_ref, token_ref, panel_ref, pattern_ref, sem):
    del token_ref
    width = diag_ref.shape[1]
    pattern_copy = pltpu.make_async_copy(pattern_hbm, pattern_ref, sem)
    pattern_copy.start()
    diag_high, diag_low = split(diag_ref[0])
    solved = []
    for a in range(pattern_hbm.shape[0]):
        high, low = split(cross_ref[pl.ds(a * width, width), :])
        solved.append(dot(high, diag_high) + (dot(high, diag_low) + dot(low, diag_high)))
    pattern_copy.wait()
    for a, block in enumerate(solved):
        kept = jnp.where(pattern_ref[a] != 0, block, 0.0)
        panel_ref[pl.ds(a * width, width), :] = kept.astype(jnp.bfloat16)


def build_panel(cross_blocks, diag_inverse, pattern):
    return pl.pallas_call(
        panel_kernel,
        out_shape=pltpu.VMEM(cross_blocks.shape, jnp.bfloat16),
        in_specs=[HBM, VMEM, VMEM, ANY],
        out_specs=VMEM,
        scratch_shapes=[pltpu.SMEM((pattern.size,), jnp.int32), pltpu.SemaphoreType.DMA],
        compiler_params=PARAMS,
        name="panel",
    )(
        pltpu.with_memory_space_constraint(pattern.reshape(-1), pltpu.HBM),
        cross_blocks,
        diag_inverse,
        token(),
    )


def relay_kernel(*refs):
    del refs


def after(block, *gates, cost=0):
    return pl.pallas_call(
        relay_kernel,
        out_shape=jax.ShapeDtypeStruct(block.shape, block.dtype),
        in_specs=[ANY] * (1 + len(gates)),
        out_specs=ANY,
        input_output_aliases={0: 0},
        compiler_params=SMALL,
        cost_estimate=pl.CostEstimate(flops=cost, bytes_accessed=cost // 256, transcendentals=0),
        name="relay",
    )(block, *gates)


def store_upper(out_ref, update, *others):
    half = update.shape[0] // 2
    quarter = half // 2
    left, right = update[:, :half], update[:, half:]
    lanes = lax.broadcasted_iota(jnp.int32, (quarter, half), 1)
    last = jnp.where(lanes < quarter, pltpu.roll(right[3 * quarter:], quarter, 1), left[quarter:half])
    tiles = [left[:quarter], right[:quarter], right[quarter:half], right[half:3 * quarter], last]
    for t, tile in enumerate(tiles):
        columns = pl.ds(t * half, half)
        for other in others:
            tile += other[:, columns].astype(jnp.float32)
        out_ref[:, columns] = tile.astype(out_ref.dtype)


def place_of(n, d, f):
    pairs = n // PAIR
    row, col = lax.axis_index("prow"), lax.axis_index("pcol")
    pair = (row // PAIR + d + pairs - col // PAIR) % pairs
    side = (row + f + col) % PAIR
    return pair * PAIR + side


def partial_kernel(n, *refs):
    tops, panels = refs[:n], refs[n:n + n // 2 + 1]
    turned_ref, partial_ref, update_ref, panel_buf = refs[n + n // 2 + 1:]

    def run(pairs):
        total = dot(*[ref[...] for ref in pairs[0]])
        for top, panel in pairs[1:]:
            total += dot(top[...], panel[...])
        partial_ref[...] = total
        store_upper(update_ref, dot(turned_ref[...], total.astype(jnp.bfloat16)))

    if n == 2 * PAIR:
        place = place_of(n, 0, 0)
        for own in range(n):
            pl.when(place == own)(functools.partial(run, list(zip([tops[own ^ s] for s in (0, 1, 3)], panels))))
        return
    pairs = n // PAIR
    held = [(0, 0)] + [(d, 1) for d in range(pairs)]
    for (d, f), panel in zip(held, panels):
        panel_buf[place_of(n, d, f)] = panel[...]
    for d in range(1, pairs):
        panel_buf[place_of(n, d, 0)] = jnp.zeros(panel_buf.shape[1:], panel_buf.dtype)
    run([(tops[t], panel_buf.at[t]) for t in range(n)])


def partial_product(tops, panels, turned):
    n = len(tops)
    rows, width = panels[0].shape
    return pl.pallas_call(
        functools.partial(partial_kernel, n),
        out_shape=(
            jax.ShapeDtypeStruct((rows, width), jnp.float32),
            jax.ShapeDtypeStruct((width // 4, 5 * (width // 2)), jnp.bfloat16),
        ),
        in_specs=[VMEM] * (n + len(panels) + 1),
        out_specs=(VMEM, VMEM),
        scratch_shapes=[pltpu.VMEM((n, rows, width), jnp.bfloat16)],
        compiler_params=PARAMS,
        cost_estimate=pl.CostEstimate(
            flops=2 * n * rows * rows * width, bytes_accessed=2 * n * rows * (rows + width), transcendentals=0
        ),
        name="partial",
    )(*tops, *panels, turned)


def stage_kernel(panel_ref, top_hbm, turned_ref, top_ref, sem):
    copy = pltpu.make_async_copy(top_hbm, top_ref, sem)
    copy.start()
    turned_ref[...] = panel_ref[...].astype(jnp.float32).T.astype(jnp.bfloat16)
    copy.wait()


def stage(panel, inverse_top):
    return pl.pallas_call(
        stage_kernel,
        out_shape=(pltpu.VMEM(panel.shape[::-1], panel.dtype), pltpu.VMEM(inverse_top.shape, inverse_top.dtype)),
        in_specs=[VMEM, HBM],
        out_specs=(VMEM, VMEM),
        scratch_shapes=[pltpu.SemaphoreType.DMA],
        compiler_params=PARAMS,
        name="stage",
    )(panel, pltpu.with_memory_space_constraint(inverse_top, pltpu.HBM))


def choose_kernel(n, *refs):
    tops, (turned_ref, chosen_ref, left_ref) = refs[:n], refs[n:]
    for d in range(1, n // PAIR):
        place = place_of(n, d, 0)
        for t in range(n):
            @pl.when(place == t)
            def _():
                chosen_ref[d - 1] = tops[t][...]
        left_ref[d - 1] = dot(turned_ref[...], chosen_ref[d - 1]).astype(jnp.bfloat16)


def choose(tops, turned):
    n = len(tops)
    return pl.pallas_call(
        functools.partial(choose_kernel, n),
        out_shape=(
            jax.ShapeDtypeStruct((n // 2 - 1,) + tops[0].shape, jnp.bfloat16),
            jax.ShapeDtypeStruct((n // 2 - 1,) + turned.shape, jnp.bfloat16),
        ),
        in_specs=[VMEM] * (n + 1),
        out_specs=(VMEM, VMEM),
        compiler_params=PARAMS,
        name="choose",
    )(*tops, turned)


def last_terms(left_ref, panels):
    total = dot(left_ref[0], panels[0][...])
    for d, panel in enumerate(panels[1:], 1):
        total += dot(left_ref[d], panel[...])
    return total


def late_kernel(left_ref, early_ref, *refs):
    panels, update_ref = refs[:-1], refs[-1]
    update = last_terms(left_ref, panels)
    if len(panels) == 1:
        update += update.T
    store_upper(update_ref, update, early_ref)


def late_share(left, panels, early):
    return pl.pallas_call(
        late_kernel,
        out_shape=jax.ShapeDtypeStruct(early.shape, jnp.float32),
        in_specs=[VMEM] * (2 + len(panels)),
        out_specs=VMEM,
        compiler_params=PARAMS,
        name="late",
    )(left, early, *panels)


def cross_kernel(partial_ref, chosen_ref, *refs):
    refs[-1][...] = -(partial_ref[...] + last_terms(chosen_ref, refs[:-1]))


def cross_result(partial, chosen, panels):
    rows, width = partial.shape
    return pl.pallas_call(
        cross_kernel,
        out_shape=jax.ShapeDtypeStruct(partial.shape, jnp.float32),
        in_specs=[VMEM] * (2 + len(panels)),
        out_specs=VMEM,
        compiler_params=PARAMS,
        cost_estimate=pl.CostEstimate(
            flops=2 * len(panels) * rows * rows * width, bytes_accessed=8 * rows * width, transcendentals=0
        ),
        name="cross",
    )(partial, chosen, *panels)


def finish_kernel(diag_ref, *refs):
    updates, (out_hbm, out_ref, sems) = refs[:-3], refs[-3:]
    total = updates[0][...].astype(jnp.float32)
    for ref in updates[1:]:
        total += ref[...].astype(jnp.float32)
    quarter = total.shape[0]
    half = 2 * quarter
    tiles = [total[:, t * half:(t + 1) * half] for t in range(5)]
    rows = lax.broadcasted_iota(jnp.int32, (half, half), 0)
    columns = lax.broadcasted_iota(jnp.int32, (half, half), 1)
    mirrored = (rows >= quarter) & (columns < quarter)
    stores = [
        pltpu.make_async_copy(out_ref.at[h], out_hbm.at[0, pl.ds(h * half, half)], sems.at[h]) for h in range(2)
    ]

    def corner(top, bottom):
        block = jnp.concatenate([top, bottom], axis=0)
        return jnp.where(mirrored, block.T, block)

    side = jnp.concatenate([tiles[1], tiles[2]], axis=0)
    out_ref[0, :, :half] = diag_ref[0, :half, :half] + corner(tiles[0], tiles[4])
    out_ref[0, :, half:] = diag_ref[0, :half, half:] + side
    stores[0].start()
    out_ref[1, :, :half] = diag_ref[0, half:, :half] + side.T
    out_ref[1, :, half:] = diag_ref[0, half:, half:] + corner(tiles[3], pltpu.roll(tiles[4], quarter, 1))
    stores[1].start()
    for store in stores:
        store.wait()


def finish(diag_inverse, updates):
    width = diag_inverse.shape[1]
    return pl.pallas_call(
        finish_kernel,
        out_shape=jax.ShapeDtypeStruct(diag_inverse.shape, jnp.float32),
        in_specs=[VMEM] * (1 + len(updates)),
        out_specs=ANY,
        scratch_shapes=[pltpu.VMEM((2, width // 2, width), jnp.float32), pltpu.SemaphoreType.DMA((2,))],
        compiler_params=PARAMS,
        name="finish",
    )(diag_inverse, *updates)


def on_device(n, inverse_top, diag_inverse, cross_blocks, pattern):
    pairs = n // PAIR

    def from_pair(block, axis, shift, flip):
        moves = [
            (((m + shift) % pairs) * PAIR + (b ^ flip), m * PAIR + b) for m in range(pairs) for b in range(PAIR)
        ]
        return lax.ppermute(block, axis, moves)

    def mate(block, axis):
        return from_pair(block, axis, 0, 1)

    near = [from_pair(inverse_top, "pcol", d, 0) for d in range(1, pairs)]
    factor_panel = build_panel(cross_blocks, diag_inverse, pattern)
    beside = mate(factor_panel, "prow")
    crossed = [from_pair(factor_panel, "prow", d, 1) for d in range(1, pairs)]
    turned, inverse_top = stage(factor_panel, inverse_top)
    near = [after(block, turned) for block in near]
    crossed = [after(block, near[0], cost=HOP_COST) for block in crossed]
    beside = after(beside, *crossed, cost=2 * HOP_COST)
    swapped = [mate(block, "prow") for block in crossed]

    tops = [inverse_top, mate(inverse_top, "pcol")]
    for block in near:
        tops += [block, mate(block, "pcol")]

    partial, early = partial_product(tops, [factor_panel, beside] + crossed, turned)
    chosen, left = choose(tops, turned)
    crossing = [after(from_pair(early, "prow", d, 0), swapped[-1]) for d in range(1, pairs)]
    late = late_share(left, swapped, early)
    parts = [late] + crossing
    if pairs > 2:
        rest = (late - early.astype(jnp.float32)).astype(jnp.bfloat16)
        parts += [from_pair(rest, "prow", d, 0) for d in range(1, pairs)]
    update = functools.reduce(jnp.add, [part.astype(jnp.float32) for part in parts]).astype(jnp.bfloat16)
    return cross_result(partial, chosen, swapped), finish(diag_inverse, [update, mate(update, "prow")])


def solution(mesh):
    placed = (
        P(("pole", "prow"), "pcol"),
        P(("pole", "pcol"), None, None),
        P(("pole", "prow"), "pcol"),
        P("prow", "pcol"),
    )
    return jax.shard_map(
        functools.partial(on_device, mesh.shape["pcol"]),
        mesh=mesh,
        in_specs=placed,
        out_specs=(P(("pole", "prow"), "pcol"), P(("pole", "pcol"), None, None)),
        check_vma=False,
    )
```

```python
import functools
import jax
import jax.numpy as jnp
from jax import lax
from jax.experimental import pallas as pl
from jax.experimental.pallas import tpu as pltpu
from jax.sharding import PartitionSpec as P

PAIR = 2
HOP_COST = 10**10
VMEM_LIMIT = 40 * 1024 * 1024
PARAMS = pltpu.CompilerParams(vmem_limit_bytes=VMEM_LIMIT)
SMALL = pltpu.CompilerParams(vmem_limit_bytes=1024 * 1024)
VMEM = pl.BlockSpec(memory_space=pltpu.VMEM)
ANY = pl.BlockSpec(memory_space=pl.ANY)
HBM = pl.BlockSpec(memory_space=pltpu.HBM)


def split(value):
    high = value.astype(jnp.bfloat16)
    return high, (value - high.astype(jnp.float32)).astype(jnp.bfloat16)


def dot(left, right):
    return jnp.dot(left, right, preferred_element_type=jnp.float32)


def token_kernel(out_ref):
    out_ref[...] = jnp.zeros_like(out_ref)


def token():
    return pl.pallas_call(
        token_kernel,
        out_shape=jax.ShapeDtypeStruct((8, 128), jnp.float32),
        out_specs=VMEM,
        compiler_params=SMALL,
        cost_estimate=pl.CostEstimate(flops=HOP_COST, bytes_accessed=0, transcendentals=0),
        name="token",
    )()


def panel_kernel(pattern_hbm, cross_ref, diag_ref, token_ref, panel_ref, pattern_ref, sem):
    del token_ref
    width = diag_ref.shape[1]
    pattern_copy = pltpu.make_async_copy(pattern_hbm, pattern_ref, sem)
    pattern_copy.start()
    diag_high, diag_low = split(diag_ref[0])
    solved = []
    for a in range(pattern_hbm.shape[0]):
        high, low = split(cross_ref[pl.ds(a * width, width), :])
        solved.append(dot(high, diag_high) + (dot(high, diag_low) + dot(low, diag_high)))
    pattern_copy.wait()
    for a, block in enumerate(solved):
        kept = jnp.where(pattern_ref[a] != 0, block, 0.0)
        panel_ref[pl.ds(a * width, width), :] = kept.astype(jnp.bfloat16)


def build_panel(cross_blocks, diag_inverse, pattern):
    return pl.pallas_call(
        panel_kernel,
        out_shape=pltpu.VMEM(cross_blocks.shape, jnp.bfloat16),
        in_specs=[HBM, VMEM, VMEM, ANY],
        out_specs=VMEM,
        scratch_shapes=[pltpu.SMEM((pattern.size,), jnp.int32), pltpu.SemaphoreType.DMA],
        compiler_params=PARAMS,
        name="panel",
    )(
        pltpu.with_memory_space_constraint(pattern.reshape(-1), pltpu.HBM),
        cross_blocks,
        diag_inverse,
        token(),
    )


def relay_kernel(*refs):
    del refs


def after(block, *gates, cost=0):
    return pl.pallas_call(
        relay_kernel,
        out_shape=jax.ShapeDtypeStruct(block.shape, block.dtype),
        in_specs=[ANY] * (1 + len(gates)),
        out_specs=ANY,
        input_output_aliases={0: 0},
        compiler_params=SMALL,
        cost_estimate=pl.CostEstimate(flops=cost, bytes_accessed=cost // 256, transcendentals=0),
        name="relay",
    )(block, *gates)


def store_upper(out_ref, update, *others):
    half = update.shape[0] // 2
    quarter = half // 2
    left, right = update[:, :half], update[:, half:]
    lanes = lax.broadcasted_iota(jnp.int32, (quarter, half), 1)
    last = jnp.where(lanes < quarter, pltpu.roll(right[3 * quarter:], quarter, 1), left[quarter:half])
    tiles = [left[:quarter], right[:quarter], right[quarter:half], right[half:3 * quarter], last]
    for t, tile in enumerate(tiles):
        columns = pl.ds(t * half, half)
        for other in others:
            tile += other[:, columns].astype(jnp.float32)
        out_ref[:, columns] = tile.astype(out_ref.dtype)


def place_of(n, d, f):
    pairs = n // PAIR
    row, col = lax.axis_index("prow"), lax.axis_index("pcol")
    pair = (row // PAIR + d + pairs - col // PAIR) % pairs
    side = (row + f + col) % PAIR
    return pair * PAIR + side


def matched(n, tops, panels, panel_buf, run):
    if n == 2 * PAIR:
        place = place_of(n, 0, 0)
        for own in range(n):
            pl.when(place == own)(functools.partial(run, list(zip([tops[own ^ s] for s in (0, 1, 3)], panels))))
        return
    pairs = n // PAIR
    held = [(0, 0)] + [(d, 1) for d in range(pairs)]
    for (d, f), panel in zip(held, panels):
        panel_buf[place_of(n, d, f)] = panel[...]
    for d in range(1, pairs):
        panel_buf[place_of(n, d, 0)] = jnp.zeros(panel_buf.shape[1:], panel_buf.dtype)
    run([(tops[t], panel_buf.at[t]) for t in range(n)])


def product(pairs):
    total = dot(*[ref[...] for ref in pairs[0]])
    for top, panel in pairs[1:]:
        total += dot(top[...], panel[...])
    return total


def lefts_kernel(n, *refs):
    tops, (turned_ref, lefts_ref) = refs[:n], refs[n:]
    held = [(0, 0)] + [(d, 1) for d in range(n // PAIR)]
    for p, (d, f) in enumerate(held):
        place = place_of(n, d, f)
        for t in range(n):
            @pl.when(place == t)
            def _():
                lefts_ref[p] = dot(turned_ref[...], tops[t][...]).astype(jnp.bfloat16)


def early_lefts(tops, turned):
    n = len(tops)
    return pl.pallas_call(
        functools.partial(lefts_kernel, n),
        out_shape=jax.ShapeDtypeStruct((n // 2 + 1,) + turned.shape, jnp.bfloat16),
        in_specs=[VMEM] * (n + 1),
        out_specs=VMEM,
        compiler_params=PARAMS,
        name="lefts",
    )(*tops, turned)


def early_kernel(lefts_ref, *refs):
    store_upper(refs[-1], last_terms(lefts_ref, refs[:-1]))


def early_share(lefts, panels):
    width = panels[0].shape[1]
    return pl.pallas_call(
        early_kernel,
        out_shape=jax.ShapeDtypeStruct((width // 4, 5 * (width // 2)), jnp.bfloat16),
        in_specs=[VMEM] * (1 + len(panels)),
        out_specs=VMEM,
        compiler_params=PARAMS,
        name="early",
    )(lefts, *panels)


def stage_kernel(panel_ref, top_hbm, turned_ref, top_ref, sem):
    copy = pltpu.make_async_copy(top_hbm, top_ref, sem)
    copy.start()
    turned_ref[...] = panel_ref[...].astype(jnp.float32).T.astype(jnp.bfloat16)
    copy.wait()


def stage(panel, inverse_top):
    return pl.pallas_call(
        stage_kernel,
        out_shape=(pltpu.VMEM(panel.shape[::-1], panel.dtype), pltpu.VMEM(inverse_top.shape, inverse_top.dtype)),
        in_specs=[VMEM, HBM],
        out_specs=(VMEM, VMEM),
        scratch_shapes=[pltpu.SemaphoreType.DMA],
        compiler_params=PARAMS,
        name="stage",
    )(panel, pltpu.with_memory_space_constraint(inverse_top, pltpu.HBM))


def choose_kernel(n, *refs):
    tops, (turned_ref, chosen_ref, left_ref) = refs[:n], refs[n:]
    for d in range(1, n // PAIR):
        place = place_of(n, d, 0)
        for t in range(n):
            @pl.when(place == t)
            def _():
                chosen_ref[d - 1] = tops[t][...]
        left_ref[d - 1] = dot(turned_ref[...], chosen_ref[d - 1]).astype(jnp.bfloat16)


def choose(tops, turned):
    n = len(tops)
    return pl.pallas_call(
        functools.partial(choose_kernel, n),
        out_shape=(
            jax.ShapeDtypeStruct((n // 2 - 1,) + tops[0].shape, jnp.bfloat16),
            jax.ShapeDtypeStruct((n // 2 - 1,) + turned.shape, jnp.bfloat16),
        ),
        in_specs=[VMEM] * (n + 1),
        out_specs=(VMEM, VMEM),
        compiler_params=PARAMS,
        name="choose",
    )(*tops, turned)


def last_terms(left_ref, panels):
    total = dot(left_ref[0], panels[0][...])
    for d, panel in enumerate(panels[1:], 1):
        total += dot(left_ref[d], panel[...])
    return total


def late_kernel(left_ref, early_ref, *refs):
    panels, update_ref = refs[:-1], refs[-1]
    update = last_terms(left_ref, panels)
    if len(panels) == 1:
        update += update.T
    store_upper(update_ref, update, early_ref)


def late_share(left, panels, early):
    return pl.pallas_call(
        late_kernel,
        out_shape=jax.ShapeDtypeStruct(early.shape, jnp.float32),
        in_specs=[VMEM] * (2 + len(panels)),
        out_specs=VMEM,
        compiler_params=PARAMS,
        name="late",
    )(left, early, *panels)


def cross_kernel(n, *refs):
    tops, panels = refs[:n], refs[n:n + n // 2 + 1]
    chosen_ref, *swapped, out_ref, panel_buf = refs[n + n // 2 + 1:]

    def run(pairs):
        out_ref[...] = -(product(pairs) + last_terms(chosen_ref, swapped))

    matched(n, tops, panels, panel_buf, run)


def cross_result(tops, panels, chosen, swapped):
    n = len(tops)
    rows, width = panels[0].shape
    return pl.pallas_call(
        functools.partial(cross_kernel, n),
        out_shape=jax.ShapeDtypeStruct((rows, width), jnp.float32),
        in_specs=[VMEM] * (n + len(panels) + 1 + len(swapped)),
        out_specs=VMEM,
        scratch_shapes=[pltpu.VMEM((n, rows, width), jnp.bfloat16)],
        compiler_params=PARAMS,
        cost_estimate=pl.CostEstimate(
            flops=2 * n * rows * rows * width, bytes_accessed=4 * rows * width, transcendentals=0
        ),
        name="cross",
    )(*tops, *panels, chosen, *swapped)


def finish_kernel(diag_ref, *refs):
    updates, (out_hbm, out_ref, sems) = refs[:-3], refs[-3:]
    total = updates[0][...].astype(jnp.float32)
    for ref in updates[1:]:
        total += ref[...].astype(jnp.float32)
    quarter = total.shape[0]
    half = 2 * quarter
    tiles = [total[:, t * half:(t + 1) * half] for t in range(5)]
    rows = lax.broadcasted_iota(jnp.int32, (half, half), 0)
    columns = lax.broadcasted_iota(jnp.int32, (half, half), 1)
    mirrored = (rows >= quarter) & (columns < quarter)
    stores = [
        pltpu.make_async_copy(out_ref.at[h], out_hbm.at[0, pl.ds(h * half, half)], sems.at[h]) for h in range(2)
    ]

    def corner(top, bottom):
        block = jnp.concatenate([top, bottom], axis=0)
        return jnp.where(mirrored, block.T, block)

    side = jnp.concatenate([tiles[1], tiles[2]], axis=0)
    out_ref[0, :, :half] = diag_ref[0, :half, :half] + corner(tiles[0], tiles[4])
    out_ref[0, :, half:] = diag_ref[0, :half, half:] + side
    stores[0].start()
    out_ref[1, :, :half] = diag_ref[0, half:, :half] + side.T
    out_ref[1, :, half:] = diag_ref[0, half:, half:] + corner(tiles[3], pltpu.roll(tiles[4], quarter, 1))
    stores[1].start()
    for store in stores:
        store.wait()


def finish(diag_inverse, updates):
    width = diag_inverse.shape[1]
    return pl.pallas_call(
        finish_kernel,
        out_shape=jax.ShapeDtypeStruct(diag_inverse.shape, jnp.float32),
        in_specs=[VMEM] * (1 + len(updates)),
        out_specs=ANY,
        scratch_shapes=[pltpu.VMEM((2, width // 2, width), jnp.float32), pltpu.SemaphoreType.DMA((2,))],
        compiler_params=PARAMS,
        name="finish",
    )(diag_inverse, *updates)


def on_device(n, inverse_top, diag_inverse, cross_blocks, pattern):
    pairs = n // PAIR

    def from_pair(block, axis, shift, flip):
        moves = [
            (((m + shift) % pairs) * PAIR + (b ^ flip), m * PAIR + b) for m in range(pairs) for b in range(PAIR)
        ]
        return lax.ppermute(block, axis, moves)

    def mate(block, axis):
        return from_pair(block, axis, 0, 1)

    near = [from_pair(inverse_top, "pcol", d, 0) for d in range(1, pairs)]
    factor_panel = build_panel(cross_blocks, diag_inverse, pattern)
    beside = mate(factor_panel, "prow")
    crossed = [from_pair(factor_panel, "prow", d, 1) for d in range(1, pairs)]
    turned, inverse_top = stage(factor_panel, inverse_top)
    near = [after(block, turned) for block in near]
    crossed = [after(block, near[0], cost=HOP_COST) for block in crossed]
    swapped = [mate(block, "prow") for block in crossed]

    tops = [inverse_top, mate(inverse_top, "pcol")]
    for block in near:
        tops += [block, mate(block, "pcol")]

    lefts = early_lefts(tops, turned)
    beside = after(beside, lefts, *crossed, cost=2 * HOP_COST)
    panels = [factor_panel, beside] + crossed
    early = early_share(lefts, panels)
    chosen, left = choose(tops, turned)
    crossing = [after(from_pair(early, "prow", d, 0), swapped[-1]) for d in range(1, pairs)]
    late = late_share(left, swapped, early)
    parts = [late] + crossing
    if pairs > 2:
        rest = (late - early.astype(jnp.float32)).astype(jnp.bfloat16)
        parts += [from_pair(rest, "prow", d, 0) for d in range(1, pairs)]
    update = functools.reduce(jnp.add, [part.astype(jnp.float32) for part in parts]).astype(jnp.bfloat16)
    return cross_result(tops, panels, chosen, swapped), finish(diag_inverse, [update, mate(update, "prow")])


def solution(mesh):
    placed = (
        P(("pole", "prow"), "pcol"),
        P(("pole", "pcol"), None, None),
        P(("pole", "prow"), "pcol"),
        P("prow", "pcol"),
    )
    return jax.shard_map(
        functools.partial(on_device, mesh.shape["pcol"]),
        mesh=mesh,
        in_specs=placed,
        out_specs=(P(("pole", "prow"), "pcol"), P(("pole", "pcol"), None, None)),
        check_vma=False,
    )
```

```python
import functools
import jax
import jax.numpy as jnp
from jax import lax
from jax.experimental import pallas as pl
from jax.experimental.pallas import tpu as pltpu
from jax.sharding import PartitionSpec as P

PAIR = 2
HOP_COST = 10**10
VMEM_LIMIT = 40 * 1024 * 1024
PARAMS = pltpu.CompilerParams(vmem_limit_bytes=VMEM_LIMIT)
SMALL = pltpu.CompilerParams(vmem_limit_bytes=1024 * 1024)
VMEM = pl.BlockSpec(memory_space=pltpu.VMEM)
ANY = pl.BlockSpec(memory_space=pl.ANY)
HBM = pl.BlockSpec(memory_space=pltpu.HBM)


def split(value):
    high = value.astype(jnp.bfloat16)
    return high, (value - high.astype(jnp.float32)).astype(jnp.bfloat16)


def dot(left, right):
    return jnp.dot(left, right, preferred_element_type=jnp.float32)


def token_kernel(out_ref):
    out_ref[...] = jnp.zeros_like(out_ref)


def token():
    return pl.pallas_call(
        token_kernel,
        out_shape=jax.ShapeDtypeStruct((8, 128), jnp.float32),
        out_specs=VMEM,
        compiler_params=SMALL,
        cost_estimate=pl.CostEstimate(flops=HOP_COST, bytes_accessed=0, transcendentals=0),
        name="token",
    )()


def panel_kernel(pattern_hbm, cross_ref, diag_ref, token_ref, panel_ref, pattern_ref, sem):
    del token_ref
    width = diag_ref.shape[1]
    pattern_copy = pltpu.make_async_copy(pattern_hbm, pattern_ref, sem)
    pattern_copy.start()
    diag_high, diag_low = split(diag_ref[0])
    solved = []
    for a in range(pattern_hbm.shape[0]):
        high, low = split(cross_ref[pl.ds(a * width, width), :])
        solved.append(dot(high, diag_high) + (dot(high, diag_low) + dot(low, diag_high)))
    pattern_copy.wait()
    for a, block in enumerate(solved):
        kept = jnp.where(pattern_ref[a] != 0, block, 0.0)
        panel_ref[pl.ds(a * width, width), :] = kept.astype(jnp.bfloat16)


def build_panel(cross_blocks, diag_inverse, pattern):
    return pl.pallas_call(
        panel_kernel,
        out_shape=pltpu.VMEM(cross_blocks.shape, jnp.bfloat16),
        in_specs=[HBM, VMEM, VMEM, ANY],
        out_specs=VMEM,
        scratch_shapes=[pltpu.SMEM((pattern.size,), jnp.int32), pltpu.SemaphoreType.DMA],
        compiler_params=PARAMS,
        name="panel",
    )(
        pltpu.with_memory_space_constraint(pattern.reshape(-1), pltpu.HBM),
        cross_blocks,
        diag_inverse,
        token(),
    )


def relay_kernel(*refs):
    del refs


def after(block, *gates, cost=0):
    return pl.pallas_call(
        relay_kernel,
        out_shape=jax.ShapeDtypeStruct(block.shape, block.dtype),
        in_specs=[ANY] * (1 + len(gates)),
        out_specs=ANY,
        input_output_aliases={0: 0},
        compiler_params=SMALL,
        cost_estimate=pl.CostEstimate(flops=cost, bytes_accessed=cost // 256, transcendentals=0),
        name="relay",
    )(block, *gates)


def store_upper(out_ref, update, *others):
    half = update.shape[0] // 2
    quarter = half // 2
    left, right = update[:, :half], update[:, half:]
    lanes = lax.broadcasted_iota(jnp.int32, (quarter, half), 1)
    last = jnp.where(lanes < quarter, pltpu.roll(right[3 * quarter:], quarter, 1), left[quarter:half])
    tiles = [left[:quarter], right[:quarter], right[quarter:half], right[half:3 * quarter], last]
    for t, tile in enumerate(tiles):
        columns = pl.ds(t * half, half)
        for other in others:
            tile += other[:, columns].astype(jnp.float32)
        out_ref[:, columns] = tile.astype(out_ref.dtype)


def place_of(n, d, f):
    pairs = n // PAIR
    row, col = lax.axis_index("prow"), lax.axis_index("pcol")
    pair = (row // PAIR + d + pairs - col // PAIR) % pairs
    side = (row + f + col) % PAIR
    return pair * PAIR + side


def matched(n, tops, panels, panel_buf, run):
    if n == 2 * PAIR:
        place = place_of(n, 0, 0)
        for own in range(n):
            pl.when(place == own)(functools.partial(run, list(zip([tops[own ^ s] for s in (0, 1, 3)], panels))))
        return
    pairs = n // PAIR
    held = [(0, 0)] + [(d, 1) for d in range(pairs)]
    for (d, f), panel in zip(held, panels):
        panel_buf[place_of(n, d, f)] = panel[...]
    for d in range(1, pairs):
        panel_buf[place_of(n, d, 0)] = jnp.zeros(panel_buf.shape[1:], panel_buf.dtype)
    run([(tops[t], panel_buf.at[t]) for t in range(n)])


def product(pairs):
    total = dot(*[ref[...] for ref in pairs[0]])
    for top, panel in pairs[1:]:
        total += dot(top[...], panel[...])
    return total


def lefts_kernel(n, *refs):
    tops, (turned_ref, lefts_ref) = refs[:n], refs[n:]
    held = [(0, 0)] + [(d, 1) for d in range(n // PAIR)]
    for p, (d, f) in enumerate(held):
        place = place_of(n, d, f)
        for t in range(n):
            @pl.when(place == t)
            def _():
                lefts_ref[p] = dot(turned_ref[...], tops[t][...]).astype(jnp.bfloat16)


def early_lefts(tops, turned):
    n = len(tops)
    return pl.pallas_call(
        functools.partial(lefts_kernel, n),
        out_shape=jax.ShapeDtypeStruct((n // 2 + 1,) + turned.shape, jnp.bfloat16),
        in_specs=[VMEM] * (n + 1),
        out_specs=VMEM,
        compiler_params=PARAMS,
        name="lefts",
    )(*tops, turned)


def early_kernel(lefts_ref, *refs):
    store_upper(refs[-1], last_terms(lefts_ref, refs[:-1]))


def early_share(lefts, panels):
    width = panels[0].shape[1]
    return pl.pallas_call(
        early_kernel,
        out_shape=jax.ShapeDtypeStruct((width // 4, 5 * (width // 2)), jnp.bfloat16),
        in_specs=[VMEM] * (1 + len(panels)),
        out_specs=VMEM,
        compiler_params=PARAMS,
        name="early",
    )(lefts, *panels)


def stage_kernel(panel_ref, top_hbm, turned_ref, top_ref, sem):
    copy = pltpu.make_async_copy(top_hbm, top_ref, sem)
    copy.start()
    turned_ref[...] = panel_ref[...].astype(jnp.float32).T.astype(jnp.bfloat16)
    copy.wait()


def stage(panel, inverse_top):
    return pl.pallas_call(
        stage_kernel,
        out_shape=(pltpu.VMEM(panel.shape[::-1], panel.dtype), pltpu.VMEM(inverse_top.shape, inverse_top.dtype)),
        in_specs=[VMEM, HBM],
        out_specs=(VMEM, VMEM),
        scratch_shapes=[pltpu.SemaphoreType.DMA],
        compiler_params=PARAMS,
        name="stage",
    )(panel, pltpu.with_memory_space_constraint(inverse_top, pltpu.HBM))


def choose_kernel(n, *refs):
    tops, (turned_ref, chosen_ref, left_ref) = refs[:n], refs[n:]
    for d in range(1, n // PAIR):
        place = place_of(n, d, 0)
        for t in range(n):
            @pl.when(place == t)
            def _():
                chosen_ref[d - 1] = tops[t][...]
        left_ref[d - 1] = dot(turned_ref[...], chosen_ref[d - 1]).astype(jnp.bfloat16)


def choose(tops, turned):
    n = len(tops)
    return pl.pallas_call(
        functools.partial(choose_kernel, n),
        out_shape=(
            jax.ShapeDtypeStruct((n // 2 - 1,) + tops[0].shape, jnp.bfloat16),
            jax.ShapeDtypeStruct((n // 2 - 1,) + turned.shape, jnp.bfloat16),
        ),
        in_specs=[VMEM] * (n + 1),
        out_specs=(VMEM, VMEM),
        compiler_params=PARAMS,
        name="choose",
    )(*tops, turned)


def last_terms(left_ref, panels):
    total = dot(left_ref[0], panels[0][...])
    for d, panel in enumerate(panels[1:], 1):
        total += dot(left_ref[d], panel[...])
    return total


def late_kernel(left_ref, early_ref, *refs):
    panels, update_ref = refs[:-1], refs[-1]
    update = last_terms(left_ref, panels)
    if len(panels) == 1:
        update += update.astype(jnp.bfloat16).T.astype(jnp.float32)
    store_upper(update_ref, update, early_ref)


def late_share(left, panels, early):
    return pl.pallas_call(
        late_kernel,
        out_shape=jax.ShapeDtypeStruct(early.shape, jnp.float32),
        in_specs=[VMEM] * (2 + len(panels)),
        out_specs=VMEM,
        compiler_params=PARAMS,
        name="late",
    )(left, early, *panels)


def cross_kernel(n, *refs):
    tops, panels = refs[:n], refs[n:n + n // 2 + 1]
    chosen_ref, *swapped, out_ref, panel_buf = refs[n + n // 2 + 1:]

    def run(pairs):
        out_ref[...] = -(product(pairs) + last_terms(chosen_ref, swapped))

    matched(n, tops, panels, panel_buf, run)


def cross_result(tops, panels, chosen, swapped):
    n = len(tops)
    rows, width = panels[0].shape
    return pl.pallas_call(
        functools.partial(cross_kernel, n),
        out_shape=jax.ShapeDtypeStruct((rows, width), jnp.float32),
        in_specs=[VMEM] * (n + len(panels) + 1 + len(swapped)),
        out_specs=VMEM,
        scratch_shapes=[pltpu.VMEM((n, rows, width), jnp.bfloat16)],
        compiler_params=PARAMS,
        cost_estimate=pl.CostEstimate(
            flops=2 * n * rows * rows * width, bytes_accessed=4 * rows * width, transcendentals=0
        ),
        name="cross",
    )(*tops, *panels, chosen, *swapped)


def finish_kernel(diag_ref, *refs):
    updates, (out_hbm, out_ref, sems) = refs[:-3], refs[-3:]
    total = updates[0][...].astype(jnp.float32)
    for ref in updates[1:]:
        total += ref[...].astype(jnp.float32)
    quarter = total.shape[0]
    half = 2 * quarter
    tiles = [total[:, t * half:(t + 1) * half] for t in range(5)]
    rows = lax.broadcasted_iota(jnp.int32, (half, half), 0)
    columns = lax.broadcasted_iota(jnp.int32, (half, half), 1)
    mirrored = (rows >= quarter) & (columns < quarter)
    stores = [
        pltpu.make_async_copy(out_ref.at[h], out_hbm.at[0, pl.ds(h * half, half)], sems.at[h]) for h in range(2)
    ]

    def corner(top, bottom):
        block = jnp.concatenate([top, bottom], axis=0)
        return jnp.where(mirrored, block.T, block)

    side = jnp.concatenate([tiles[1], tiles[2]], axis=0)
    out_ref[0, :, :half] = diag_ref[0, :half, :half] + corner(tiles[0], tiles[4])
    out_ref[0, :, half:] = diag_ref[0, :half, half:] + side
    stores[0].start()
    out_ref[1, :, :half] = diag_ref[0, half:, :half] + side.T
    out_ref[1, :, half:] = diag_ref[0, half:, half:] + corner(tiles[3], pltpu.roll(tiles[4], quarter, 1))
    stores[1].start()
    for store in stores:
        store.wait()


def finish(diag_inverse, updates):
    width = diag_inverse.shape[1]
    return pl.pallas_call(
        finish_kernel,
        out_shape=jax.ShapeDtypeStruct(diag_inverse.shape, jnp.float32),
        in_specs=[VMEM] * (1 + len(updates)),
        out_specs=ANY,
        scratch_shapes=[pltpu.VMEM((2, width // 2, width), jnp.float32), pltpu.SemaphoreType.DMA((2,))],
        compiler_params=PARAMS,
        name="finish",
    )(diag_inverse, *updates)


def on_device(n, inverse_top, diag_inverse, cross_blocks, pattern):
    pairs = n // PAIR

    def from_pair(block, axis, shift, flip):
        moves = [
            (((m + shift) % pairs) * PAIR + (b ^ flip), m * PAIR + b) for m in range(pairs) for b in range(PAIR)
        ]
        return lax.ppermute(block, axis, moves)

    def mate(block, axis):
        return from_pair(block, axis, 0, 1)

    near = [from_pair(inverse_top, "pcol", d, 0) for d in range(1, pairs)]
    factor_panel = build_panel(cross_blocks, diag_inverse, pattern)
    beside = mate(factor_panel, "prow")
    crossed = [from_pair(factor_panel, "prow", d, 1) for d in range(1, pairs)]
    turned, inverse_top = stage(factor_panel, inverse_top)
    near = [after(block, turned) for block in near]
    crossed = [after(block, near[0], cost=HOP_COST) for block in crossed]
    swapped = [mate(block, "prow") for block in crossed]

    tops = [inverse_top, mate(inverse_top, "pcol")]
    for block in near:
        tops += [block, mate(block, "pcol")]

    lefts = early_lefts(tops, turned)
    beside = after(beside, lefts, *crossed, cost=2 * HOP_COST)
    panels = [factor_panel, beside] + crossed
    early = early_share(lefts, panels)
    chosen, left = choose(tops, turned)
    crossing = [after(from_pair(early, "prow", d, 0), swapped[-1]) for d in range(1, pairs)]
    late = late_share(left, swapped, early)
    parts = [late] + crossing
    if pairs > 2:
        rest = (late - early.astype(jnp.float32)).astype(jnp.bfloat16)
        parts += [from_pair(rest, "prow", d, 0) for d in range(1, pairs)]
    update = functools.reduce(jnp.add, [part.astype(jnp.float32) for part in parts]).astype(jnp.bfloat16)
    return cross_result(tops, panels, chosen, swapped), finish(diag_inverse, [update, mate(update, "prow")])


def solution(mesh):
    placed = (
        P(("pole", "prow"), "pcol"),
        P(("pole", "pcol"), None, None),
        P(("pole", "prow"), "pcol"),
        P("prow", "pcol"),
    )
    return jax.shard_map(
        functools.partial(on_device, mesh.shape["pcol"]),
        mesh=mesh,
        in_specs=placed,
        out_specs=(P(("pole", "prow"), "pcol"), P(("pole", "pcol"), None, None)),
        check_vma=False,
    )
```
